32 devices in a mesh: dev: 32 (over z, y, x, core).
Axes of the slice: x: 2, y: 2, z: 4, core: 2. Of those that a mesh axis runs over, the one named last changes fastest.
Arguments:
- tokens: float32 [10240, 1024], P('dev'), may hold values from -6 to 6
- segments: int32 [10240], P('dev'), may hold values from 0 to 1, as said below
- norm1_gain: float32 [1024], P('dev'), may hold values from 0.5 to 1.5
- norm1_bias: float32 [1024], P('dev'), may hold values from -4 to 4
- qkv_weight: float32 [1024, 3072], P('dev'), may hold values from -0.1875 to 0.1875
- qv_bias: float32 [2048], P('dev'), may hold values from -6 to 6
- out_weight: float32 [1024, 1024], P('dev'), may hold values from -1.5 to 1.5
- out_bias: float32 [1024], P('dev'), may hold values from -6 to 6
- norm2_gain: float32 [1024], P('dev'), may hold values from 0.5 to 1.5
- norm2_bias: float32 [1024], P('dev'), may hold values from -4 to 4
- fc1_weight: float32 [1024, 4096], P('dev'), may hold values from -0.1875 to 0.1875
- fc1_bias: float32 [4096], P('dev'), may hold values from -6 to 6
- fc2_weight: float32 [4096, 1024], P('dev'), may hold values from -0.09375 to 0.09375
- fc2_bias: float32 [1024], P('dev'), may hold values from -6 to 6
- cotangent: float32 [10240, 1024], P('dev'), may hold values from -6 to 6
Outputs:
- activations: float32 [10240, 1024], P('dev')
- input_grad: float32 [10240, 1024], P('dev')
- grad_norm1_gain: float32 [1024], P('dev')
- grad_norm1_bias: float32 [1024], P('dev')
- grad_qkv_weight: float32 [1024, 3072], P('dev')
- grad_qv_bias: float32 [2048], P('dev')
- grad_out_weight: float32 [1024, 1024], P('dev')
- grad_out_bias: float32 [1024], P('dev')
- grad_norm2_gain: float32 [1024], P('dev')
- grad_norm2_bias: float32 [1024], P('dev')
- grad_fc1_weight: float32 [1024, 4096], P('dev')
- grad_fc1_bias: float32 [4096], P('dev')
- grad_fc2_weight: float32 [4096, 1024], P('dev')
- grad_fc2_bias: float32 [1024], P('dev')
The draws below stay inside these ranges and needn't reach their ends.
Inputs may be any that keep to these rules, and one draw needn't show every extreme that they name: `segments`: each block of 320 slots holds one image, image k numbered k, each of 64 to 320 consecutive slots; in every draw some image has exactly 320 slots; the slots after a block's last image are padding, numbered 1.
All inputs are finite; a program needn't handle non-finite values.
Results may differ from the reference program's by a relative error of at most 0.012.
The reference program's roundings to bfloat16 on the way count: a program that leaves them out, or rounds other values in their place, can miss the bound.
Values may be sent and summed in bfloat16 or wider, within the bound.
A program may use at most 256 MiB of HBM per device.

```python
import jax
import jax.numpy as jnp
from jax import lax

D = 1024
HEADS = 16
HEAD_DIM = 64
FF = 4096
PATCHES = 256
BUFFER = 64
IMG_DEV = 1
TOK_DEV = 320
TOKENS = 10240


def draw_segments(key, part):
    key = jax.random.fold_in(key, 7)
    device_count = TOKENS // TOK_DEV
    kept_counts = jax.random.randint(jax.random.fold_in(key, 1), (device_count * IMG_DEV,), 0, PATCHES + 1)
    full_slot = jax.random.randint(jax.random.fold_in(key, 2), (), 0, device_count * IMG_DEV)
    kept_counts = jnp.where(jnp.arange(device_count * IMG_DEV) == full_slot, PATCHES, kept_counts)
    lengths = BUFFER + kept_counts.reshape(device_count, IMG_DEV)
    image_ends = jnp.cumsum(lengths, axis=1)
    positions = jnp.arange(TOK_DEV)
    numbers = jnp.sum((positions[None, :, None] >= image_ends[:, None, :]).astype(jnp.int32), -1)
    return numbers.reshape(TOKENS).astype(jnp.int32)


def strengthened(entries, stream_key, source, target, blocks, factor):
    owner, partner = [(jnp.arange(entries.shape[dim]) // (entries.shape[dim] // blocks)).reshape([-1 if axis == dim else 1 for axis in range(entries.ndim)]) for dim in (source, target)]
    chosen = jax.random.permutation(stream_key, blocks)[partner]
    strong = (owner == chosen) | (owner == (partner + blocks // 2) % blocks)
    return jnp.where(strong, factor * entries, entries)


def block_scale(key, extent, shards, smallest, high):
    def one(position, blocks):
        draws = jax.random.uniform(jax.random.fold_in(jax.random.fold_in(key, 6), position), (blocks,), jnp.float32, smallest / len(shards), high / len(shards))
        return jnp.repeat(jnp.exp(draws), extent[position] // blocks).reshape((-1,) + (1,) * (len(extent) - position - 1))

    loudness = one(*shards[0])
    for cut in shards[1:]:
        loudness = loudness * one(*cut)
    return loudness


def bell_draw(key, dims, scale, limit, shards=(), kind=jnp.bfloat16):
    result = jax.random.normal(key, dims, jnp.float32) * scale
    if len(shards) > 0:
        result = block_scale(key, dims, shards, -0.22, 0.18) * result
    return jnp.clip(result, min=-limit, max=limit).astype(kind)


def heavy_noise(stream_key, shape, scale, most, pieces, heavy, kind=jnp.bfloat16):
    result = scale * jax.random.normal(stream_key, shape, jnp.float32)
    if pieces:
        result = result * block_scale(stream_key, shape, pieces, -0.22, 0.18)
    return jnp.clip(strengthened(result, jax.random.fold_in(stream_key, 3), *heavy), -most, most).astype(kind)


def setup_inputs(seed: int = 0) -> dict:
    key_list = jax.random.split(jax.random.key(seed), 16)
    return {
        "tokens": heavy_noise(key_list[0], (TOKENS, D), 1.0, 6.0, ((0, 32),), (0, 1, 32, 2.75), jnp.float32),
        "segments": draw_segments(jax.random.fold_in(key_list[15], 71), 0),
        "norm1_gain": jnp.clip(1.0 + 0.1 * jax.random.normal(key_list[2], (D,), jnp.float32), 0.5, 1.5),
        "norm1_bias": bell_draw(key_list[3], (D,), 0.3, 4.0, ((0, 32),), jnp.float32),
        "qkv_weight": bell_draw(key_list[4], (D, 3 * D), D ** -0.5, 0.1875, ((0, 32),), jnp.float32),
        "qv_bias": bell_draw(key_list[5], (2 * D,), 0.5, 6.0, ((0, 32),), jnp.float32),
        "out_weight": bell_draw(key_list[6], (D, D), (D // 64) ** -0.5, 1.5, ((0, 32),), jnp.float32),
        "out_bias": bell_draw(key_list[7], (D,), 0.5, 6.0, ((0, 32),), jnp.float32),
        "norm2_gain": jnp.clip(1.0 + 0.1 * jax.random.normal(key_list[8], (D,), jnp.float32), 0.5, 1.5),
        "norm2_bias": bell_draw(key_list[9], (D,), 0.3, 4.0, ((0, 32),), jnp.float32),
        "fc1_weight": bell_draw(key_list[10], (D, FF), D ** -0.5, 0.1875, ((0, 32),), jnp.float32),
        "fc1_bias": bell_draw(key_list[11], (FF,), 0.5, 6.0, ((0, 32),), jnp.float32),
        "fc2_weight": bell_draw(key_list[12], (FF, D), FF ** -0.5, 0.09375, ((0, 32),), jnp.float32),
        "fc2_bias": bell_draw(key_list[13], (D,), 0.5, 6.0, ((0, 32),), jnp.float32),
        "cotangent": heavy_noise(key_list[14], (TOKENS, D), 1.0, 6.0, ((0, 32),), (0, 1, 32, 2.75), jnp.float32),
    }


@jax.custom_vjp
def low(v):
    return lax.optimization_barrier(v.astype(jnp.bfloat16)).astype(jnp.float32)

@jax.custom_vjp
def low_back(v):
    return v

def low_keep(v):
    return (low(v), None)

def low_pass(kept, grad):
    return (grad,)

def back_keep(v):
    return (v, None)

def back_low(kept, grad):
    return (low(grad),)
low.defvjp(low_keep, low_pass)
low_back.defvjp(back_keep, back_low)

def layer_norm(rows_in, gain, bias):
    centre = rows_in - lax.optimization_barrier(jnp.mean(rows_in, -1, keepdims=True))
    spread = lax.optimization_barrier(jnp.mean(centre * centre, -1, keepdims=True))
    return centre * lax.rsqrt(spread + 1e-06) * gain + bias

def matmul(left, right):
    return jnp.dot(left, right, preferred_element_type=jnp.float32, precision=lax.Precision.HIGHEST)

def block_forward(token_block, segment_block, rounded):
    gain_one, bias_one, mix_weight, mix_bias, proj_weight, proj_bias, gain_two, bias_two, up_weight, up_bias, down_weight, down_bias = rounded
    valid_slot = segment_block < IMG_DEV
    allowed = (segment_block[:, None] == segment_block[None, :]) & valid_slot[None, :]
    first = low(layer_norm(token_block, gain_one, bias_one))
    bias_row = jnp.concatenate([mix_bias[:D], jnp.zeros((D,), jnp.float32), mix_bias[D:]])
    projected = matmul(first, mix_weight) + bias_row
    queries = low(low_back(projected[:, :D] * HEAD_DIM ** (-0.5)))
    key_rows = low(low_back(projected[:, D:2 * D]))
    values = low(low_back(projected[:, 2 * D:]))
    query_heads = queries.reshape(TOK_DEV, HEADS, HEAD_DIM)
    key_heads = key_rows.reshape(TOK_DEV, HEADS, HEAD_DIM)
    value_heads = values.reshape(TOK_DEV, HEADS, HEAD_DIM)
    scores = low_back(jnp.einsum('qhd,khd->hqk', query_heads, key_heads, precision=lax.Precision.HIGHEST))
    scores = jnp.where(allowed[None], scores, -1e+30)
    row_top = lax.optimization_barrier(jnp.max(scores, -1, keepdims=True))
    powered = jnp.exp(scores - row_top)
    probability = powered / lax.optimization_barrier(jnp.sum(powered, -1, keepdims=True))
    attended = jnp.einsum('hqk,khd->qhd', low(probability), value_heads, precision=lax.Precision.HIGHEST)
    attended = low(low_back(attended.reshape(TOK_DEV, D)))
    residual = token_block + low_back(matmul(attended, proj_weight) + proj_bias)
    second = low(layer_norm(residual, gain_two, bias_two))
    inner = low_back(matmul(second, up_weight) + up_bias)
    active = low(jax.nn.gelu(inner, approximate=False))
    branch = low_back(matmul(active, down_weight) + down_bias)
    return jnp.where(valid_slot[:, None], residual + branch, 0.0)

def reference(tokens, segments, norm1_gain, norm1_bias, qkv_weight, qv_bias, out_weight, out_bias, norm2_gain, norm2_bias, fc1_weight, fc1_bias, fc2_weight, fc2_bias, cotangent):
    masters = (norm1_gain, norm1_bias, qkv_weight, qv_bias, out_weight, out_bias, norm2_gain, norm2_bias, fc1_weight, fc1_bias, fc2_weight, fc2_bias)
    segment_blocks = segments.reshape(TOKENS // TOK_DEV, TOK_DEV)
    checked = jax.checkpoint(block_forward)

    def forward(token_input, *weights_in):
        rounded = tuple((low(weight) for weight in weights_in))
        token_blocks = token_input.reshape(TOKENS // TOK_DEV, TOK_DEV, D)
        blocks_out = lax.map(lambda inputs: checked(inputs[0], inputs[1], rounded), (token_blocks, segment_blocks))
        return blocks_out.reshape(TOKENS, D)
    activations, pullback = jax.vjp(forward, tokens, *masters)
    grads = pullback(cotangent)
    return (activations, grads[0], grads[1], grads[2], grads[3], grads[4], grads[5], grads[6], grads[7], grads[8], grads[9], grads[10], grads[11], grads[12])
```

```python
import functools
from functools import partial

import jax
import jax.numpy as jnp
from jax import lax
from jax.experimental import pallas as pl
from jax.experimental.pallas import tpu as pltpu
from jax.sharding import PartitionSpec as P

HEAD_DIM = 64
IMG_DEV = 1
MESH = pl.DeviceIdType.MESH


def layer_norm(rows_in, gain, bias):
    centre = rows_in - jnp.mean(rows_in, -1, keepdims=True)
    spread = jnp.mean(centre * centre, -1, keepdims=True)
    return centre * lax.rsqrt(spread + 1e-06) * gain + bias


def halved(array_in):
    return array_in.astype(jnp.bfloat16)


def contract_rows(left, right):
    return lax.dot_general(
        left, right, (((0,), (0,)), ((), ())), preferred_element_type=jnp.float32
    )


def contract_cols(left, right):
    return lax.dot_general(
        left, right, (((1,), (1,)), ((), ())), preferred_element_type=jnp.float32
    )


def head_pairs(block):
    return block.reshape(block.shape[0], -1, 2 * HEAD_DIM).transpose(1, 0, 2)


def join_pairs(stack):
    return stack.transpose(1, 0, 2).reshape(stack.shape[1], stack.shape[0] * stack.shape[2])


def masked_scores(query_heads, key_heads, allowed):
    scores = jnp.einsum("qhd,khd->hqk", query_heads, key_heads, preferred_element_type=jnp.float32)
    return jnp.where(allowed[None], scores, -1e30)


def pair_forward(pieces, allowed):
    q_pair, k_pair, v_pair = pieces
    row_count = q_pair.shape[0]
    query_heads = q_pair.reshape(row_count, 2, HEAD_DIM)
    key_heads = k_pair.reshape(row_count, 2, HEAD_DIM)
    value_heads = v_pair.reshape(row_count, 2, HEAD_DIM)
    scores = masked_scores(query_heads, key_heads, allowed)
    row_top = jnp.max(scores, -1, keepdims=True)
    powered = jnp.exp(scores - row_top)
    totals = jnp.sum(powered, -1, keepdims=True)
    probability = halved(powered / totals)
    attended = jnp.einsum(
        "hqk,khd->qhd", probability, value_heads, preferred_element_type=jnp.float32
    )
    return (attended.reshape(row_count, 2 * HEAD_DIM), row_top + jnp.log(totals))


def pair_backward(pieces, allowed):
    q_pair, k_pair, v_pair, g_pair, lse_pair = pieces
    row_count = q_pair.shape[0]
    query_heads = q_pair.reshape(row_count, 2, HEAD_DIM)
    key_heads = k_pair.reshape(row_count, 2, HEAD_DIM)
    value_heads = v_pair.reshape(row_count, 2, HEAD_DIM)
    grad_heads = g_pair.reshape(row_count, 2, HEAD_DIM)
    probability = jnp.exp(masked_scores(query_heads, key_heads, allowed) - lse_pair)
    d_prob = jnp.einsum("qhd,khd->hqk", grad_heads, value_heads, preferred_element_type=jnp.float32)
    row_inner = jnp.sum(probability * d_prob, -1, keepdims=True)
    d_scores = halved(probability * (d_prob - row_inner))
    d_query = halved(
        jnp.einsum("hqk,khd->qhd", d_scores, key_heads, preferred_element_type=jnp.float32)
    )
    d_query = d_query * jnp.bfloat16(HEAD_DIM ** (-0.5))
    d_key = halved(
        jnp.einsum("hqk,qhd->khd", d_scores, query_heads, preferred_element_type=jnp.float32)
    )
    d_value = halved(
        jnp.einsum(
            "hqk,qhd->khd", halved(probability), grad_heads, preferred_element_type=jnp.float32
        )
    )
    width_pair = 2 * HEAD_DIM
    return (
        d_query.reshape(row_count, width_pair),
        d_key.reshape(row_count, width_pair),
        d_value.reshape(row_count, width_pair),
    )


LINE, PLANE = 4, 8

def place():
    me = lax.axis_index("dev")
    core = me % 2
    x = (me // 2) % 2
    y = (me // 4) % 2
    z = me // PLANE
    a_bit = x * (1 - core) + y * core
    b_bit = y * (1 - core) + x * core
    a_step = (2 + 2 * core) * (1 - 2 * a_bit)
    b_step = (4 - 2 * core) * (1 - 2 * b_bit)
    return me, z, core, a_step, b_step, x, y


def remote(src, dst, send_sem, recv_sem, device):
    return pltpu.make_async_remote_copy(
        src_ref=src, dst_ref=dst, send_sem=send_sem, recv_sem=recv_sem, device_id=(device,), device_id_type=MESH
    )


def wait_for(ref, sem):
    pltpu.make_async_copy(ref, ref, sem).wait()


def entry_barrier(z, devices, up, down, far):
    bar = pltpu.get_barrier_semaphore()
    for dev in devices:
        pl.semaphore_signal(bar, inc=1, device_id=(dev,), device_id_type=MESH)

    @pl.when(z < LINE - 1)
    def _():
        pl.semaphore_signal(bar, inc=1, device_id=(up,), device_id_type=MESH)

    @pl.when(z > 0)
    def _():
        pl.semaphore_signal(bar, inc=1, device_id=(down,), device_id_type=MESH)

    pl.semaphore_signal(bar, inc=1, device_id=(far,), device_id_type=MESH)
    count = len(devices) + 1
    inner = (z > 0) & (z < LINE - 1)

    @pl.when(inner)
    def _():
        pl.semaphore_wait(bar, count + 2)

    @pl.when(jnp.logical_not(inner))
    def _():
        pl.semaphore_wait(bar, count + 1)


class Vec:
    def __init__(self, held, got, send, recv):
        me, z, core, _, _, x, y = place()
        self.to = [
            me + 1 - 2 * core,
            me + 2 - 4 * x,
            me + 4 - 8 * y,
            me + 8 - 16 * (z % 2),
            me + 16 - 32 * (z // 2),
        ]
        self.held, self.got, self.send, self.recv = held, got, send, recv

    def copy(self, i):
        return remote(self.held.at[i], self.got.at[i], self.send.at[i], self.recv.at[i], self.to[i])

    def start(self, i):
        self.copy(i).start()

    def step(self, i):
        self.copy(i).wait()
        self.held[i + 1] = self.held[i] + self.got[i]
        if i < 4:
            self.start(i + 1)


class Gather:
    def __init__(self, piece, shard, full, z_first, send, recv, core_recv, own):
        self.p, self.shard, self.full, self.z_first = piece, shard, full, z_first
        self.send, self.recv, self.core_recv, self.own_sem = send, recv, core_recv, own
        self.rows = shard.shape[0]
        self.me, self.z, self.core, self.a_step, self.b_step, _, _ = place()
        self.sib = self.me + 1 - 2 * self.core

    def block(self, dev):
        return self.full.at[pl.ds(pl.multiple_of(dev * self.rows, self.rows), self.rows)]

    def ici(self, src, dev, way, to):
        remote(src, self.block(dev), self.send.at[self.p, way], self.recv.at[self.p, dev // 2], to).start()

    def to_a(self, src, dev):
        self.ici(src, dev, 0, self.me + self.a_step)

    def to_b(self, src, dev):
        self.ici(src, dev, 1, self.me + self.b_step)

    def to_core(self, src, dev):
        remote(src, self.block(dev), self.send.at[self.p, 2], self.core_recv.at[self.p], self.sib).start()

    def up(self, src, dev):
        @pl.when(self.z < LINE - 1)
        def _():
            self.ici(src, dev, 3, self.me + PLANE)

    def down(self, src, dev):
        @pl.when(self.z > 0)
        def _():
            self.ici(src, dev, 3, self.me - PLANE)

    def arrive(self, dev):
        wait_for(self.block(dev), self.recv.at[self.p, dev // 2])

    def own(self):
        pltpu.make_async_copy(self.shard, self.block(self.me), self.own_sem.at[self.p]).start()
        src = self.shard
        if self.z_first:
            self.up(src, self.me)
            self.down(src, self.me)
            self.to_a(src, self.me)
        else:
            self.to_a(src, self.me)
            self.up(src, self.me)
            self.down(src, self.me)
        self.to_b(src, self.me)
        self.to_core(src, self.me)

    def from_a(self, k=None):
        if not self.z_first:
            dev = self.me + self.a_step
            self.arrive(dev)
            src = self.block(dev)
            self.up(src, dev)
            self.down(src, dev)
            self.to_b(src, dev)
            self.to_core(src, dev)
            return

        def one(dev):
            self.arrive(dev)
            src = self.block(dev)
            self.to_b(src, dev)
            self.to_core(src, dev)

        self.sides(k, lambda off: one(self.me + self.a_step + off))

    def sides(self, k, fn):
        if k == 0:
            fn(0)
            return

        @pl.when(self.z >= k)
        def _():
            fn(-PLANE * k)

        @pl.when(self.z + k <= LINE - 1)
        def _():
            fn(PLANE * k)

    def from_z(self, k):
        for base in [self.me] if self.z_first else [self.me, self.me + self.a_step]:

            @pl.when(self.z >= k)
            def _():
                dev = base - PLANE * k
                self.arrive(dev)
                src = self.block(dev)
                self.up(src, dev)
                if self.z_first:
                    self.to_a(src, dev)
                self.to_b(src, dev)
                self.to_core(src, dev)

            @pl.when(self.z + k <= LINE - 1)
            def _():
                dev = base + PLANE * k
                self.arrive(dev)
                src = self.block(dev)
                self.down(src, dev)
                if self.z_first:
                    self.to_a(src, dev)
                self.to_b(src, dev)
                self.to_core(src, dev)

    def from_b(self, k):
        for base in [self.me + self.b_step, self.me + self.b_step + self.a_step]:

            def one(off):
                dev = base + off
                self.arrive(dev)
                self.to_core(self.block(dev), dev)

            self.sides(k, one)

    def many(self, count):
        return self.full.at[pl.ds(0, count * self.rows)]

    def ready(self):
        wait_for(self.shard, self.own_sem.at[self.p])
        wait_for(self.many(16), self.core_recv.at[self.p])

    def drain(self):
        a_count = 4 if self.z_first else 1
        z_unit = 1 if self.z_first else 2
        wait_for(self.many(a_count), self.send.at[self.p, 0])
        wait_for(self.many(8), self.send.at[self.p, 1])
        wait_for(self.many(16), self.send.at[self.p, 2])
        inner = (self.z > 0) & (self.z < LINE - 1)

        @pl.when(inner)
        def _():
            wait_for(self.many(5 * z_unit), self.send.at[self.p, 3])

        @pl.when(jnp.logical_not(inner))
        def _():
            wait_for(self.many(z_unit), self.send.at[self.p, 3])


def add_blocks(dst, terms, rows):
    def body(i, carry):
        r = pl.multiple_of(i * 16, 16)
        total = terms[0][pl.ds(r, 16), :].astype(jnp.float32)
        for term in terms[1:]:
            total = total + term[pl.ds(r, 16), :].astype(jnp.float32)
        dst[pl.ds(r, 16), :] = total.astype(dst.dtype)
        return carry

    lax.fori_loop(0, rows // 16, body, 0)


class Scatter:
    def __init__(self, piece, grad, out, z_first, mine, sib_buf, b_buf, z_buf, a_buf, send, load, c_recv, b_recv, z_recv, a_recv):
        self.p, self.grad, self.out, self.z_first = piece, grad, out, z_first
        self.mine, self.sib_buf, self.b_buf, self.z_buf, self.a_buf = mine, sib_buf, b_buf, z_buf, a_buf
        self.send, self.load, self.c_recv, self.b_recv, self.z_recv, self.a_recv = send, load, c_recv, b_recv, z_recv, a_recv
        self.rows = out.shape[0]
        self.me, self.z, self.core, self.a_step, self.b_step, self.x, self.y = place()
        self.sib = self.me + 1 - 2 * self.core

    def block(self, dev):
        return self.grad.at[pl.ds(pl.multiple_of(dev * self.rows, self.rows), self.rows)]

    def sides(self, k, fn):
        if k == 0:
            fn(0)
            return

        @pl.when(self.z >= k)
        def _():
            fn(-k)

        @pl.when(self.z + k <= LINE - 1)
        def _():
            fn(k)

    def order(self):
        return [3, 2, 1, 0]

    def exchange(self):
        def one(dev):
            chip = dev // 2
            pltpu.make_async_copy(self.block(dev), self.mine.at[chip], self.load.at[self.p, chip]).start()
            sdev = dev + 1 - 2 * self.core
            remote(self.block(sdev), self.sib_buf.at[chip], self.send.at[self.p, 2], self.c_recv.at[self.p, chip], self.sib).start()

        for b in (self.b_step, 0):
            for k in self.order():
                for a in (self.a_step, 0):
                    self.sides(k, lambda s: one(self.me + b + a + PLANE * s))

    def local(self, dev):
        chip = dev // 2
        wait_for(self.mine.at[chip], self.load.at[self.p, chip])
        wait_for(self.sib_buf.at[chip], self.c_recv.at[self.p, chip])
        return [self.mine.at[chip], self.sib_buf.at[chip]]

    def send_b(self, k):
        for a in (self.a_step, 0):

            def one(s):
                dev = self.me + self.b_step + a + PLANE * s
                chip = dev // 2
                terms = self.local(dev)
                add_blocks(self.mine.at[chip], terms, self.rows)
                slot = self.b_slot(dev)
                remote(self.mine.at[chip], self.b_buf.at[slot], self.send.at[self.p, 1], self.b_recv.at[self.p, slot], self.me + self.b_step).start()

            self.sides(k, one)

    def b_slot(self, dev):
        x = (dev // 2) % 2
        y = (dev // 4) % 2
        a_bit = x * (1 - self.core) + y * self.core
        return (dev // PLANE) * 2 + a_bit

    def after_b(self, dev):
        slot = self.b_slot(dev)
        wait_for(self.b_buf.at[slot], self.b_recv.at[self.p, slot])
        return self.local(dev) + [self.b_buf.at[slot]]

    def a_slot(self, dev):
        return dev // PLANE if self.z_first else 0

    def send_a(self, dev, terms):
        chip = dev // 2
        add_blocks(self.mine.at[chip], terms, self.rows)
        slot = self.a_slot(dev)
        remote(self.mine.at[chip], self.a_buf.at[slot], self.send.at[self.p, 0], self.a_recv.at[self.p, slot], self.me + self.a_step).start()

    def send_a_early(self, k):
        def one(s):
            dev = self.me + self.a_step + PLANE * s
            self.send_a(dev, self.after_b(dev))

        self.sides(k, one)

    def after_a(self, dev):
        slot = self.a_slot(dev)
        wait_for(self.a_buf.at[slot], self.a_recv.at[self.p, slot])
        return [self.a_buf.at[slot]]

    def z_index(self, i, dest):
        return i * 5 + dest

    def along_z(self, k):
        for i, a in [(0, 0)] if self.z_first else [(1, self.a_step), (0, 0)]:
            for sign in (-1, 1):

                @pl.when((self.z >= k) if sign < 0 else (self.z + k <= LINE - 1))
                def _():
                    dev = self.me + a + sign * PLANE * k
                    chip = dev // 2
                    dest = self.z + sign * k
                    terms = self.after_b(dev)
                    if self.z_first:
                        terms = terms + self.after_a(dev)
                    slot = self.z_index(i, dest)
                    last = k == 1
                    there = self.z_index(i, LINE) if (last and sign > 0) else slot
                    more = (self.z < LINE - 1) if sign < 0 else (self.z > 0)

                    @pl.when(more)
                    def _():
                        wait_for(self.z_buf.at[slot], self.z_recv.at[self.p, slot])
                        add_blocks(self.mine.at[chip], terms + [self.z_buf.at[slot]], self.rows)

                    @pl.when(jnp.logical_not(more))
                    def _():
                        add_blocks(self.mine.at[chip], terms, self.rows)

                    remote(self.mine.at[chip], self.z_buf.at[there], self.send.at[self.p, 3], self.z_recv.at[self.p, there], self.me + sign * PLANE).start()

    def at_home(self, i, a):
        dev = self.me + a
        chip = dev // 2
        terms = self.after_b(dev)
        if self.z_first:
            terms = terms + self.after_a(dev)
        above = self.z_index(i, self.z)
        below = self.z_index(i, LINE)
        def finish(terms):
            if i == 1:
                add_blocks(self.mine.at[chip], terms, self.rows)
            else:
                if not self.z_first:
                    terms = terms + self.after_a(dev)
                add_blocks(self.out, terms, self.rows)

        for has_above, has_below, cond in (
            (True, False, self.z == 0),
            (True, True, (self.z > 0) & (self.z < LINE - 1)),
            (False, True, self.z == LINE - 1),
        ):

            @pl.when(cond)
            def _():
                more = list(terms)
                if has_above:
                    wait_for(self.z_buf.at[above], self.z_recv.at[self.p, above])
                    more.append(self.z_buf.at[above])
                if has_below:
                    wait_for(self.z_buf.at[below], self.z_recv.at[self.p, below])
                    more.append(self.z_buf.at[below])
                finish(more)

        if i == 1:
            remote(self.mine.at[chip], self.a_buf.at[0], self.send.at[self.p, 0], self.a_recv.at[self.p, 0], self.me + self.a_step).start()

    def stages(self):
        first = [functools.partial(self.send_b, k) for k in self.order()]
        second = []
        if self.z_first:
            second += [functools.partial(self.send_a_early, k) for k in self.order()]
            second += [functools.partial(self.along_z, k) for k in (3, 2, 1)]
            third = [functools.partial(self.at_home, 0, 0)]
        else:
            second += [functools.partial(self.along_z, k) for k in (3, 2, 1)]
            second += [functools.partial(self.at_home, 1, self.a_step)]
            third = [functools.partial(self.at_home, 0, 0)]
        return first, second, third

    def drain(self):
        wait_for(self.mine, self.send.at[self.p, 2])
        wait_for(self.mine.at[pl.ds(0, 8)], self.send.at[self.p, 1])
        wait_for(self.mine.at[pl.ds(0, 4 if self.z_first else 1)], self.send.at[self.p, 0])
        wait_for(self.mine.at[pl.ds(0, 3 if self.z_first else 6)], self.send.at[self.p, 3])


def peers():
    me, z, core, a_step, b_step, x, y = place()
    near = [me + 1 - 2 * core, me + a_step, me + b_step]
    return z, near, me + PLANE, me - PLANE, me + 16 - 32 * (z // 2)


Z_FIRST = (False, False, True, False)


def gather_kernel(shards, vec, fulls, vec_out, held, got, send, recv, core_recv, own, vsend, vrecv):
    z, near, up, down, far = peers()
    entry_barrier(z, near, up, down, far)
    held[0] = vec[...]
    v = Vec(held, got, vsend, vrecv)
    v.start(0)
    q, o, u, d = [Gather(p, shards[p], fulls[p], Z_FIRST[p], send, recv, core_recv, own) for p in range(4)]
    q.own(); o.own()
    v.step(0)
    q.from_a(); o.from_a()
    v.step(1)
    u.own()
    q.from_z(1); o.from_z(1)
    v.step(2)
    u.from_z(1)
    q.from_z(2); o.from_z(2)
    v.step(3)
    u.from_z(2)
    d.own()
    q.from_z(3); o.from_z(3)
    v.step(4)
    u.from_z(3)
    d.from_a()
    for k in range(4):
        q.from_b(k); o.from_b(k)
    u.from_a(0)
    d.from_z(1)
    u.from_a(1)
    d.from_z(2)
    u.from_a(2)
    d.from_z(3)
    u.from_a(3)
    for k in range(4):
        u.from_b(k); d.from_b(k)
    vec_out[...] = held[5]
    for g in (q, o, u, d):
        g.ready()
    for g in (q, o, u, d):
        g.drain()


def gather_all(shards, vec):
    count = len(shards)
    n = 32

    def kernel(*refs):
        sh, v = refs[:count], refs[count]
        fulls, vo = refs[count + 1 : 2 * count + 1], refs[2 * count + 1]
        gather_kernel(sh, v, fulls, vo, *refs[2 * count + 2 :])

    anyspec = pl.BlockSpec(memory_space=pl.ANY)
    vm = pl.BlockSpec(memory_space=pltpu.VMEM)
    dma = pltpu.SemaphoreType.DMA
    return pl.pallas_call(
        kernel,
        out_shape=[jax.ShapeDtypeStruct((n * s.shape[0], s.shape[1]), s.dtype) for s in shards] + [jax.ShapeDtypeStruct(vec.shape, vec.dtype)],
        in_specs=[anyspec] * count + [vm],
        out_specs=[anyspec] * count + [vm],
        scratch_shapes=[
            pltpu.VMEM((6,) + vec.shape, jnp.float32),
            pltpu.VMEM((5,) + vec.shape, jnp.float32),
            dma((count, 4)), dma((count, 16)), dma((count,)), dma((count,)), dma((5,)), dma((5,)),
        ],
        compiler_params=pltpu.CompilerParams(collective_id=0, has_side_effects=True),
    )(*shards, vec)


def scatter_kernel(grads, vec, outs, vec_out, bufs, held, got, send, load, c_recv, b_recv, z_recv, a_recv, vsend, vrecv, order):
    z, near, up, down, far = peers()
    entry_barrier(z, near, up, down, far)
    pieces = {}
    for p in order:
        pieces[p] = Scatter(p, grads[p], outs[p], Z_FIRST[p], *bufs[5 * p : 5 * p + 5], send, load, c_recv, b_recv, z_recv, a_recv)
        pieces[p].exchange()
    held[0] = vec[...]
    v = Vec(held, got, vsend, vrecv)
    v.start(0)
    st = [pieces[p].stages() for p in order]
    seq = []
    n = len(order)
    for i in range(n + 2):
        groups = []
        if i < n:
            groups.append(st[i][0])
        if 0 <= i - 1 < n:
            groups.append(st[i - 1][1])
        if 0 <= i - 2 < n:
            groups.append(st[i - 2][2])
        longest = max(len(g) for g in groups)
        for j in range(longest):
            for g in groups:
                if j < len(g):
                    seq.append(g[j])
    step = 0
    for i, fn in enumerate(seq):
        fn()
        if i % 4 == 3 and step < 5:
            v.step(step)
            step += 1
    vec_out[...] = held[5]
    for p in order:
        pieces[p].drain()


def scatter_all(grads, vec):
    count = len(grads)
    n = 32

    def kernel(*refs):
        gr, v = refs[:count], refs[count]
        outs, vo = refs[count + 1 : 2 * count + 1], refs[2 * count + 1]
        rest = refs[2 * count + 2 :]
        scatter_kernel(gr, v, outs, vo, rest[: 5 * count], *rest[5 * count :], order=(3, 2, 1, 0))

    anyspec = pl.BlockSpec(memory_space=pl.ANY)
    vm = pl.BlockSpec(memory_space=pltpu.VMEM)
    dma = pltpu.SemaphoreType.DMA
    bufs = []
    for p, g in enumerate(grads):
        blk = (g.shape[0] // n, g.shape[1])
        zf = Z_FIRST[p]
        bufs += [pltpu.VMEM((c,) + blk, jnp.bfloat16) for c in (16, 16, 8, 5 if zf else 10, 4 if zf else 1)]
    return pl.pallas_call(
        kernel,
        out_shape=[jax.ShapeDtypeStruct((g.shape[0] // n, g.shape[1]), jnp.float32) for g in grads] + [jax.ShapeDtypeStruct(vec.shape, vec.dtype)],
        in_specs=[anyspec] * count + [vm],
        out_specs=[vm] * (count + 1),
        scratch_shapes=bufs
        + [
            pltpu.VMEM((6,) + vec.shape, jnp.float32),
            pltpu.VMEM((5,) + vec.shape, jnp.float32),
            dma((count, 4)), dma((count, 16)), dma((count, 16)), dma((count, 8)), dma((count, 10)), dma((count, 4)), dma((5,)), dma((5,)),
        ],
        compiler_params=pltpu.CompilerParams(collective_id=1, has_side_effects=True, vmem_limit_bytes=56 << 20),
    )(*grads, vec)

VECTOR_ROWS = 16


def spread_vectors(parts, position, count):
    rows = []
    for part in parts:
        size = part.shape[0]
        whole = jnp.where(
            (jnp.arange(count) == position)[:, None], halved(part).astype(jnp.float32)[None], 0.0
        )
        rows.append(whole.reshape(size * count))
    return jnp.concatenate(rows)


def local_math(tokens, segments, cotangent, vectors, weights):
    gain_one, bias_one, mix_bias, proj_bias, gain_two, bias_two, up_bias, down_bias = vectors
    mix_weight, proj_weight, up_weight, down_weight = weights
    model_width = tokens.shape[1]
    valid_slot = segments < IMG_DEV
    allowed = (segments[:, None] == segments[None, :]) & valid_slot[None, :]
    gain_one_f = gain_one.astype(jnp.float32)
    bias_one_f = bias_one.astype(jnp.float32)
    first = halved(layer_norm(tokens, gain_one_f, bias_one_f))
    mix_bias_f = mix_bias.astype(jnp.float32)
    bias_row = jnp.concatenate(
        [mix_bias_f[:model_width], jnp.zeros((model_width,), jnp.float32), mix_bias_f[model_width:]]
    )
    projected = jnp.dot(first, mix_weight, preferred_element_type=jnp.float32) + bias_row
    queries = halved(projected[:, :model_width] * HEAD_DIM ** (-0.5))
    key_rows = halved(projected[:, model_width : 2 * model_width])
    values = halved(projected[:, 2 * model_width :])
    attended_stack, lse_stack = lax.map(
        lambda pieces: pair_forward(pieces, allowed),
        (head_pairs(queries), head_pairs(key_rows), head_pairs(values)),
    )
    attended = halved(join_pairs(attended_stack))
    residual = (
        tokens
        + jnp.dot(attended, proj_weight, preferred_element_type=jnp.float32)
        + proj_bias.astype(jnp.float32)
    )
    gain_two_f = gain_two.astype(jnp.float32)
    bias_two_f = bias_two.astype(jnp.float32)
    second = halved(layer_norm(residual, gain_two_f, bias_two_f))
    inner = jnp.dot(second, up_weight, preferred_element_type=jnp.float32) + up_bias.astype(
        jnp.float32
    )
    active = halved(jax.nn.gelu(inner, approximate=False))
    branch = jnp.dot(active, down_weight, preferred_element_type=jnp.float32) + down_bias.astype(
        jnp.float32
    )
    activations = jnp.where(valid_slot[:, None], residual + branch, 0.0)
    d_out = jnp.where(valid_slot[:, None], cotangent, 0.0)
    d_mlp = halved(d_out)
    grad_fc2_bias = jnp.sum(d_mlp, 0, dtype=jnp.float32)
    grad_fc2_weight = contract_rows(active, d_mlp)
    d_active = contract_cols(d_mlp, down_weight)
    gelu_back = jax.vjp(partial(jax.nn.gelu, approximate=False), inner)[1]
    d_inner = halved(gelu_back(d_active)[0])
    grad_fc1_bias = jnp.sum(d_inner, 0, dtype=jnp.float32)
    grad_fc1_weight = contract_rows(second, d_inner)
    d_second = contract_cols(d_inner, up_weight)
    norm_two_back = jax.vjp(layer_norm, residual, gain_two_f, bias_two_f)[1]
    d_norm2, grad_norm2_gain, grad_norm2_bias = norm_two_back(d_second)
    d_resid = d_out + d_norm2
    d_branch = halved(d_resid)
    grad_out_bias = jnp.sum(d_branch, 0, dtype=jnp.float32)
    grad_out_weight = contract_rows(attended, d_branch)
    d_attended = halved(contract_cols(d_branch, proj_weight))
    d_query_stack, d_key_stack, d_value_stack = lax.map(
        lambda pieces: pair_backward(pieces, allowed),
        (
            head_pairs(queries),
            head_pairs(key_rows),
            head_pairs(values),
            head_pairs(d_attended),
            lse_stack,
        ),
    )
    d_query = join_pairs(d_query_stack)
    d_value = join_pairs(d_value_stack)
    d_projected = jnp.concatenate([d_query, join_pairs(d_key_stack), d_value], 1)
    grad_qv_bias = jnp.concatenate(
        [jnp.sum(d_query, 0, dtype=jnp.float32), jnp.sum(d_value, 0, dtype=jnp.float32)]
    )
    grad_qkv_weight = contract_rows(first, d_projected)
    d_first = contract_cols(d_projected, mix_weight)
    norm_one_back = jax.vjp(layer_norm, tokens, gain_one_f, bias_one_f)[1]
    d_norm1, grad_norm1_gain, grad_norm1_bias = norm_one_back(d_first)
    input_grad = d_resid + d_norm1
    return (
        activations,
        input_grad,
        (grad_qkv_weight, grad_out_weight, grad_fc1_weight, grad_fc2_weight),
        (
            grad_norm1_gain,
            grad_norm1_bias,
            grad_qv_bias,
            grad_out_bias,
            grad_norm2_gain,
            grad_norm2_bias,
            grad_fc1_bias,
            grad_fc2_bias,
        ),
    )


def shards(count, tokens,
    segments,
    norm1_gain,
    norm1_bias,
    qkv_weight,
    qv_bias,
    out_weight,
    out_bias,
    norm2_gain,
    norm2_bias,
    fc1_weight,
    fc1_bias,
    fc2_weight,
    fc2_bias,
    cotangent,
):
    vector_shards = (norm1_gain, norm1_bias, qv_bias, out_bias, norm2_gain, norm2_bias, fc1_bias, fc2_bias)
    weight_shards = tuple(halved(w) for w in (qkv_weight, out_weight, fc1_weight, fc2_weight))
    sizes = [v.shape[0] * count for v in vector_shards]
    starts = [sum(sizes[:i]) for i in range(len(sizes) + 1)]
    width = tokens.shape[1]
    position = lax.axis_index("dev")
    kernels = count == 32

    def packed(flat):
        rows = flat.reshape(-1, width)
        return jnp.pad(rows, ((0, VECTOR_ROWS - rows.shape[0]), (0, 0)))

    if kernels:
        *weights, vector_rows = gather_all(
            weight_shards, packed(spread_vectors(vector_shards, position, count))
        )
        flat = vector_rows.reshape(-1)
        vectors = [flat[starts[i] : starts[i + 1]] for i in range(len(sizes))]
    else:
        weights = [lax.all_gather(w, "dev", axis=0, tiled=True) for w in weight_shards]
        vectors = [
            lax.all_gather(halved(v), "dev", axis=0, tiled=True).astype(jnp.float32)
            for v in vector_shards
        ]
    activations, input_grad, weight_grads, vector_grads = local_math(
        tokens, segments, cotangent, vectors, weights
    )
    if kernels:
        *weight_owned, vector_rows = scatter_all(
            [halved(g) for g in weight_grads], packed(jnp.concatenate(vector_grads))
        )
        flat = vector_rows.reshape(-1)
        vector_owned = [
            lax.dynamic_slice(flat, (starts[i] + position * (sizes[i] // count),), (sizes[i] // count,))
            for i in range(len(sizes))
        ]
    else:
        weight_owned = [
            lax.psum_scatter(g, "dev", scatter_dimension=0, tiled=True) for g in weight_grads
        ]
        vector_owned = [
            lax.psum_scatter(g, "dev", scatter_dimension=0, tiled=True) for g in vector_grads
        ]
    g1, b1, qvb, ob, g2, b2, f1b, f2b = vector_owned
    qkv_g, out_g, fc1_g, fc2_g = weight_owned
    return (activations, input_grad, g1, b1, qkv_g, qvb, out_g, ob, g2, b2, fc1_g, f1b, fc2_g, f2b)


def solution(mesh):
    in_specs = (
        P("dev", None),
        P("dev"),
        P("dev"),
        P("dev"),
        P("dev", None),
        P("dev"),
        P("dev", None),
        P("dev"),
        P("dev"),
        P("dev"),
        P("dev", None),
        P("dev"),
        P("dev", None),
        P("dev"),
        P("dev", None),
    )
    out_specs = (
        P("dev", None),
        P("dev", None),
        P("dev"),
        P("dev"),
        P("dev", None),
        P("dev"),
        P("dev", None),
        P("dev"),
        P("dev"),
        P("dev"),
        P("dev", None),
        P("dev"),
        P("dev", None),
        P("dev"),
    )
    return jax.shard_map(
        partial(shards, mesh.size), mesh=mesh, in_specs=in_specs, out_specs=out_specs, check_vma=False)
```

```python
import functools
from functools import partial

import jax
import jax.numpy as jnp
from jax import lax
from jax.experimental import pallas as pl
from jax.experimental.pallas import tpu as pltpu
from jax.sharding import PartitionSpec as P

HEAD_DIM = 64
IMG_DEV = 1
MESH = pl.DeviceIdType.MESH


def layer_norm(rows_in, gain, bias):
    centre = rows_in - jnp.mean(rows_in, -1, keepdims=True)
    spread = jnp.mean(centre * centre, -1, keepdims=True)
    return centre * lax.rsqrt(spread + 1e-06) * gain + bias


def halved(array_in):
    return array_in.astype(jnp.bfloat16)


def contract_rows(left, right):
    return lax.dot_general(
        left, right, (((0,), (0,)), ((), ())), preferred_element_type=jnp.float32
    )


def contract_cols(left, right):
    return lax.dot_general(
        left, right, (((1,), (1,)), ((), ())), preferred_element_type=jnp.float32
    )


def head_pairs(block):
    return block.reshape(block.shape[0], -1, 2 * HEAD_DIM).transpose(1, 0, 2)


def join_pairs(stack):
    return stack.transpose(1, 0, 2).reshape(stack.shape[1], stack.shape[0] * stack.shape[2])


def masked_scores(query_heads, key_heads, allowed):
    scores = jnp.einsum("qhd,khd->hqk", query_heads, key_heads, preferred_element_type=jnp.float32)
    return jnp.where(allowed[None], scores, -1e30)


def pair_forward(pieces, allowed):
    q_pair, k_pair, v_pair = pieces
    row_count = q_pair.shape[0]
    query_heads = q_pair.reshape(row_count, 2, HEAD_DIM)
    key_heads = k_pair.reshape(row_count, 2, HEAD_DIM)
    value_heads = v_pair.reshape(row_count, 2, HEAD_DIM)
    scores = masked_scores(query_heads, key_heads, allowed)
    row_top = jnp.max(scores, -1, keepdims=True)
    powered = jnp.exp(scores - row_top)
    totals = jnp.sum(powered, -1, keepdims=True)
    probability = halved(powered / totals)
    attended = jnp.einsum(
        "hqk,khd->qhd", probability, value_heads, preferred_element_type=jnp.float32
    )
    return (attended.reshape(row_count, 2 * HEAD_DIM), row_top + jnp.log(totals))


def pair_backward(pieces, allowed):
    q_pair, k_pair, v_pair, g_pair, lse_pair = pieces
    row_count = q_pair.shape[0]
    query_heads = q_pair.reshape(row_count, 2, HEAD_DIM)
    key_heads = k_pair.reshape(row_count, 2, HEAD_DIM)
    value_heads = v_pair.reshape(row_count, 2, HEAD_DIM)
    grad_heads = g_pair.reshape(row_count, 2, HEAD_DIM)
    probability = jnp.exp(masked_scores(query_heads, key_heads, allowed) - lse_pair)
    d_prob = jnp.einsum("qhd,khd->hqk", grad_heads, value_heads, preferred_element_type=jnp.float32)
    row_inner = jnp.sum(probability * d_prob, -1, keepdims=True)
    d_scores = halved(probability * (d_prob - row_inner))
    d_query = halved(
        jnp.einsum("hqk,khd->qhd", d_scores, key_heads, preferred_element_type=jnp.float32)
    )
    d_query = d_query * jnp.bfloat16(HEAD_DIM ** (-0.5))
    d_key = halved(
        jnp.einsum("hqk,qhd->khd", d_scores, query_heads, preferred_element_type=jnp.float32)
    )
    d_value = halved(
        jnp.einsum(
            "hqk,qhd->khd", halved(probability), grad_heads, preferred_element_type=jnp.float32
        )
    )
    width_pair = 2 * HEAD_DIM
    return (
        d_query.reshape(row_count, width_pair),
        d_key.reshape(row_count, width_pair),
        d_value.reshape(row_count, width_pair),
    )


LINE, PLANE = 4, 8

def place():
    me = lax.axis_index("dev")
    core = me % 2
    x = (me // 2) % 2
    y = (me // 4) % 2
    z = me // PLANE
    a_bit = x * (1 - core) + y * core
    b_bit = y * (1 - core) + x * core
    a_step = (2 + 2 * core) * (1 - 2 * a_bit)
    b_step = (4 - 2 * core) * (1 - 2 * b_bit)
    return me, z, core, a_step, b_step, x, y


def remote(src, dst, send_sem, recv_sem, device):
    return pltpu.make_async_remote_copy(
        src_ref=src, dst_ref=dst, send_sem=send_sem, recv_sem=recv_sem, device_id=(device,), device_id_type=MESH
    )


def wait_for(ref, sem):
    pltpu.make_async_copy(ref, ref, sem).wait()


def entry_barrier(z, devices, up, down, far):
    bar = pltpu.get_barrier_semaphore()
    for dev in devices:
        pl.semaphore_signal(bar, inc=1, device_id=(dev,), device_id_type=MESH)

    @pl.when(z < LINE - 1)
    def _():
        pl.semaphore_signal(bar, inc=1, device_id=(up,), device_id_type=MESH)

    @pl.when(z > 0)
    def _():
        pl.semaphore_signal(bar, inc=1, device_id=(down,), device_id_type=MESH)

    pl.semaphore_signal(bar, inc=1, device_id=(far,), device_id_type=MESH)
    count = len(devices) + 1
    inner = (z > 0) & (z < LINE - 1)

    @pl.when(inner)
    def _():
        pl.semaphore_wait(bar, count + 2)

    @pl.when(jnp.logical_not(inner))
    def _():
        pl.semaphore_wait(bar, count + 1)


class Vec:
    def __init__(self, held, got, send, recv):
        me, z, core, _, _, x, y = place()
        self.to = [
            me + 1 - 2 * core,
            me + 2 - 4 * x,
            me + 4 - 8 * y,
            me + 8 - 16 * (z % 2),
            me + 16 - 32 * (z // 2),
        ]
        self.held, self.got, self.send, self.recv = held, got, send, recv

    def copy(self, i):
        return remote(self.held.at[i], self.got.at[i], self.send.at[i], self.recv.at[i], self.to[i])

    def start(self, i):
        self.copy(i).start()

    def step(self, i):
        self.copy(i).wait()
        self.held[i + 1] = self.held[i] + self.got[i]
        if i < 4:
            self.start(i + 1)


class Gather:
    def __init__(self, piece, shard, full, z_first, send, recv, core_recv, own):
        self.p, self.shard, self.full, self.z_first = piece, shard, full, z_first
        self.send, self.recv, self.core_recv, self.own_sem = send, recv, core_recv, own
        self.rows = shard.shape[0]
        self.me, self.z, self.core, self.a_step, self.b_step, _, _ = place()
        self.sib = self.me + 1 - 2 * self.core

    def block(self, dev):
        return self.full.at[pl.ds(pl.multiple_of(dev * self.rows, self.rows), self.rows)]

    def ici(self, src, dev, way, to):
        remote(src, self.block(dev), self.send.at[self.p, way], self.recv.at[self.p, dev // 2], to).start()

    def to_a(self, src, dev):
        self.ici(src, dev, 0, self.me + self.a_step)

    def to_b(self, src, dev):
        self.ici(src, dev, 1, self.me + self.b_step)

    def to_core(self, src, dev):
        remote(src, self.block(dev), self.send.at[self.p, 2], self.core_recv.at[self.p], self.sib).start()

    def up(self, src, dev):
        @pl.when(self.z < LINE - 1)
        def _():
            self.ici(src, dev, 3, self.me + PLANE)

    def down(self, src, dev):
        @pl.when(self.z > 0)
        def _():
            self.ici(src, dev, 3, self.me - PLANE)

    def arrive(self, dev):
        wait_for(self.block(dev), self.recv.at[self.p, dev // 2])

    def own(self):
        pltpu.make_async_copy(self.shard, self.block(self.me), self.own_sem.at[self.p]).start()
        src = self.shard
        if self.z_first:
            self.up(src, self.me)
            self.down(src, self.me)
            self.to_a(src, self.me)
        else:
            self.to_a(src, self.me)
            self.up(src, self.me)
            self.down(src, self.me)
        self.to_b(src, self.me)
        self.to_core(src, self.me)

    def from_a(self, k=None):
        if not self.z_first:
            dev = self.me + self.a_step
            self.arrive(dev)
            src = self.block(dev)
            self.up(src, dev)
            self.down(src, dev)
            self.to_b(src, dev)
            self.to_core(src, dev)
            return

        def one(dev):
            self.arrive(dev)
            src = self.block(dev)
            self.to_b(src, dev)
            self.to_core(src, dev)

        self.sides(k, lambda off: one(self.me + self.a_step + off))

    def sides(self, k, fn):
        if k == 0:
            fn(0)
            return

        @pl.when(self.z >= k)
        def _():
            fn(-PLANE * k)

        @pl.when(self.z + k <= LINE - 1)
        def _():
            fn(PLANE * k)

    def from_z(self, k):
        for base in [self.me] if self.z_first else [self.me, self.me + self.a_step]:

            @pl.when(self.z >= k)
            def _():
                dev = base - PLANE * k
                self.arrive(dev)
                src = self.block(dev)
                self.up(src, dev)
                if self.z_first:
                    self.to_a(src, dev)
                self.to_b(src, dev)
                self.to_core(src, dev)

            @pl.when(self.z + k <= LINE - 1)
            def _():
                dev = base + PLANE * k
                self.arrive(dev)
                src = self.block(dev)
                self.down(src, dev)
                if self.z_first:
                    self.to_a(src, dev)
                self.to_b(src, dev)
                self.to_core(src, dev)

    def from_b(self, k):
        for base in [self.me + self.b_step, self.me + self.b_step + self.a_step]:

            def one(off):
                dev = base + off
                self.arrive(dev)
                self.to_core(self.block(dev), dev)

            self.sides(k, one)

    def many(self, count):
        return self.full.at[pl.ds(0, count * self.rows)]

    def ready(self):
        wait_for(self.shard, self.own_sem.at[self.p])
        wait_for(self.many(16), self.core_recv.at[self.p])

    def drain(self):
        a_count = 4 if self.z_first else 1
        z_unit = 1 if self.z_first else 2
        wait_for(self.many(a_count), self.send.at[self.p, 0])
        wait_for(self.many(8), self.send.at[self.p, 1])
        wait_for(self.many(16), self.send.at[self.p, 2])
        inner = (self.z > 0) & (self.z < LINE - 1)

        @pl.when(inner)
        def _():
            wait_for(self.many(5 * z_unit), self.send.at[self.p, 3])

        @pl.when(jnp.logical_not(inner))
        def _():
            wait_for(self.many(z_unit), self.send.at[self.p, 3])


def add_blocks(dst, terms, rows):
    def body(i, carry):
        r = pl.multiple_of(i * 16, 16)
        total = terms[0][pl.ds(r, 16), :].astype(jnp.float32)
        for term in terms[1:]:
            total = total + term[pl.ds(r, 16), :].astype(jnp.float32)
        dst[pl.ds(r, 16), :] = total.astype(dst.dtype)
        return carry

    lax.fori_loop(0, rows // 16, body, 0)


def peers():
    me, z, core, a_step, b_step, x, y = place()
    near = [me + 1 - 2 * core, me + a_step, me + b_step]
    return z, near, me + PLANE, me - PLANE, me + 16 - 32 * (z // 2)


Z_FIRST = (False, False, True, False)


EPS = 1e-06
PAIR = 128
TILE = 512
ROWS = 32
GAIN_ONE, BIAS_ONE, QUERY_BIAS, VALUE_BIAS, OUT_BIAS, GAIN_TWO, BIAS_TWO, UP_BIAS, DOWN_BIAS = 0, 1, 2, 3, 4, 5, 6, 7, 11


def dot(left, right):
    return jnp.dot(left, right, preferred_element_type=jnp.float32)


def dot_nt(left, right):
    return lax.dot_general(left, right, (((1,), (1,)), ((), ())), preferred_element_type=jnp.float32)


def dot_tn(left, right):
    return lax.dot_general(left, right, (((0,), (0,)), ((), ())), preferred_element_type=jnp.float32)


def columns(start, size):
    return pl.ds(pl.multiple_of(start, 128), size)


def loop(count, body):
    def step(i, carry):
        body(i)
        return carry

    lax.fori_loop(0, count, step, 0)


def centred(rows):
    centre = rows - jnp.mean(rows, -1, keepdims=True)
    spread = jnp.mean(centre * centre, -1, keepdims=True)
    return centre, lax.rsqrt(spread + EPS)


def norm_into(dst, src, vec, gain_row, bias_row):
    gain = vec[gain_row : gain_row + 1, :]
    bias = vec[bias_row : bias_row + 1, :]

    def body(i):
        r = pl.ds(pl.multiple_of(i * ROWS, ROWS), ROWS)
        centre, scale = centred(src[r, :])
        dst[r, :] = (centre * scale * gain + bias).astype(dst.dtype)

    loop(src.shape[0] // ROWS, body)


def norm_back(d_rows, src, vec, gain_row, sums, emit):
    gain = vec[gain_row : gain_row + 1, :]
    sums[...] = jnp.zeros_like(sums)

    def body(i):
        r = pl.ds(pl.multiple_of(i * ROWS, ROWS), ROWS)
        centre, scale = centred(src[r, :])
        n = centre * scale
        d = d_rows[r, :]
        e = d * gain
        dn = d * n
        for part in range(ROWS // 8):
            sums[0:8, :] += dn[8 * part : 8 * part + 8, :]
            sums[8:16, :] += d[8 * part : 8 * part + 8, :]
        back = scale * (e - jnp.mean(e, -1, keepdims=True) - n * jnp.mean(e * n, -1, keepdims=True))
        emit(r, back)

    loop(src.shape[0] // ROWS, body)


def mask_bias(out, seg_col, seg_row):
    row = seg_row[...]
    allowed = (seg_col[...] == row) & (row < IMG_DEV)
    out[...] = jnp.where(allowed, 0.0, -1e30)


def own_half(rows, head):
    lane = lax.broadcasted_iota(jnp.int32, rows.shape, 1)
    inside = (lane < HEAD_DIM) if head == 0 else (lane >= HEAD_DIM)
    return jnp.where(inside, rows, jnp.zeros_like(rows))


def halves(first, second):
    lane = lax.broadcasted_iota(jnp.int32, first.shape, 1)
    return jnp.where(lane < HEAD_DIM, first, second)


def probabilities(query, key, bias):
    scores = dot_nt(query, key) + bias
    powered = jnp.exp(scores - jnp.max(scores, -1, keepdims=True))
    return powered * (1.0 / jnp.sum(powered, -1, keepdims=True))


def attend_pair(i, width, qkv, bias, attended):
    q = qkv[:, columns(i * PAIR, PAIR)]
    k = qkv[:, columns(width + i * PAIR, PAIR)]
    v = qkv[:, columns(2 * width + i * PAIR, PAIR)]
    parts = []
    for head in (0, 1):
        p = probabilities(own_half(q, head), k, bias[...]).astype(jnp.bfloat16)
        parts.append(dot(p, v))
    attended[:, columns(i * PAIR, PAIR)] = halves(*parts).astype(jnp.bfloat16)


class Forward:
    def __init__(self, width, hidden, tokens, seg_col, seg_row, cotangent, vec, weights, s):
        self.width, self.hidden = width, hidden
        self.tokens, self.seg_col, self.seg_row, self.cotangent, self.vec = tokens, seg_col, seg_row, cotangent, vec
        self.wq, self.wo, self.wu, self.wd = weights
        self.__dict__.update(s)

    def start(self):
        mask_bias(self.bias, self.seg_col, self.seg_row)
        valid = self.seg_col[...] < IMG_DEV
        self.d_mlp[...] = jnp.where(valid, self.cotangent[...], 0.0).astype(jnp.bfloat16)

    def first_norm(self):
        norm_into(self.first, self.tokens, self.vec, GAIN_ONE, BIAS_ONE)

    def project(self, part):
        w = self.width

        def body(j):
            c = columns(part * w + j * TILE, TILE)
            out = dot(self.first[...], self.wq[:, c])
            if part == 0:
                out = (out + self.vec[QUERY_BIAS : QUERY_BIAS + 1, columns(j * TILE, TILE)]) * HEAD_DIM ** (-0.5)
            elif part == 2:
                out = out + self.vec[VALUE_BIAS : VALUE_BIAS + 1, columns(j * TILE, TILE)]
            self.qkv[:, c] = out.astype(jnp.bfloat16)

        loop(w // TILE, body)

    def attend(self, begin, count):
        loop(count, lambda i: attend_pair(begin + i, self.width, self.qkv, self.bias, self.attended))

    def project_out(self):
        def body(j):
            c = columns(j * TILE, TILE)
            self.residual[:, c] = (
                self.tokens[:, c] + dot(self.attended[...], self.wo[:, c]) + self.vec[OUT_BIAS : OUT_BIAS + 1, c]
            )

        loop(self.width // TILE, body)

    def second_norm(self):
        norm_into(self.second, self.residual, self.vec, GAIN_TWO, BIAS_TWO)

    def up(self, begin, count):
        per = self.width // TILE

        def body(n):
            j = begin + n
            c = columns(j * TILE, TILE)
            t = dot(self.second[...], self.wu[:, c])
            t = t + self.vec[pl.ds(UP_BIAS + j // per, 1), columns((j % per) * TILE, TILE)]
            cdf = 0.5 + 0.5 * lax.erf(t * (0.5**0.5))
            act = (t * cdf).astype(jnp.bfloat16)
            self.active[:, c] = act
            for part in range(TILE // 128):
                own = self.split.at[part % 2]
                own[:, columns((2 * j + part // 2) * 128, 128)] = act[:, 128 * part : 128 * part + 128]
            self.slope[:, c] = cdf + t * (0.3989422804014327 * jnp.exp(-0.5 * t * t))

        loop(count, body)

    def d_inner_tiles(self, begin, count):
        per = self.width // TILE

        def body(n):
            j = begin + n
            rows = pl.ds(pl.multiple_of(j * TILE, TILE), TILE)
            c = columns(j * TILE, TILE)
            d = (dot_nt(self.d_mlp[...], self.wd[rows, :]) * self.slope[:, c]).astype(jnp.bfloat16)
            self.d_inner[:, c] = d
            self.gvec[pl.ds(UP_BIAS + j // per, 1), columns((j % per) * TILE, TILE)] = jnp.sum(
                d.astype(jnp.float32), 0, keepdims=True
            )

        loop(count, body)

    def down(self):
        valid = self.seg_col[...] < IMG_DEV

        def body(j):
            c = columns(j * TILE, TILE)
            branch = dot(self.active[...], self.wd[:, c]) + self.vec[DOWN_BIAS : DOWN_BIAS + 1, c]
            self.activations[:, c] = jnp.where(valid, self.residual[:, c] + branch, 0.0)
            self.gvec[DOWN_BIAS : DOWN_BIAS + 1, c] = jnp.sum(self.d_mlp[:, c].astype(jnp.float32), 0, keepdims=True)

        loop(self.width // TILE, body)

    def d_second_rows(self):
        size = TILE // 2

        def body(j):
            rows = pl.ds(pl.multiple_of(j * size, size), size)
            self.d_norm[:, columns(j * size, size)] = dot_nt(self.d_inner[...], self.wu[rows, :])

        loop(self.width // size, body)

    def second_norm_back(self):
        def emit(r, back):
            valid = self.seg_col[r, :] < IMG_DEV
            d_resid = jnp.where(valid, self.cotangent[r, :], 0.0) + back
            self.d_resid[r, :] = d_resid
            self.d_branch[r, :] = d_resid.astype(jnp.bfloat16)

        norm_back(self.d_norm, self.residual, self.vec, GAIN_TWO, self.sums, emit)
        self.gvec[GAIN_TWO : GAIN_TWO + 1, :] = jnp.sum(self.sums[0:8, :], 0, keepdims=True)
        self.gvec[BIAS_TWO : BIAS_TWO + 1, :] = jnp.sum(self.sums[8:16, :], 0, keepdims=True)


FORWARD_OUT = ("activations", "d_resid", "first", "qkv", "attended", "second", "split", "d_inner", "d_mlp", "d_branch")


def forward_all(count, tokens, segments, cotangent, shards, vec, comm=True):
    rows, width = tokens.shape
    hidden = shards[2].shape[1]
    f32, b16 = jnp.float32, jnp.bfloat16
    kinds = {
        "activations": ((rows, width), f32),
        "d_resid": ((rows, width), f32),
        "first": ((rows, width), b16),
        "qkv": ((rows, 3 * width), b16),
        "attended": ((rows, width), b16),
        "second": ((rows, width), b16),
        "active": ((rows, hidden), b16),
        "split": ((2, rows, hidden // 2), b16),
        "d_branch": ((rows, width), b16),
        "d_inner": ((rows, hidden), b16),
        "d_mlp": ((rows, width), b16),
        "residual": ((rows, width), f32),
        "slope": ((rows, hidden), f32),
        "d_norm": ((rows, width), f32),
        "bias": ((rows, rows), f32),
        "sums": ((16, width), f32),
    }
    names = list(kinds)
    fulls = [((count * s.shape[0], s.shape[1]), b16) for s in shards]

    def kernel(tok, sc, sr, cot, q_sh, o_sh, u_sh, d_sh, v_in, *refs):
        outs = dict(zip(FORWARD_OUT, refs[: len(FORWARD_OUT)]))
        refs = refs[len(FORWARD_OUT) :]
        wq_out, wo_out, vec_out, gvec = refs[:4]
        refs = refs[4:]
        s = dict(zip(names, refs[: len(names)]))
        refs = refs[len(names) :]
        weights = refs[:4]
        held, got, send, recv, core_recv, own, vsend, vrecv, out_sem = refs[4:]
        s["gvec"] = gvec
        started = []

        def put(src, dst):
            copy = pltpu.make_async_copy(src, dst, out_sem.at[len(started)])
            copy.start()
            started.append(copy)

        def leave(*which):
            for name in which:
                put(s[name], outs[name])

        f = Forward(width, hidden, tok, sc, sr, cot, vec_out, weights, s)
        z, near, up, down, far = peers()
        entry_barrier(z, near, up, down, far)
        held[0] = v_in[...]
        v = Vec(held, got, vsend, vrecv)
        v.start(0)
        q, o, u, d = [
            Gather(p, sh, weights[p], Z_FIRST[p], send, recv, core_recv, own)
            for p, sh in enumerate((q_sh, o_sh, u_sh, d_sh))
        ]
        gvec[...] = jnp.zeros_like(gvec)
        q.own()
        o.own()
        v.step(0)
        q.from_a()
        o.from_a()
        v.step(1)
        u.own()
        q.from_z(1)
        o.from_z(1)
        v.step(2)
        u.from_z(1)
        q.from_z(2)
        o.from_z(2)
        v.step(3)
        u.from_z(2)
        d.own()
        q.from_z(3)
        o.from_z(3)
        v.step(4)
        vec_out[...] = held[5]
        u.from_z(3)
        d.from_a()
        f.start()
        q.from_b(0)
        o.from_b(0)
        q.from_b(1)
        o.from_b(1)
        f.first_norm()
        leave("d_mlp", "first")
        u.from_a(0)
        d.from_z(1)
        q.from_b(2)
        o.from_b(2)
        q.from_b(3)
        o.from_b(3)
        u.from_a(1)
        d.from_z(2)
        q.ready()
        put(weights[0], wq_out)
        f.project(0)
        u.from_a(2)
        d.from_z(3)
        f.project(1)
        u.from_a(3)
        u.from_b(0)
        d.from_b(0)
        f.project(2)
        leave("qkv")
        u.from_b(1)
        d.from_b(1)
        f.attend(0, 2)
        u.from_b(2)
        f.attend(2, 2)
        u.from_b(3)
        f.attend(4, 2)
        d.from_b(2)
        f.attend(6, 2)
        leave("attended")
        o.ready()
        put(weights[1], wo_out)
        f.project_out()
        d.from_b(3)
        f.second_norm()
        leave("second")
        u.ready()
        f.up(0, hidden // TILE)
        leave("split")
        d.ready()
        f.d_inner_tiles(0, hidden // TILE)
        leave("d_inner")
        f.d_second_rows()
        f.down()
        leave("activations")
        f.second_norm_back()
        leave("d_resid", "d_branch")
        for g in (q, o, u, d):
            g.drain()
        for copy in started:
            copy.wait()

    anyspec = pl.BlockSpec(memory_space=pl.ANY)
    vm = pl.BlockSpec(memory_space=pltpu.VMEM)
    dma = pltpu.SemaphoreType.DMA
    n = len(shards)
    shape = jax.ShapeDtypeStruct
    results = pl.pallas_call(
        kernel,
        out_shape=[shape(*kinds[k]) for k in FORWARD_OUT]
        + [shape(*fulls[0]), shape(*fulls[1]), shape(vec.shape, f32), shape(vec.shape, f32)],
        in_specs=[vm] * 4 + [anyspec] * n + [vm],
        out_specs=[anyspec] * (len(FORWARD_OUT) + 2) + [vm] * 2,
        scratch_shapes=[pltpu.VMEM(*kinds[k]) for k in names]
        + [pltpu.VMEM(*f) for f in fulls]
        + [
            pltpu.VMEM((6,) + vec.shape, f32),
            pltpu.VMEM((5,) + vec.shape, f32),
            dma((n, 4)),
            dma((n, 16)),
            dma((n,)),
            dma((n,)),
            dma((5,)),
            dma((5,)),
            dma((len(FORWARD_OUT) + 2,)),
        ],
        compiler_params=pltpu.CompilerParams(collective_id=0, has_side_effects=True, vmem_limit_bytes=60 << 20),
    )(tokens, segments.reshape(rows, 1), segments.reshape(1, rows), cotangent, *shards, vec)
    saved = dict(zip(FORWARD_OUT, results))
    saved["wq"], saved["wo"], saved["vec"], saved["gvec"] = results[len(FORWARD_OUT) :]
    return saved


UNITS = 4
UNIT = 32
CHIPS = 16


class Reduce:
    def __init__(self, piece, z_first, mine, b_buf, z_buf, a_buf, send, b_recv, z_recv, a_recv, emit):
        self.p, self.z_first, self.emit = piece, z_first, emit
        self.mine, self.b_buf, self.z_buf, self.a_buf = mine, b_buf, z_buf, a_buf
        self.send, self.b_recv, self.z_recv, self.a_recv = send, b_recv, z_recv, a_recv
        self.rows = mine.shape[1]
        self.me, self.z, self.core, self.a_step, self.b_step, self.x, self.y = place()

    def sides(self, k, fn):
        if k == 0:
            fn(0)
            return

        @pl.when(self.z >= k)
        def _():
            fn(-k)

        @pl.when(self.z + k <= LINE - 1)
        def _():
            fn(k)

    def b_slot(self, dev):
        x = (dev // 2) % 2
        y = (dev // 4) % 2
        a_bit = x * (1 - self.core) + y * self.core
        return (dev // PLANE) * 2 + a_bit

    def send_b(self, k):
        for a in (self.a_step, 0):

            def one(s):
                dev = self.me + self.b_step + a + PLANE * s
                slot = self.b_slot(dev)
                remote(
                    self.mine.at[dev // 2],
                    self.b_buf.at[slot],
                    self.send.at[self.p, 1],
                    self.b_recv.at[self.p, slot],
                    self.me + self.b_step,
                ).start()

            self.sides(k, one)

    def after_b(self, dev):
        slot = self.b_slot(dev)
        wait_for(self.b_buf.at[slot], self.b_recv.at[self.p, slot])
        return [self.mine.at[dev // 2], self.b_buf.at[slot]]

    def a_slot(self, dev):
        return dev // PLANE if self.z_first else 0

    def to_a(self, dev):
        slot = self.a_slot(dev)
        remote(
            self.mine.at[dev // 2],
            self.a_buf.at[slot],
            self.send.at[self.p, 0],
            self.a_recv.at[self.p, slot],
            self.me + self.a_step,
        ).start()

    def send_a(self, k):
        def one(s):
            dev = self.me + self.a_step + PLANE * s
            add_blocks(self.mine.at[dev // 2], self.after_b(dev), self.rows)
            self.to_a(dev)

        self.sides(k, one)

    def after_a(self, dev):
        slot = self.a_slot(dev)
        wait_for(self.a_buf.at[slot], self.a_recv.at[self.p, slot])
        return [self.a_buf.at[slot]]

    def z_slot(self, i, dest):
        return i * (LINE + 1) + dest

    def along_z(self, k):
        for i, a in [(0, 0)] if self.z_first else [(1, self.a_step), (0, 0)]:
            for sign in (-1, 1):

                @pl.when((self.z >= k) if sign < 0 else (self.z + k <= LINE - 1))
                def _():
                    dev = self.me + a + sign * PLANE * k
                    chip = dev // 2
                    terms = self.after_b(dev)
                    if self.z_first:
                        terms = terms + self.after_a(dev)
                    slot = self.z_slot(i, self.z + sign * k)
                    there = self.z_slot(i, LINE) if (k == 1 and sign > 0) else slot
                    more = (self.z < LINE - 1) if sign < 0 else (self.z > 0)

                    @pl.when(more)
                    def _():
                        wait_for(self.z_buf.at[slot], self.z_recv.at[self.p, slot])
                        add_blocks(self.mine.at[chip], terms + [self.z_buf.at[slot]], self.rows)

                    @pl.when(jnp.logical_not(more))
                    def _():
                        add_blocks(self.mine.at[chip], terms, self.rows)

                    remote(
                        self.mine.at[chip],
                        self.z_buf.at[there],
                        self.send.at[self.p, 3],
                        self.z_recv.at[self.p, there],
                        self.me + sign * PLANE,
                    ).start()

    def home_terms(self, i, dev, fn):
        terms = self.after_b(dev)
        if self.z_first:
            terms = terms + self.after_a(dev)
        above = self.z_slot(i, self.z)
        below = self.z_slot(i, LINE)
        for has_above, has_below, cond in (
            (True, False, self.z == 0),
            (True, True, (self.z > 0) & (self.z < LINE - 1)),
            (False, True, self.z == LINE - 1),
        ):

            @pl.when(cond)
            def _():
                more = list(terms)
                for slot, has in ((above, has_above), (below, has_below)):
                    if has:
                        wait_for(self.z_buf.at[slot], self.z_recv.at[self.p, slot])
                        more.append(self.z_buf.at[slot])
                fn(more)

    def home_a(self):
        dev = self.me + self.a_step
        self.home_terms(1, dev, lambda terms: add_blocks(self.mine.at[dev // 2], terms, self.rows))
        self.to_a(dev)

    def home(self):
        def finish(terms):
            if not self.z_first:
                terms = terms + self.after_a(self.me)
            for chunk in range(self.rows // 16):
                r = slice(16 * chunk, 16 * chunk + 16)
                total = terms[0][r, :].astype(jnp.float32)
                for term in terms[1:]:
                    total = total + term[r, :].astype(jnp.float32)
                self.emit(chunk, total)

        self.home_terms(0, self.me, finish)

    def stages(self):
        if self.z_first:
            later = [functools.partial(self.send_a, k) for k in (3, 2, 1, 0)]
            later += [functools.partial(self.along_z, k) for k in (3, 2, 1)]
            return later + [self.home]
        return [functools.partial(self.along_z, k) for k in (3, 2, 1)] + [self.home_a, self.home]

    def send_all_b(self):
        for k in (3, 2, 1, 0):
            self.send_b(k)

    def drain(self):
        wait_for(self.mine.at[pl.ds(0, 8)], self.send.at[self.p, 1])
        wait_for(self.mine.at[pl.ds(0, 4 if self.z_first else 1)], self.send.at[self.p, 0])
        wait_for(self.mine.at[pl.ds(0, 3 if self.z_first else 6)], self.send.at[self.p, 3])


def attend_back_pair(i, width, qkv, d_attended, bias, d_proj, gvec):
    rows = d_attended.shape[0]
    q = qkv[:, columns(i * PAIR, PAIR)]
    k = qkv[:, columns(width + i * PAIR, PAIR)]
    v = qkv[:, columns(2 * width + i * PAIR, PAIR)]
    g = d_attended[:, columns(i * PAIR, PAIR)]
    d_query, d_key, d_value = [], 0.0, 0.0
    for head in (0, 1):
        qh, gh = own_half(q, head), own_half(g, head)
        p = probabilities(qh, k, bias[...])
        d_p = dot_nt(gh, v)
        inner = jnp.sum(p * d_p, -1, keepdims=True)
        d_s = (p * (d_p - inner)).astype(jnp.bfloat16)
        d_query.append(dot(d_s, k))
        d_key = d_key + dot_tn(d_s, qh)
        d_value = d_value + dot_tn(p.astype(jnp.bfloat16), gh)
    d_q = halves(*d_query).astype(jnp.bfloat16).astype(jnp.float32) * HEAD_DIM ** (-0.5)
    d_v = d_value.astype(jnp.bfloat16)
    top = pl.ds(0, rows)
    d_proj[top, columns(i * PAIR, PAIR)] = d_q.astype(jnp.bfloat16)
    d_proj[top, columns(width + i * PAIR, PAIR)] = d_key.astype(jnp.bfloat16)
    d_proj[top, columns(2 * width + i * PAIR, PAIR)] = d_v
    gvec[QUERY_BIAS : QUERY_BIAS + 1, columns(i * PAIR, PAIR)] = jnp.sum(d_q, 0, keepdims=True)
    gvec[VALUE_BIAS : VALUE_BIAS + 1, columns(i * PAIR, PAIR)] = jnp.sum(
        d_v.astype(jnp.float32), 0, keepdims=True
    )


def transpose_blocks(stack, turned):
    def body(i):
        part = stack[:, columns(i * 128, 128)].astype(jnp.float32).T.astype(jnp.bfloat16)
        turned[pl.ds(2 * i, 2)] = part.reshape(2, 2, UNIT, stack.shape[0])

    loop(stack.shape[1] // 128, body)


def turned_product(turned, core, right, mine, unit, right_column):
    width = mine.shape[2]
    tokens = turned.shape[3]

    def body(j):
        left = turned[:, pl.ds(core, 1)].reshape(CHIPS * UNIT, tokens)
        out = dot(left, right[:, columns(right_column + j * TILE, TILE)]).astype(jnp.bfloat16)
        mine[:, UNIT * unit : UNIT * unit + UNIT, columns(j * TILE, TILE)] = out.reshape(CHIPS, UNIT, TILE)

    loop(width // TILE, body)


SAVED_IN = ("d_resid", "first", "qkv", "attended", "second", "active", "d_inner", "d_mlp", "d_branch", "wq", "wo")


def backward_all(count, tokens, segments, saved):
    rows, width = tokens.shape
    hidden = saved["d_inner"].shape[1]
    f32, b16 = jnp.float32, jnp.bfloat16
    both = 2 * rows
    half = hidden // 2
    block = (hidden // count, width)
    z_first = (False, True, False)
    kinds = {
        "x_active": ((both, half), b16),
        "y_mlp": ((both, width), b16),
        "y_inner": ((both, hidden), b16),
        "x_second": ((both, width), b16),
        "x_attended": ((both, width), b16),
        "y_branch": ((both, width), b16),
        "x_first": ((both, width), b16),
        "y_proj": ((both, 3 * width), b16),
        "turned": ((CHIPS, 2, UNIT, both), b16),
        "qkv": ((rows, 3 * width), b16),
        "wo": (saved["wo"].shape, b16),
        "wq": ((2, TILE // 2, 3 * width), b16),
        "d_attended": ((rows, width), b16),
        "d_norm": ((rows, width), f32),
        "d_resid": ((rows, width), f32),
        "bias": ((rows, rows), f32),
        "sums": ((16, width), f32),
        "gvec": (saved["gvec"].shape, f32),
    }
    names = list(kinds)
    sent = ("active", "d_mlp", "second", "d_inner", "attended", "d_branch", "first")
    stacks = ("x_active", "y_mlp", "x_second", "y_inner", "x_attended", "y_branch", "x_first")

    def kernel(tok, sc, sr, vec, gvec_in, *refs):
        src = dict(zip(SAVED_IN, refs[: len(SAVED_IN)]))
        refs = refs[len(SAVED_IN) :]
        grad_out, q_out, o_out, u_out, d_out, gvec_out = refs[:6]
        refs = refs[6:]
        s = dict(zip(names, refs[: len(names)]))
        refs = refs[len(names) :]
        bufs, refs = refs[:12], refs[12:]
        held, got, send, b_recv, z_recv, a_recv, vsend, vrecv, x_send, x_recv, load, misc = refs
        me, z, core, _, _, _, _ = place()
        sib = me + 1 - 2 * core
        _, near, up, down, far = peers()
        entry_barrier(z, near, up, down, far)

        def source(name, which):
            return src[name].at[which] if name == "active" else src[name]

        top, low = pl.ds(0, rows), pl.ds(rows, rows)

        def load_copy(i):
            return pltpu.make_async_copy(source(sent[i], core), s[stacks[i]].at[top], load.at[i])

        def cross_copy(i):
            return remote(source(sent[i], 1 - core), s[stacks[i]].at[low], x_send.at[i], x_recv.at[i], sib)

        for i in range(len(sent)):
            load_copy(i).start()
            cross_copy(i).start()
        early = [pltpu.make_async_copy(src[n], s[n], misc.at[i]) for i, n in enumerate(("qkv", "wo", "d_resid"))]
        for copy in early:
            copy.start()

        def ready(*which):
            for i in which:
                load_copy(i).wait()
                cross_copy(i).wait()

        def emit_down(chunk, total):
            d_out[16 * chunk : 16 * chunk + 16, :] = total

        def emit_up(chunk, total):
            unit, r = chunk // 2, 16 * (chunk % 2)
            u_out[r : r + 16, width * unit : width * unit + width] = total

        def emit_attn(chunk, total):
            unit, r = chunk // 2, 16 * (chunk % 2)
            if unit == 3:
                o_out[r : r + 16, :] = total
            else:
                q_out[r : r + 16, width * unit : width * unit + width] = total

        down_r, up_r, attn_r = [
            Reduce(p, z_first[p], *bufs[4 * p : 4 * p + 4], send, b_recv, z_recv, a_recv, emit)
            for p, emit in enumerate((emit_down, emit_up, emit_attn))
        ]
        gvec = s["gvec"]
        gvec[...] = gvec_in[...]
        mask_bias(s["bias"], sc, sr)
        ready(0, 1)

        def down_grad(i):
            left = s["x_active"][:, columns(i * TILE, TILE)]
            out = dot_tn(left, s["y_mlp"][...]).astype(b16)
            down_r.mine[pl.ds(4 * i, 4)] = out.reshape(4, block[0], width)

        loop(half // TILE, down_grad)
        down_r.send_all_b()
        ready(2, 3)
        transpose_blocks(s["x_second"], s["turned"])
        for unit in range(UNITS):
            turned_product(s["turned"], core, s["y_inner"], up_r.mine, unit, unit * width)
        up_r.send_all_b()
        for copy in early:
            copy.wait()
        ready(4, 5, 6)

        def d_attended_tile(j):
            size = TILE // 2
            wrows = pl.ds(pl.multiple_of(j * size, size), size)
            c = columns(j * size, size)
            s["d_attended"][:, c] = dot_nt(s["y_branch"][top, :], s["wo"][wrows, :]).astype(b16)
            gvec[OUT_BIAS : OUT_BIAS + 1, c] = jnp.sum(s["y_branch"][top, c].astype(f32), 0, keepdims=True)

        loop(width // (TILE // 2), d_attended_tile)

        def attend_back(begin, n):
            loop(
                n,
                lambda i: attend_back_pair(
                    begin + i, width, s["qkv"], s["d_attended"], s["bias"], s["y_proj"], gvec
                ),
            )

        dn, upn, att = down_r.stages(), up_r.stages(), attn_r.stages()
        attend_back(0, 2)
        dn[0]()
        attend_back(2, 2)
        dn[1]()
        upn[0]()
        attend_back(4, 2)
        dn[2]()
        upn[1]()
        attend_back(6, 2)
        proj_cross = remote(s["y_proj"].at[top], s["y_proj"].at[low], misc.at[3], misc.at[4], sib)
        proj_cross.start()
        upn[2]()
        upn[3]()
        transpose_blocks(s["x_attended"], s["turned"])
        turned_product(s["turned"], core, s["y_branch"], attn_r.mine, 3, 0)
        transpose_blocks(s["x_first"], s["turned"])
        proj_cross.wait()
        for unit in range(3):
            turned_product(s["turned"], core, s["y_proj"], attn_r.mine, unit, unit * width)
        attn_r.send_all_b()
        dn[3]()
        upn[4]()
        size = TILE // 2
        tiles = width // size

        def wq_copy(j):
            wrows = pl.ds(pl.multiple_of(j * size, size), size)
            return pltpu.make_async_copy(src["wq"].at[wrows], s["wq"].at[j % 2], load.at[len(sent) + j % 2])

        wq_copy(0).start()

        def d_first_tile(j):
            @pl.when(j + 1 < tiles)
            def _():
                wq_copy(j + 1).start()

            wq_copy(j).wait()
            s["d_norm"][:, columns(j * size, size)] = dot_nt(s["y_proj"][top, :], s["wq"][j % 2])

        for j in range(tiles):
            d_first_tile(j)
        upn[5]()

        def emit(r, back):
            s["d_resid"][r, :] += back

        norm_back(s["d_norm"], tok, vec, GAIN_ONE, s["sums"], emit)
        gvec[GAIN_ONE : GAIN_ONE + 1, :] = jnp.sum(s["sums"][0:8, :], 0, keepdims=True)
        gvec[BIAS_ONE : BIAS_ONE + 1, :] = jnp.sum(s["sums"][8:16, :], 0, keepdims=True)
        leave = pltpu.make_async_copy(s["d_resid"], grad_out, misc.at[5])
        leave.start()
        held[0] = gvec[...]
        v = Vec(held, got, vsend, vrecv)
        v.start(0)
        upn[6]()
        v.step(0)
        att[0]()
        dn[4]()
        v.step(1)
        att[1]()
        v.step(2)
        upn[7]()
        att[2]()
        v.step(3)
        att[3]()
        v.step(4)
        gvec_out[...] = held[5]
        att[4]()
        for r in (down_r, up_r, attn_r):
            r.drain()
        leave.wait()

    anyspec = pl.BlockSpec(memory_space=pl.ANY)
    vm = pl.BlockSpec(memory_space=pltpu.VMEM)
    dma = pltpu.SemaphoreType.DMA
    shape = jax.ShapeDtypeStruct
    vec_shape = saved["vec"].shape
    bufs = []
    for zf in z_first:
        bufs += [pltpu.VMEM((n,) + block, b16) for n in (CHIPS, 8, 5 if zf else 10, 4 if zf else 1)]
    outs = [
        ((rows, width), f32),
        ((width // count, 3 * width), f32),
        ((width // count, width), f32),
        ((width // count, hidden), f32),
        (block, f32),
        (vec_shape, f32),
    ]
    return pl.pallas_call(
        kernel,
        out_shape=[shape(*o) for o in outs],
        in_specs=[vm] * 5 + [anyspec] * len(SAVED_IN),
        out_specs=[anyspec] + [vm] * 5,
        scratch_shapes=[pltpu.VMEM(*kinds[k]) for k in names]
        + bufs
        + [
            pltpu.VMEM((6,) + vec_shape, f32),
            pltpu.VMEM((5,) + vec_shape, f32),
            dma((3, 4)),
            dma((3, 8)),
            dma((3, 10)),
            dma((3, 4)),
            dma((5,)),
            dma((5,)),
            dma((len(sent),)),
            dma((len(sent),)),
            dma((len(sent) + 2,)),
            dma((6,)),
        ],
        compiler_params=pltpu.CompilerParams(collective_id=1, has_side_effects=True, vmem_limit_bytes=63 << 20),
    )(
        tokens,
        segments.reshape(rows, 1),
        segments.reshape(1, rows),
        saved["vec"],
        saved["gvec"],
        *[saved[k] for k in SAVED_IN],
    )


VECTOR_ROWS = 16


def spread_vectors(parts, position, count):
    rows = []
    for part in parts:
        size = part.shape[0]
        whole = jnp.where(
            (jnp.arange(count) == position)[:, None], lax.reduce_precision(part, 8, 7)[None], 0.0
        )
        rows.append(whole.reshape(size * count))
    return jnp.concatenate(rows)


def local_math(tokens, segments, cotangent, vectors, weights):
    gain_one, bias_one, mix_bias, proj_bias, gain_two, bias_two, up_bias, down_bias = vectors
    mix_weight, proj_weight, up_weight, down_weight = weights
    model_width = tokens.shape[1]
    valid_slot = segments < IMG_DEV
    allowed = (segments[:, None] == segments[None, :]) & valid_slot[None, :]
    gain_one_f = gain_one.astype(jnp.float32)
    bias_one_f = bias_one.astype(jnp.float32)
    first = halved(layer_norm(tokens, gain_one_f, bias_one_f))
    mix_bias_f = mix_bias.astype(jnp.float32)
    bias_row = jnp.concatenate(
        [mix_bias_f[:model_width], jnp.zeros((model_width,), jnp.float32), mix_bias_f[model_width:]]
    )
    projected = jnp.dot(first, mix_weight, preferred_element_type=jnp.float32) + bias_row
    queries = halved(projected[:, :model_width] * HEAD_DIM ** (-0.5))
    key_rows = halved(projected[:, model_width : 2 * model_width])
    values = halved(projected[:, 2 * model_width :])
    attended_stack, lse_stack = lax.map(
        lambda pieces: pair_forward(pieces, allowed),
        (head_pairs(queries), head_pairs(key_rows), head_pairs(values)),
    )
    attended = halved(join_pairs(attended_stack))
    residual = (
        tokens
        + jnp.dot(attended, proj_weight, preferred_element_type=jnp.float32)
        + proj_bias.astype(jnp.float32)
    )
    gain_two_f = gain_two.astype(jnp.float32)
    bias_two_f = bias_two.astype(jnp.float32)
    second = halved(layer_norm(residual, gain_two_f, bias_two_f))
    inner = jnp.dot(second, up_weight, preferred_element_type=jnp.float32) + up_bias.astype(
        jnp.float32
    )
    active = halved(jax.nn.gelu(inner, approximate=False))
    branch = jnp.dot(active, down_weight, preferred_element_type=jnp.float32) + down_bias.astype(
        jnp.float32
    )
    activations = jnp.where(valid_slot[:, None], residual + branch, 0.0)
    d_out = jnp.where(valid_slot[:, None], cotangent, 0.0)
    d_mlp = halved(d_out)
    grad_fc2_bias = jnp.sum(d_mlp, 0, dtype=jnp.float32)
    grad_fc2_weight = contract_rows(active, d_mlp)
    d_active = contract_cols(d_mlp, down_weight)
    gelu_back = jax.vjp(partial(jax.nn.gelu, approximate=False), inner)[1]
    d_inner = halved(gelu_back(d_active)[0])
    grad_fc1_bias = jnp.sum(d_inner, 0, dtype=jnp.float32)
    grad_fc1_weight = contract_rows(second, d_inner)
    d_second = contract_cols(d_inner, up_weight)
    norm_two_back = jax.vjp(layer_norm, residual, gain_two_f, bias_two_f)[1]
    d_norm2, grad_norm2_gain, grad_norm2_bias = norm_two_back(d_second)
    d_resid = d_out + d_norm2
    d_branch = halved(d_resid)
    grad_out_bias = jnp.sum(d_branch, 0, dtype=jnp.float32)
    grad_out_weight = contract_rows(attended, d_branch)
    d_attended = halved(contract_cols(d_branch, proj_weight))
    d_query_stack, d_key_stack, d_value_stack = lax.map(
        lambda pieces: pair_backward(pieces, allowed),
        (
            head_pairs(queries),
            head_pairs(key_rows),
            head_pairs(values),
            head_pairs(d_attended),
            lse_stack,
        ),
    )
    d_query = join_pairs(d_query_stack)
    d_value = join_pairs(d_value_stack)
    d_projected = jnp.concatenate([d_query, join_pairs(d_key_stack), d_value], 1)
    grad_qv_bias = jnp.concatenate(
        [jnp.sum(d_query, 0, dtype=jnp.float32), jnp.sum(d_value, 0, dtype=jnp.float32)]
    )
    grad_qkv_weight = contract_rows(first, d_projected)
    d_first = contract_cols(d_projected, mix_weight)
    norm_one_back = jax.vjp(layer_norm, tokens, gain_one_f, bias_one_f)[1]
    d_norm1, grad_norm1_gain, grad_norm1_bias = norm_one_back(d_first)
    input_grad = d_resid + d_norm1
    return (
        activations,
        input_grad,
        (grad_qkv_weight, grad_out_weight, grad_fc1_weight, grad_fc2_weight),
        (
            grad_norm1_gain,
            grad_norm1_bias,
            grad_qv_bias,
            grad_out_bias,
            grad_norm2_gain,
            grad_norm2_bias,
            grad_fc1_bias,
            grad_fc2_bias,
        ),
    )


def shards(count, tokens,
    segments,
    norm1_gain,
    norm1_bias,
    qkv_weight,
    qv_bias,
    out_weight,
    out_bias,
    norm2_gain,
    norm2_bias,
    fc1_weight,
    fc1_bias,
    fc2_weight,
    fc2_bias,
    cotangent,
):
    vector_shards = (norm1_gain, norm1_bias, qv_bias, out_bias, norm2_gain, norm2_bias, fc1_bias, fc2_bias)
    weight_shards = tuple(halved(w) for w in (qkv_weight, out_weight, fc1_weight, fc2_weight))
    sizes = [v.shape[0] * count for v in vector_shards]
    starts = [sum(sizes[:i]) for i in range(len(sizes) + 1)]
    width = tokens.shape[1]
    position = lax.axis_index("dev")
    kernels = count == 32

    def packed(flat):
        rows = flat.reshape(-1, width)
        return jnp.pad(rows, ((0, VECTOR_ROWS - rows.shape[0]), (0, 0)))

    if kernels:
        saved = forward_all(
            count,
            tokens,
            segments,
            cotangent,
            weight_shards,
            packed(spread_vectors(vector_shards, position, count)),
        )
        activations = saved["activations"]
        saved["active"] = saved["split"]
        input_grad, *weight_owned, vector_rows = backward_all(count, tokens, segments, saved)
    else:
        weights = [lax.all_gather(w, "dev", axis=0, tiled=True) for w in weight_shards]
        vectors = [
            lax.all_gather(halved(v), "dev", axis=0, tiled=True).astype(jnp.float32)
            for v in vector_shards
        ]
        activations, input_grad, weight_grads, vector_grads = local_math(
            tokens, segments, cotangent, vectors, weights
        )
    if kernels:
        flat = vector_rows.reshape(-1)
        vector_owned = [
            lax.dynamic_slice(flat, (starts[i] + position * (sizes[i] // count),), (sizes[i] // count,))
            for i in range(len(sizes))
        ]
    else:
        weight_owned = [
            lax.psum_scatter(g, "dev", scatter_dimension=0, tiled=True) for g in weight_grads
        ]
        vector_owned = [
            lax.psum_scatter(g, "dev", scatter_dimension=0, tiled=True) for g in vector_grads
        ]
    g1, b1, qvb, ob, g2, b2, f1b, f2b = vector_owned
    qkv_g, out_g, fc1_g, fc2_g = weight_owned
    return (activations, input_grad, g1, b1, qkv_g, qvb, out_g, ob, g2, b2, fc1_g, f1b, fc2_g, f2b)


def solution(mesh):
    in_specs = (
        P("dev", None),
        P("dev"),
        P("dev"),
        P("dev"),
        P("dev", None),
        P("dev"),
        P("dev", None),
        P("dev"),
        P("dev"),
        P("dev"),
        P("dev", None),
        P("dev"),
        P("dev", None),
        P("dev"),
        P("dev", None),
    )
    out_specs = (
        P("dev", None),
        P("dev", None),
        P("dev"),
        P("dev"),
        P("dev", None),
        P("dev"),
        P("dev", None),
        P("dev"),
        P("dev"),
        P("dev"),
        P("dev", None),
        P("dev"),
        P("dev", None),
        P("dev"),
    )
    return jax.shard_map(
        partial(shards, mesh.size), mesh=mesh, in_specs=in_specs, out_specs=out_specs, check_vma=False)
```

```python
import functools
from functools import partial

import jax
import jax.numpy as jnp
from jax import lax
from jax.experimental import pallas as pl
from jax.experimental.pallas import tpu as pltpu
from jax.sharding import PartitionSpec as P

HEAD_DIM = 64
IMG_DEV = 1
AXIS = "dev"
MESH = pl.DeviceIdType.MESH


def layer_norm(rows_in, gain, bias):
    centre = rows_in - jnp.mean(rows_in, -1, keepdims=True)
    spread = jnp.mean(centre * centre, -1, keepdims=True)
    return centre * lax.rsqrt(spread + 1e-06) * gain + bias


def halved(array_in):
    return array_in.astype(jnp.bfloat16)


def contract_rows(left, right):
    return lax.dot_general(
        left, right, (((0,), (0,)), ((), ())), preferred_element_type=jnp.float32
    )


def contract_cols(left, right):
    return lax.dot_general(
        left, right, (((1,), (1,)), ((), ())), preferred_element_type=jnp.float32
    )


def head_pairs(block):
    return block.reshape(block.shape[0], -1, 2 * HEAD_DIM).transpose(1, 0, 2)


def join_pairs(stack):
    return stack.transpose(1, 0, 2).reshape(stack.shape[1], stack.shape[0] * stack.shape[2])


def masked_scores(query_heads, key_heads, allowed):
    scores = jnp.einsum("qhd,khd->hqk", query_heads, key_heads, preferred_element_type=jnp.float32)
    return jnp.where(allowed[None], scores, -1e30)


def pair_forward(pieces, allowed):
    q_pair, k_pair, v_pair = pieces
    row_count = q_pair.shape[0]
    query_heads = q_pair.reshape(row_count, 2, HEAD_DIM)
    key_heads = k_pair.reshape(row_count, 2, HEAD_DIM)
    value_heads = v_pair.reshape(row_count, 2, HEAD_DIM)
    scores = masked_scores(query_heads, key_heads, allowed)
    row_top = jnp.max(scores, -1, keepdims=True)
    powered = jnp.exp(scores - row_top)
    totals = jnp.sum(powered, -1, keepdims=True)
    probability = halved(powered / totals)
    attended = jnp.einsum(
        "hqk,khd->qhd", probability, value_heads, preferred_element_type=jnp.float32
    )
    return (attended.reshape(row_count, 2 * HEAD_DIM), row_top + jnp.log(totals))


def pair_backward(pieces, allowed):
    q_pair, k_pair, v_pair, g_pair, lse_pair = pieces
    row_count = q_pair.shape[0]
    query_heads = q_pair.reshape(row_count, 2, HEAD_DIM)
    key_heads = k_pair.reshape(row_count, 2, HEAD_DIM)
    value_heads = v_pair.reshape(row_count, 2, HEAD_DIM)
    grad_heads = g_pair.reshape(row_count, 2, HEAD_DIM)
    probability = jnp.exp(masked_scores(query_heads, key_heads, allowed) - lse_pair)
    d_prob = jnp.einsum("qhd,khd->hqk", grad_heads, value_heads, preferred_element_type=jnp.float32)
    row_inner = jnp.sum(probability * d_prob, -1, keepdims=True)
    d_scores = halved(probability * (d_prob - row_inner))
    d_query = halved(
        jnp.einsum("hqk,khd->qhd", d_scores, key_heads, preferred_element_type=jnp.float32)
    )
    d_query = d_query * jnp.bfloat16(HEAD_DIM ** (-0.5))
    d_key = halved(
        jnp.einsum("hqk,qhd->khd", d_scores, query_heads, preferred_element_type=jnp.float32)
    )
    d_value = halved(
        jnp.einsum(
            "hqk,qhd->khd", halved(probability), grad_heads, preferred_element_type=jnp.float32
        )
    )
    width_pair = 2 * HEAD_DIM
    return (
        d_query.reshape(row_count, width_pair),
        d_key.reshape(row_count, width_pair),
        d_value.reshape(row_count, width_pair),
    )


LINE, PLANE = 4, 8

def place():
    me = lax.axis_index(AXIS)
    core = me % 2
    x = (me // 2) % 2
    y = (me // 4) % 2
    z = me // PLANE
    a_bit = x * (1 - core) + y * core
    b_bit = y * (1 - core) + x * core
    a_step = (2 + 2 * core) * (1 - 2 * a_bit)
    b_step = (4 - 2 * core) * (1 - 2 * b_bit)
    return me, z, core, a_step, b_step, x, y


def remote(src, dst, send_sem, recv_sem, device):
    return pltpu.make_async_remote_copy(
        src_ref=src, dst_ref=dst, send_sem=send_sem, recv_sem=recv_sem, device_id=(device,), device_id_type=MESH
    )


def wait_for(ref, sem):
    pltpu.make_async_copy(ref, ref, sem).wait()


def entry_barrier(z, devices, up, down, far):
    bar = pltpu.get_barrier_semaphore()
    for dev in devices:
        pl.semaphore_signal(bar, inc=1, device_id=(dev,), device_id_type=MESH)

    @pl.when(z < LINE - 1)
    def _():
        pl.semaphore_signal(bar, inc=1, device_id=(up,), device_id_type=MESH)

    @pl.when(z > 0)
    def _():
        pl.semaphore_signal(bar, inc=1, device_id=(down,), device_id_type=MESH)

    pl.semaphore_signal(bar, inc=1, device_id=(far,), device_id_type=MESH)
    count = len(devices) + 1
    inner = (z > 0) & (z < LINE - 1)

    @pl.when(inner)
    def _():
        pl.semaphore_wait(bar, count + 2)

    @pl.when(jnp.logical_not(inner))
    def _():
        pl.semaphore_wait(bar, count + 1)


class Vec:
    def __init__(self, held, got, send, recv):
        me, z, core, _, _, x, y = place()
        self.to = [
            me + 1 - 2 * core,
            me + 2 - 4 * x,
            me + 4 - 8 * y,
            me + 8 - 16 * (z % 2),
            me + 16 - 32 * (z // 2),
        ]
        self.held, self.got, self.send, self.recv = held, got, send, recv

    def copy(self, i):
        return remote(self.held, self.got.at[i], self.send.at[i], self.recv.at[i], self.to[i])

    def start(self, i):
        self.copy(i).start()

    def step(self, i):
        self.copy(i).wait()
        self.held[...] += self.got[i]
        if i < 4:
            self.start(i + 1)


class Gather:
    def __init__(self, part, shard, full, z_first, start, size, send, recv, core_recv, own):
        self.p, self.z_first = part, z_first
        cols = pl.ds(start, size)
        self.shard, self.full, self.cols = shard.at[:, cols], full, cols
        self.send, self.recv, self.core_recv, self.own_sem = send, recv, core_recv, own
        self.rows = shard.shape[0]
        self.me, self.z, self.core, self.a_step, self.b_step, _, _ = place()
        self.sib = self.me + 1 - 2 * self.core

    def block(self, dev):
        return self.full.at[pl.ds(pl.multiple_of(dev * self.rows, self.rows), self.rows), self.cols]

    def ici(self, src, dev, way, to):
        remote(src, self.block(dev), self.send.at[self.p, way], self.recv.at[self.p, dev // 2], to).start()

    def to_a(self, src, dev):
        self.ici(src, dev, 0, self.me + self.a_step)

    def to_b(self, src, dev):
        self.ici(src, dev, 1, self.me + self.b_step)

    def to_core(self, src, dev):
        remote(src, self.block(dev), self.send.at[self.p, 2], self.core_recv.at[self.p], self.sib).start()

    def up(self, src, dev):
        @pl.when(self.z < LINE - 1)
        def _():
            self.ici(src, dev, 3, self.me + PLANE)

    def down(self, src, dev):
        @pl.when(self.z > 0)
        def _():
            self.ici(src, dev, 3, self.me - PLANE)

    def arrive(self, dev):
        wait_for(self.block(dev), self.recv.at[self.p, dev // 2])

    def own(self):
        pltpu.make_async_copy(self.shard, self.block(self.me), self.own_sem.at[self.p]).start()
        src = self.shard
        if self.z_first:
            self.up(src, self.me)
            self.down(src, self.me)
            self.to_a(src, self.me)
        else:
            self.to_a(src, self.me)
            self.up(src, self.me)
            self.down(src, self.me)
        self.to_b(src, self.me)
        self.to_core(src, self.me)

    def from_a(self, k=None):
        if not self.z_first:
            dev = self.me + self.a_step
            self.arrive(dev)
            src = self.block(dev)
            self.up(src, dev)
            self.down(src, dev)
            self.to_b(src, dev)
            self.to_core(src, dev)
            return

        def one(dev):
            self.arrive(dev)
            src = self.block(dev)
            self.to_b(src, dev)
            self.to_core(src, dev)

        self.sides(k, lambda off: one(self.me + self.a_step + off))

    def sides(self, k, fn):
        if k == 0:
            fn(0)
            return

        @pl.when(self.z >= k)
        def _():
            fn(-PLANE * k)

        @pl.when(self.z + k <= LINE - 1)
        def _():
            fn(PLANE * k)

    def from_z(self, k):
        for base in [self.me] if self.z_first else [self.me, self.me + self.a_step]:

            @pl.when(self.z >= k)
            def _():
                dev = base - PLANE * k
                self.arrive(dev)
                src = self.block(dev)
                self.up(src, dev)
                if self.z_first:
                    self.to_a(src, dev)
                self.to_b(src, dev)
                self.to_core(src, dev)

            @pl.when(self.z + k <= LINE - 1)
            def _():
                dev = base + PLANE * k
                self.arrive(dev)
                src = self.block(dev)
                self.down(src, dev)
                if self.z_first:
                    self.to_a(src, dev)
                self.to_b(src, dev)
                self.to_core(src, dev)

    def from_b(self, k):
        for base in [self.me + self.b_step, self.me + self.b_step + self.a_step]:

            def one(off):
                dev = base + off
                self.arrive(dev)
                self.to_core(self.block(dev), dev)

            self.sides(k, one)

    def many(self, count):
        return self.full.at[pl.ds(0, count * self.rows), self.cols]

    def steps(self):
        step = functools.partial
        z_steps = [step(self.from_z, k) for k in (1, 2, 3)]
        a_steps = [step(self.from_a, k) for k in range(LINE)] if self.z_first else [self.from_a]
        b_steps = [step(self.from_b, k) for k in range(LINE)]
        middle = z_steps + a_steps if self.z_first else a_steps + z_steps
        return [self.own] + middle + b_steps

    def ready(self):
        wait_for(self.shard, self.own_sem.at[self.p])
        wait_for(self.many(16), self.core_recv.at[self.p])

    def drain(self):
        a_count = 4 if self.z_first else 1
        z_unit = 1 if self.z_first else 2
        wait_for(self.many(a_count), self.send.at[self.p, 0])
        wait_for(self.many(8), self.send.at[self.p, 1])
        wait_for(self.many(16), self.send.at[self.p, 2])
        inner = (self.z > 0) & (self.z < LINE - 1)

        @pl.when(inner)
        def _():
            wait_for(self.many(5 * z_unit), self.send.at[self.p, 3])

        @pl.when(jnp.logical_not(inner))
        def _():
            wait_for(self.many(z_unit), self.send.at[self.p, 3])


def add_blocks(dst, terms, rows):
    def body(i, carry):
        r = pl.multiple_of(i * 16, 16)
        total = terms[0][pl.ds(r, 16), :].astype(jnp.float32)
        for term in terms[1:]:
            total = total + term[pl.ds(r, 16), :].astype(jnp.float32)
        dst[pl.ds(r, 16), :] = total.astype(dst.dtype)
        return carry

    lax.fori_loop(0, rows // 16, body, 0)


def peers():
    me, z, core, a_step, b_step, x, y = place()
    near = [me + 1 - 2 * core, me + a_step, me + b_step]
    return z, near, me + PLANE, me - PLANE, me + 16 - 32 * (z // 2)


GATHER_PARTS = (
    (0, 0, 0.5, True),
    (0, 0.5, 0.5, False),
    (1, 0, 1, False),
    (2, 0, 0.375, True),
    (2, 0.375, 0.625, False),
    (3, 0, 0.375, True),
    (3, 0.375, 0.625, False),
)
GROUPS = ((0, 1, 2), (3, 4), (5, 6))
LAG = 6
SPLIT_ROWS = 48


EPS = 1e-06
PAIR = 128
TILE = 512
ROWS = 32
GAIN_ONE, BIAS_ONE, QUERY_BIAS, VALUE_BIAS, OUT_BIAS, GAIN_TWO, BIAS_TWO, UP_BIAS, DOWN_BIAS = 0, 1, 2, 3, 4, 5, 6, 7, 11


def dot(left, right):
    return jnp.dot(left, right, preferred_element_type=jnp.float32)


def dot_nt(left, right):
    return lax.dot_general(left, right, (((1,), (1,)), ((), ())), preferred_element_type=jnp.float32)


def dot_tn(left, right):
    return lax.dot_general(left, right, (((0,), (0,)), ((), ())), preferred_element_type=jnp.float32)


def column_sums(block):
    return dot(jnp.ones((16, block.shape[0]), block.dtype), block)[0:1, :]


def columns(start, size):
    return pl.ds(pl.multiple_of(start, 128), size)


def loop(count, body):
    def step(i, carry):
        body(i)
        return carry

    lax.fori_loop(0, count, step, 0)


def centred(rows):
    centre = rows - jnp.mean(rows, -1, keepdims=True)
    spread = jnp.mean(centre * centre, -1, keepdims=True)
    return centre, lax.rsqrt(spread + EPS)


def norm_into(dst, src, vec, gain_row, bias_row):
    gain = vec[gain_row : gain_row + 1, :]
    bias = vec[bias_row : bias_row + 1, :]

    def body(i):
        r = pl.ds(pl.multiple_of(i * ROWS, ROWS), ROWS)
        centre, scale = centred(src[r, :])
        dst[r, :] = (centre * scale * gain + bias).astype(dst.dtype)

    loop(src.shape[0] // ROWS, body)


def norm_back(d_rows, src, vec, gain_row, sums, emit):
    gain = vec[gain_row : gain_row + 1, :]
    sums[...] = jnp.zeros_like(sums)

    def body(i):
        r = pl.ds(pl.multiple_of(i * ROWS, ROWS), ROWS)
        centre, scale = centred(src[r, :])
        n = centre * scale
        d = d_rows[r, :]
        e = d * gain
        dn = d * n
        for part in range(ROWS // 8):
            sums[0:8, :] += dn[8 * part : 8 * part + 8, :]
            sums[8:16, :] += d[8 * part : 8 * part + 8, :]
        back = scale * (e - jnp.mean(e, -1, keepdims=True) - n * jnp.mean(e * n, -1, keepdims=True))
        emit(r, back)

    loop(src.shape[0] // ROWS, body)


def own_half(rows, head):
    lane = lax.broadcasted_iota(jnp.int32, rows.shape, 1)
    inside = (lane < HEAD_DIM) if head == 0 else (lane >= HEAD_DIM)
    return jnp.where(inside, rows, jnp.zeros_like(rows))


def halves(first, second):
    lane = lax.broadcasted_iota(jnp.int32, first.shape, 1)
    return jnp.where(lane < HEAD_DIM, first, second)


def probabilities(query, key, bias):
    scores = dot_nt(query, key) + bias
    powered = jnp.exp(scores - jnp.max(scores, -1, keepdims=True))
    return powered * (1.0 / jnp.sum(powered, -1, keepdims=True))


def attend_pair(i, width, qkv, bias, attended):
    q = qkv[:, columns(i * PAIR, PAIR)]
    k = qkv[:, columns(width + i * PAIR, PAIR)]
    v = qkv[:, columns(2 * width + i * PAIR, PAIR)]
    parts = []
    for head in (0, 1):
        p = probabilities(own_half(q, head), k, bias[...]).astype(jnp.bfloat16)
        parts.append(dot(p, v))
    attended[:, columns(i * PAIR, PAIR)] = halves(*parts).astype(jnp.bfloat16)


UNITS = 4
VECTOR_ROWS = 16
UNIT = 32
CHIPS = 16


class Reduce:
    def __init__(self, part, z_first, first_row, mine, b_buf, z_buf, a_buf, send, b_recv, z_recv, a_recv, emit):
        self.p, self.z_first, self.first_row, self.emit = part, z_first, first_row, emit
        self.whole, self.b_buf, self.z_buf, self.a_buf = mine, b_buf, z_buf, a_buf
        self.send, self.b_recv, self.z_recv, self.a_recv = send, b_recv, z_recv, a_recv
        self.rows = b_buf.shape[1]
        self.me, self.z, self.core, self.a_step, self.b_step, self.x, self.y = place()

    def mine(self, chip):
        return self.whole.at[chip, pl.ds(self.first_row, self.rows)]

    def many(self, count):
        return self.whole.at[pl.ds(0, count), pl.ds(0, self.rows)]

    def sides(self, k, fn):
        if k == 0:
            fn(0)
            return

        @pl.when(self.z >= k)
        def _():
            fn(-k)

        @pl.when(self.z + k <= LINE - 1)
        def _():
            fn(k)

    def b_slot(self, dev):
        x = (dev // 2) % 2
        y = (dev // 4) % 2
        a_bit = x * (1 - self.core) + y * self.core
        return (dev // PLANE) * 2 + a_bit

    def send_plane(self, plane):
        for a in (self.a_step, 0):
            dev = self.me + self.b_step + a + PLANE * (plane - self.z)
            slot = self.b_slot(dev)
            remote(
                self.mine(dev // 2),
                self.b_buf.at[slot],
                self.send.at[self.p, 1],
                self.b_recv.at[self.p, slot],
                self.me + self.b_step,
            ).start()

    def send_b(self, k):
        self.sides(k, lambda sign: self.send_plane(self.z + sign))

    def after_b(self, dev):
        slot = self.b_slot(dev)
        wait_for(self.b_buf.at[slot], self.b_recv.at[self.p, slot])
        return [self.mine(dev // 2), self.b_buf.at[slot]]

    def a_slot(self, dev):
        return dev // PLANE if self.z_first else 0

    def to_a(self, dev):
        slot = self.a_slot(dev)
        remote(
            self.mine(dev // 2),
            self.a_buf.at[slot],
            self.send.at[self.p, 0],
            self.a_recv.at[self.p, slot],
            self.me + self.a_step,
        ).start()

    def send_a(self, k):
        def one(s):
            dev = self.me + self.a_step + PLANE * s
            add_blocks(self.mine(dev // 2), self.after_b(dev), self.rows)
            self.to_a(dev)

        self.sides(k, one)

    def after_a(self, dev):
        slot = self.a_slot(dev)
        wait_for(self.a_buf.at[slot], self.a_recv.at[self.p, slot])
        return [self.a_buf.at[slot]]

    def z_slot(self, i, dest):
        return i * (LINE + 1) + dest

    def along_z(self, k):
        for i, a in [(0, 0)] if self.z_first else [(1, self.a_step), (0, 0)]:
            for sign in (-1, 1):

                @pl.when((self.z >= k) if sign < 0 else (self.z + k <= LINE - 1))
                def _():
                    dev = self.me + a + sign * PLANE * k
                    chip = dev // 2
                    terms = self.after_b(dev)
                    if self.z_first:
                        terms = terms + self.after_a(dev)
                    slot = self.z_slot(i, self.z + sign * k)
                    there = self.z_slot(i, LINE) if (k == 1 and sign > 0) else slot
                    more = (self.z < LINE - 1) if sign < 0 else (self.z > 0)

                    @pl.when(more)
                    def _():
                        wait_for(self.z_buf.at[slot], self.z_recv.at[self.p, slot])
                        add_blocks(self.mine(chip), terms + [self.z_buf.at[slot]], self.rows)

                    @pl.when(jnp.logical_not(more))
                    def _():
                        add_blocks(self.mine(chip), terms, self.rows)

                    remote(
                        self.mine(chip),
                        self.z_buf.at[there],
                        self.send.at[self.p, 3],
                        self.z_recv.at[self.p, there],
                        self.me + sign * PLANE,
                    ).start()

    def home_terms(self, i, dev, fn):
        terms = self.after_b(dev)
        if self.z_first:
            terms = terms + self.after_a(dev)
        above = self.z_slot(i, self.z)
        below = self.z_slot(i, LINE)
        for has_above, has_below, cond in (
            (True, False, self.z == 0),
            (True, True, (self.z > 0) & (self.z < LINE - 1)),
            (False, True, self.z == LINE - 1),
        ):

            @pl.when(cond)
            def _():
                more = list(terms)
                for slot, has in ((above, has_above), (below, has_below)):
                    if has:
                        wait_for(self.z_buf.at[slot], self.z_recv.at[self.p, slot])
                        more.append(self.z_buf.at[slot])
                fn(more)

    def home_a(self):
        dev = self.me + self.a_step
        self.home_terms(1, dev, lambda terms: add_blocks(self.mine(dev // 2), terms, self.rows))
        self.to_a(dev)

    def home(self):
        def finish(terms):
            if not self.z_first:
                terms = terms + self.after_a(self.me)
            for chunk in range(self.rows // 16):
                r = slice(16 * chunk, 16 * chunk + 16)
                total = terms[0][r, :].astype(jnp.float32)
                for term in terms[1:]:
                    total = total + term[r, :].astype(jnp.float32)
                self.emit(self.first_row // 16 + chunk, total)

        self.home_terms(0, self.me, finish)

    def stages(self):
        step = functools.partial
        z_steps = [step(self.along_z, k) for k in (3, 2, 1)]
        if self.z_first:
            return [step(self.send_a, k) for k in (3, 2, 1, 0)] + z_steps + [self.home]
        return z_steps + [None, None, None, self.home_a, self.home]

    def drain(self):
        wait_for(self.many(8), self.send.at[self.p, 1])
        wait_for(self.many(4 if self.z_first else 1), self.send.at[self.p, 0])
        wait_for(self.many(3 if self.z_first else 6), self.send.at[self.p, 3])


def attend_back_pair(i, width, qkv, d_attended, bias, d_proj, gvec):
    rows = d_attended.shape[0]
    q = qkv[:, columns(i * PAIR, PAIR)]
    k = qkv[:, columns(width + i * PAIR, PAIR)]
    v = qkv[:, columns(2 * width + i * PAIR, PAIR)]
    g = d_attended[:, columns(i * PAIR, PAIR)]
    d_query, d_key, d_value = [], 0.0, 0.0
    for head in (0, 1):
        qh, gh = own_half(q, head), own_half(g, head)
        p = probabilities(qh, k, bias[...])
        d_p = dot_nt(gh, v)
        inner = jnp.sum(p * d_p, -1, keepdims=True)
        d_s = (p * (d_p - inner)).astype(jnp.bfloat16)
        d_query.append(dot(d_s, k))
        d_key = d_key + dot_tn(d_s, qh)
        d_value = d_value + dot_tn(p.astype(jnp.bfloat16), gh)
    d_q = (halves(*d_query).astype(jnp.bfloat16).astype(jnp.float32) * HEAD_DIM ** (-0.5)).astype(jnp.bfloat16)
    d_v = d_value.astype(jnp.bfloat16)
    top = pl.ds(0, rows)
    d_proj[top, columns(i * PAIR, PAIR)] = d_q
    d_proj[top, columns(width + i * PAIR, PAIR)] = d_key.astype(jnp.bfloat16)
    d_proj[top, columns(2 * width + i * PAIR, PAIR)] = d_v
    gvec[QUERY_BIAS : QUERY_BIAS + 1, columns(i * PAIR, PAIR)] = column_sums(d_q)
    gvec[VALUE_BIAS : VALUE_BIAS + 1, columns(i * PAIR, PAIR)] = column_sums(d_v)


def transpose_blocks(stack, turned):
    def body(i):
        part = stack[:, columns(i * 128, 128)].astype(jnp.float32).T.astype(jnp.bfloat16)
        turned[pl.ds(2 * i, 2)] = part.reshape(2, 2, UNIT, stack.shape[0])

    loop(stack.shape[1] // 128, body)


def turned_product(turned, core, right, mine, unit, right_column):
    width = mine.shape[2]
    tokens = turned.shape[3]

    def body(j):
        left = turned[:, pl.ds(core, 1)].reshape(CHIPS * UNIT, tokens)
        out = dot(left, right[:, columns(right_column + j * TILE, TILE)]).astype(jnp.bfloat16)
        mine[:, UNIT * unit : UNIT * unit + UNIT, columns(j * TILE, TILE)] = out.reshape(CHIPS, UNIT, TILE)

    loop(width // TILE, body)


class Both:
    def __init__(self, copies):
        self.copies = copies

    def start(self):
        for copy in self.copies:
            copy.start()

    def wait(self):
        for copy in self.copies:
            copy.wait()


def stream(total, begin, count, copy_of, body):
    if begin == 0:
        copy_of(0, 0).start()

    def step(n):
        j = begin + n

        @pl.when(j + 1 < total)
        def _():
            copy_of(j + 1, (j + 1) % 2).start()

        copy_of(j, j % 2).wait()
        body(j, j % 2)

    loop(count, step)


OPERANDS = ("tokens", "cotangent", "qkv", "out", "fc1", "fc2")


def small_rows(segments, parts):
    slots = jnp.pad(segments.astype(jnp.float32), (0, -segments.shape[0] % 128), constant_values=IMG_DEV)
    flat = jnp.concatenate([p for part in parts for p in [part] * (128 // part.shape[0])] + [slots])
    return jnp.pad(flat, (0, 2048 - flat.shape[0])).reshape(16, 128)


def spread(dst, small, sizes, count, width):
    me = lax.axis_index(AXIS)
    dst[...] = jnp.zeros_like(dst)
    at = 0
    for i, size in enumerate(sizes):
        row = small[i : i + 1, :].astype(jnp.bfloat16).astype(jnp.float32)
        lane = lax.broadcasted_iota(jnp.int32, (1, width), 1)
        for r in range(size * count // width):
            wide = jnp.concatenate([row] * (width // 128), 1)
            inside = (lane + r * width) // size == me
            dst[at : at + 1, :] = jnp.where(inside, wide, 0.0)
            at += 1


def settle(arrays):
    n = len(arrays)

    def kernel(*refs):
        sems = refs[3 * n]
        loads = [pltpu.make_async_copy(refs[i], refs[2 * n + i], sems.at[i]) for i in range(n)]
        stores = [pltpu.make_async_copy(refs[2 * n + i], refs[n + i], sems.at[n + i]) for i in range(n)]
        for copy in loads:
            copy.start()
        for load, store in zip(loads, stores):
            load.wait()
            store.start()
        for copy in stores:
            copy.wait()

    anyspec = pl.BlockSpec(memory_space=pl.ANY)
    return pl.pallas_call(
        kernel,
        out_shape=[jax.ShapeDtypeStruct(a.shape, a.dtype) for a in arrays],
        in_specs=[pl.BlockSpec(memory_space=pltpu.HBM)] * n,
        out_specs=[anyspec] * n,
        scratch_shapes=[pltpu.VMEM(a.shape, a.dtype) for a in arrays] + [pltpu.SemaphoreType.DMA((2 * n,))],
        compiler_params=pltpu.CompilerParams(vmem_limit_bytes=63 << 20),
    )(*arrays)


def block_all(count, tokens, segments, cotangent, shards, vectors):
    rows, width = tokens.shape
    hidden = shards[2].shape[1]
    f32, b16 = jnp.float32, jnp.bfloat16
    vec = jax.ShapeDtypeStruct((VECTOR_ROWS, width), f32)
    sizes = [v.shape[0] for v in vectors]
    both, half = 2 * rows, hidden // 2
    block = (hidden // count, width)
    tiles, tiles_in, per = hidden // TILE, width // TILE, width // TILE
    kinds = {
        "slope": ((rows, hidden), f32),
        "sh_q": (shards[0].shape, b16),
        "sh_o": (shards[1].shape, b16),
        "sh_u": (shards[2].shape, b16),
        "sh_d": (shards[3].shape, b16),
        "resid": ((rows, width), f32),
        "d_resid": ((rows, width), f32),
        "acc": ((rows, width), f32),
        "x_active": ((both, half), b16),
        "other": ((rows, half), b16),
        "y_mlp": ((both, width), b16),
        "y_inner": ((both, hidden), b16),
        "x_second": ((both, width), b16),
        "x_attended": ((both, width), b16),
        "y_branch": ((both, width), b16),
        "x_first": ((both, width), b16),
        "turned": ((CHIPS, 2, UNIT, both), b16),
        "qkv": ((rows, 3 * width), b16),
        "wo": ((width, width), b16),
        "cols": ((2, width, TILE), b16),
        "bias": ((rows, rows), f32),
        "gvec": (vec.shape, f32),
        "vecs": (vec.shape, f32),
    }
    names = list(kinds)
    crossing = ("y_mlp", "x_first", "x_second", "x_attended", "y_branch", "y_proj", "a0", "a1", "i0", "i1")

    def kernel(small, *refs):
        src = dict(zip(OPERANDS, refs[:6]))
        act_out, grad_out, wq_h, wu_h, wd_h, q_out, o_out, u_out, d_out, gvec_out = refs[6:16]
        refs = refs[16:]
        s = dict(zip(names, refs[: len(names)]))
        refs = refs[len(names) :]
        bufs, refs = refs[:21], refs[21:]
        (held, got, g_send, g_recv, g_core, g_own, vsend, vrecv) = refs[:8]
        (send, b_recv, z_recv, a_recv, x_send, x_recv, load, tile_sem, leave_sem, free) = refs[8:]
        me, z, core, _, _, _, _ = place()
        sib = me + 1 - 2 * core
        _, near, up, down, far = peers()
        top, low = pl.ds(0, rows), pl.ds(rows, rows)
        resid, d_resid, acc, vecs, gvec = (s[k] for k in ("resid", "d_resid", "acc", "vecs", "gvec"))
        tok = s["slope"].at[:, pl.ds(hidden - width, width)]

        homes = [tok, d_resid]
        at = 0
        for sh in shards:
            homes.append(s["slope"].at[pl.ds(at, sh.shape[0]), pl.ds(0, sh.shape[1])])
            at += sh.shape[0]
        loads = [pltpu.make_async_copy(src[n], h, load.at[i]) for i, (n, h) in enumerate(zip(OPERANDS, homes))]
        for i in (2, 3, 4, 5, 1):
            loads[i].start()
        entry_barrier(z, near, up, down, far)
        spread(held, small, sizes, count, width)
        v = Vec(held, got, vsend, vrecv)
        v.start(0)

        def cast_shard(i):
            loads[2 + i].wait()
            s[("sh_q", "sh_o", "sh_u", "sh_d")[i]][...] = homes[2 + i][...].astype(b16)

        homes_w = (wq_h, s["wo"], wu_h, wd_h)
        parts = []
        for p, (w, begin_at, share, zf) in enumerate(GATHER_PARTS):
            sh = s[("sh_q", "sh_o", "sh_u", "sh_d")[w]]
            wide = sh.shape[1]
            parts.append(
                Gather(p, sh, homes_w[w], zf, int(begin_at * wide), int(share * wide), g_send, g_recv, g_core, g_own)
            )
        timed = []
        for gi, group in enumerate(GROUPS):
            for p in group:
                timed += [(LAG * gi + j, gi, step) for j, step in enumerate(parts[p].steps())]

        def gather_at(t):
            for gi in range(len(GROUPS)):
                for tt, g, step in timed:
                    if (tt, g) == (t, gi):
                        step()

        def gathered(*which):
            for p in which:
                parts[p].ready()

        def cross_copy(name):
            i = crossing.index(name)
            if name == "y_proj":
                c = pl.ds(0, 3 * width)
                own, to = s["y_inner"].at[top, c], s["y_inner"].at[low, c]
            elif name in ("a0", "a1"):
                c = pl.ds(int(name[1]) * (half // 2), half // 2)
                own, to = s["other"].at[:, c], s["x_active"].at[low, c]
            elif name in ("i0", "i1"):
                c = pl.ds(int(name[1]) * half, half)
                own, to = s["y_inner"].at[top, c], s["y_inner"].at[low, c]
            else:
                own, to = s[name].at[top], s[name].at[low]
            return remote(own, to, x_send.at[i], x_recv.at[i], sib)

        def cross(name):
            cross_copy(name).start()

        def crossed(*which):
            for name in which:
                cross_copy(name).wait()

        def col_copy(full):
            return lambda j, slot: pltpu.make_async_copy(
                full.at[:, columns(j * TILE, TILE)], s["cols"].at[slot], tile_sem.at[slot]
            )

        def row_copy(full):
            def copy_of(j, slot):
                r = pl.ds(pl.multiple_of(j * TILE, TILE), TILE)
                return Both(
                    [
                        pltpu.make_async_copy(
                            full.at[r, pl.ds(i * TILE, TILE)],
                            s["cols"].at[slot, pl.ds(i * TILE, TILE)],
                            tile_sem.at[2 * (i + 1) + slot],
                        )
                        for i in range(width // TILE)
                    ]
                )

            return copy_of

        def leave(i, source, dst):
            return pltpu.make_async_copy(source, dst, leave_sem.at[i])

        first = len(sizes)
        seg_row = jnp.concatenate([small[first + i : first + i + 1, :] for i in range(-(-rows // 128))], 1)
        seg_col = jnp.broadcast_to(seg_row, (128, seg_row.shape[1])).T[:rows, 0:1]
        seg_row = seg_row[:, :rows]
        valid_col = seg_col < IMG_DEV

        def begin():
            allowed = (seg_col == seg_row) & (seg_row < IMG_DEV)
            s["bias"][...] = jnp.where(allowed, 0.0, -1e30)
            loads[1].wait()
            d_resid[...] = jnp.where(valid_col, d_resid[...], 0.0)
            s["y_mlp"][top, :] = d_resid[...].astype(b16)
            gvec[DOWN_BIAS : DOWN_BIAS + 1, :] = column_sums(s["y_mlp"][top, :])

        def project(part):
            def body(t, slot):
                j = t - tiles_in * part
                out = dot(s["x_first"][top, :], s["cols"][slot])
                if part == 0:
                    out = (out + vecs[QUERY_BIAS : QUERY_BIAS + 1, columns(j * TILE, TILE)]) * HEAD_DIM ** (-0.5)
                elif part == 2:
                    out = out + vecs[VALUE_BIAS : VALUE_BIAS + 1, columns(j * TILE, TILE)]
                s["qkv"][:, columns(t * TILE, TILE)] = out.astype(b16)

            stream(3 * tiles_in, tiles_in * part, tiles_in, col_copy(wq_h), body)

        def attend(first, n):
            loop(n, lambda i: attend_pair(first + i, width, s["qkv"], s["bias"], s["x_attended"].at[top]))

        def project_out():
            def body(j):
                c = columns(j * TILE, TILE)
                resid[:, c] = tok[:, c] + dot(s["x_attended"][top, :], s["wo"][:, c]) + vecs[OUT_BIAS : OUT_BIAS + 1, c]

            loop(tiles_in, body)

        def up_tiles(first, n):
            def body(j, slot):
                t = dot(s["x_second"][top, :], s["cols"][slot])
                t = t + vecs[pl.ds(UP_BIAS + j // per, 1), columns((j % per) * TILE, TILE)]
                cdf = 0.5 + 0.5 * lax.erf(t * (0.5**0.5))
                s["slope"][:, columns(j * TILE, TILE)] = cdf + t * (0.3989422804014327 * jnp.exp(-0.5 * t * t))
                act = (t * cdf).astype(b16)
                for i in range(TILE // 256):
                    even, odd = act[:, 256 * i : 256 * i + 128], act[:, 256 * i + 128 : 256 * i + 256]
                    c = columns((2 * j + i) * 128, 128)
                    s["x_active"][top, c] = jnp.where(core == 0, even, odd)
                    s["other"][:, c] = jnp.where(core == 0, odd, even)

            stream(tiles, first, n, col_copy(wu_h), body)

        def d_inner_tiles(first, n):
            def body(j, slot):
                size = TILE // 2
                for i in (0, 1):
                    c = columns(j * TILE + i * size, size)
                    d_act = 0.0
                    for part in range(width // TILE):
                        wrows = slice(part * TILE + i * size, part * TILE + i * size + size)
                        d_act = d_act + dot_nt(s["y_mlp"][top, part * TILE : part * TILE + TILE], s["cols"][slot, wrows, :])
                    dd = (d_act * s["slope"][:, c]).astype(b16)
                    s["y_inner"][top, c] = dd
                    gvec[pl.ds(UP_BIAS + j // per, 1), columns((j % per) * TILE + i * size, size)] = column_sums(dd)

            stream(tiles, first, n, row_copy(wd_h), body)

        def d_second_tiles(first, n):
            def body(j, slot):
                acc[...] += dot_nt(s["y_inner"][top, columns(j * TILE, TILE)], s["cols"][slot])

            stream(tiles, first, n, col_copy(wu_h), body)

        def d_first_tiles(first, n):
            def body(j, slot):
                acc[...] += dot_nt(s["y_inner"][top, columns(j * TILE, TILE)], s["cols"][slot])

            stream(3 * tiles_in, first, n, col_copy(wq_h), body)

        def down_tiles(first, n):
            def body(j, slot):
                c = columns(2 * j * 128, 256)
                for which, left in ((core, s["x_active"][top, c]), (1 - core, s["other"][:, c])):
                    for part in range(width // TILE):
                        right = [
                            s["cols"][slot, pl.ds(pl.multiple_of(part * TILE + (2 * i + which) * 128, 128), 128), :]
                            for i in (0, 1)
                        ]
                        acc[:, part * TILE : part * TILE + TILE] += dot(left, jnp.concatenate(right, 0))

            stream(tiles, first, n, row_copy(wd_h), body)

        def second_norm_back():
            def emit(r, back):
                total = d_resid[r, :] + back
                d_resid[r, :] = total
                s["y_branch"][r, :] = total.astype(b16)

            norm_back(acc, resid, vecs, GAIN_TWO, held, emit)
            gvec[GAIN_TWO : GAIN_TWO + 1, :] = jnp.sum(held[0:8, :], 0, keepdims=True)
            gvec[BIAS_TWO : BIAS_TWO + 1, :] = jnp.sum(held[8:16, :], 0, keepdims=True)

        def first_norm_back():
            def emit(r, back):
                d_resid[r, :] += back

            loads[0].wait()
            norm_back(acc, tok, vecs, GAIN_ONE, held, emit)
            gvec[GAIN_ONE : GAIN_ONE + 1, :] = jnp.sum(held[0:8, :], 0, keepdims=True)
            gvec[BIAS_ONE : BIAS_ONE + 1, :] = jnp.sum(held[8:16, :], 0, keepdims=True)

        stacked = pl.ds(96, block[0])
        results = [homes[2], homes[3]] + [s["slope"].at[stacked, pl.ds(i * width, width)] for i in (1, 0)]

        def leave_result(i):
            if i != 2:
                return leave(2 + i, results[i], (q_out, o_out, u_out, d_out)[i])
            return Both(
                [
                    leave(6 + unit, results[2].at[pl.ds(unit * UNIT, UNIT)], u_out.at[:, pl.ds(unit * width, width)])
                    for unit in range(UNITS)
                ]
            )

        def emit_down(chunk, total):
            results[3][pl.ds(16 * chunk, 16), :] = total

        def emit_up(chunk, total):
            results[2][pl.ds(16 * chunk, 16), :] = total

        def emit_attn(chunk, total):
            unit, r = chunk // 2, 16 * (chunk % 2)
            if unit == 3:
                results[1][pl.ds(r, 16), :] = total
            else:
                results[0][pl.ds(r, 16), width * unit : width * unit + width] = total

        mines = bufs[:3]
        reduces = []
        for piece, emit in enumerate((emit_down, emit_up, emit_attn)):
            pair = []
            for zf in (True, False):
                p = 2 * piece + (0 if zf else 1)
                mid = bufs[3 + 3 * p : 6 + 3 * p]
                row = 0 if zf else SPLIT_ROWS
                pair.append(Reduce(p, zf, row, mines[piece], *mid, send, b_recv, z_recv, a_recv, emit))
            reduces.append(pair)

        def stage(piece, j):
            for r in reduces[piece]:
                step = r.stages()[j]
                if step is not None:
                    step()

        def send_blocks(piece):
            for k in (3, 2, 1, 0):
                for r in reduces[piece]:
                    r.send_b(k)

        def drain(piece):
            for r in reduces[piece]:
                r.drain()

        def down_grad(n):
            i = n + (1 - z // 2) * (LINE - 1 - 2 * n)
            out = dot_tn(s["x_active"][:, columns(i * TILE, TILE)], s["y_mlp"][...]).astype(b16)
            mines[0][pl.ds(4 * i, 4)] = out.reshape(4, block[0], width)
            for r in reduces[0]:
                r.send_plane(i)

        def up_grad(first):
            for unit in (first, first + 1):
                turned_product(s["turned"], core, s["y_inner"], mines[1], unit, unit * width)

        def out_grad():
            transpose_blocks(s["x_attended"], s["turned"])
            turned_product(s["turned"], core, s["y_branch"], mines[2], 3, 0)
            transpose_blocks(s["x_first"], s["turned"])

        def qkv_grad():
            for unit in range(3):
                turned_product(s["turned"], core, s["y_inner"], mines[2], unit, unit * width)

        def finish_activations():
            resid[...] = jnp.where(valid_col, resid[...] + acc[...] + vecs[DOWN_BIAS : DOWN_BIAS + 1, :], 0.0)
            leave(0, resid, act_out).start()

        def clear():
            acc[...] = jnp.zeros_like(acc)

        def share_vectors():
            leave(1, d_resid, grad_out).start()
            held[...] = gvec[...]
            v.start(0)

        def d_attended_tile(j):
            size = TILE // 2
            wrows = pl.ds(pl.multiple_of(j * size, size), size)
            c = columns(j * size, size)
            s["y_mlp"][top, c] = dot_nt(s["y_branch"][top, :], s["wo"][wrows, :]).astype(b16)
            gvec[OUT_BIAS : OUT_BIAS + 1, c] = column_sums(s["y_branch"][top, c])

        def attend_back(first, n):
            loop(
                n,
                lambda i: attend_back_pair(
                    first + i, width, s["qkv"], s["y_mlp"].at[top], s["bias"], s["y_inner"], gvec
                ),
            )

        def known():
            vecs[...] = held[...]

        def norm_one():
            loads[0].wait()
            norm_into(s["x_first"].at[top], tok, vecs, GAIN_ONE, BIAS_ONE)

        def norm_two():
            norm_into(s["x_second"].at[top], resid, vecs, GAIN_TWO, BIAS_TWO)

        gvec[...] = jnp.zeros_like(gvec)
        for i in range(4):
            cast_shard(i)
        loads[0].start()
        gather_at(0)
        v.step(0)
        gather_at(1)
        v.step(1)
        gather_at(2)
        v.step(2)
        gather_at(3)
        v.step(3)
        gather_at(4)
        v.step(4)
        known()
        begin()
        cross("y_mlp")
        gather_at(5)
        gather_at(6)
        norm_one()
        cross("x_first")
        gather_at(7)
        gather_at(8)
        gather_at(9)
        gather_at(10)
        gather_at(11)
        gathered(0, 1)
        project(0)
        gather_at(12)
        project(1)
        project(2)
        gather_at(13)
        attend(0, 2)
        gather_at(14)
        attend(2, 2)
        attend(4, 2)
        gather_at(15)
        attend(6, 2)
        cross("x_attended")
        gathered(2)
        project_out()
        norm_two()
        cross("x_second")
        gather_at(16)
        gather_at(17)
        gathered(3, 4)
        up_tiles(0, 2)
        up_tiles(2, 2)
        cross("a0")
        gather_at(18)
        up_tiles(4, 2)
        gather_at(19)
        up_tiles(6, 2)
        cross("a1")
        gather_at(20)
        crossed("y_mlp", "a0", "a1")
        down_grad(0)
        down_grad(1)
        down_grad(2)
        down_grad(3)
        gather_at(21)
        gather_at(22)
        gather_at(23)
        crossed("x_second")
        transpose_blocks(s["x_second"], s["turned"])
        gathered(5, 6)
        d_inner_tiles(0, 2)
        d_inner_tiles(2, 2)
        cross("i0")
        stage(0, 0)
        d_inner_tiles(4, 2)
        d_inner_tiles(6, 2)
        cross("i1")
        loads[0].start()
        stage(0, 1)
        crossed("i0")
        up_grad(0)
        crossed("i1")
        up_grad(2)
        send_blocks(1)
        pl.semaphore_signal(free, inc=1, device_id=(sib,), device_id_type=MESH)
        stage(0, 2)
        clear()
        d_second_tiles(0, 4)
        d_second_tiles(4, 4)
        stage(0, 3)
        second_norm_back()
        cross("y_branch")
        loop(width // (TILE // 2), d_attended_tile)
        stage(0, 4)
        attend_back(0, 2)
        stage(0, 5)
        stage(1, 0)
        attend_back(2, 2)
        stage(1, 1)
        attend_back(4, 2)
        stage(0, 6)
        stage(1, 2)
        attend_back(6, 2)
        pl.semaphore_wait(free, 1)
        cross("y_proj")
        crossed("x_attended", "x_first", "y_branch")
        out_grad()
        stage(1, 3)
        crossed("y_proj")
        qkv_grad()
        send_blocks(2)
        stage(0, 7)
        leave_result(3).start()
        stage(1, 4)
        stage(1, 5)
        clear()
        d_first_tiles(0, 3)
        d_first_tiles(3, 3)
        stage(2, 0)
        first_norm_back()
        share_vectors()
        stage(1, 6)
        stage(2, 1)
        v.step(0)
        stage(2, 2)
        clear()
        down_tiles(0, 4)
        down_tiles(4, 4)
        finish_activations()
        stage(1, 7)
        leave_result(2).start()
        stage(2, 3)
        v.step(1)
        stage(2, 4)
        v.step(2)
        stage(2, 5)
        v.step(3)
        stage(2, 6)
        v.step(4)
        stage(2, 7)
        leave_result(0).start()
        leave_result(1).start()
        gvec_out[...] = held[...]
        for g in parts:
            g.drain()
        for piece in range(3):
            drain(piece)
        leave(0, resid, act_out).wait()
        leave(1, d_resid, grad_out).wait()
        for i in range(4):
            leave_result(i).wait()

    anyspec = pl.BlockSpec(memory_space=pl.ANY)
    vm = pl.BlockSpec(memory_space=pltpu.VMEM)
    dma = pltpu.SemaphoreType.DMA
    shape = jax.ShapeDtypeStruct
    n = len(GATHER_PARTS)
    bufs = [pltpu.VMEM((CHIPS,) + block, b16)] * 3
    for _ in range(3):
        for zf, height in ((True, SPLIT_ROWS), (False, block[0] - SPLIT_ROWS)):
            bufs += [pltpu.VMEM((m, height, width), b16) for m in (8, 5 if zf else 10, 4 if zf else 1)]
    outs = [
        ((rows, width), f32),
        ((rows, width), f32),
        ((width, 3 * width), b16),
        ((width, hidden), b16),
        ((hidden, width), b16),
        (shards[0].shape, f32),
        (shards[1].shape, f32),
        (shards[2].shape, f32),
        (shards[3].shape, f32),
        (vec.shape, f32),
    ]
    results = pl.pallas_call(
        kernel,
        out_shape=[shape(*o) for o in outs],
        in_specs=[vm] + [anyspec] * len(OPERANDS),
        out_specs=[anyspec] * 9 + [vm],
        scratch_shapes=[pltpu.VMEM(*kinds[k]) for k in names]
        + bufs
        + [
            pltpu.VMEM(vec.shape, f32),
            pltpu.VMEM((5,) + vec.shape, f32),
            dma((n, 4)),
            dma((n, 16)),
            dma((n,)),
            dma((n,)),
            dma((5,)),
            dma((5,)),
            dma((6, 4)),
            dma((6, 8)),
            dma((6, 10)),
            dma((6, 4)),
            dma((len(crossing),)),
            dma((len(crossing),)),
            dma((len(OPERANDS),)),
            dma((2 * (1 + width // TILE),)),
            dma((6 + UNITS,)),
            pltpu.SemaphoreType.REGULAR,
        ],
        compiler_params=pltpu.CompilerParams(collective_id=0, has_side_effects=True, vmem_limit_bytes=63 << 20),
    )(small_rows(segments, vectors), tokens, cotangent, *shards)
    settled = settle([results[0], results[1], *results[5:9]])
    return settled[0], settled[1], settled[2:], results[9]


def local_math(tokens, segments, cotangent, vectors, weights):
    gain_one, bias_one, mix_bias, proj_bias, gain_two, bias_two, up_bias, down_bias = vectors
    mix_weight, proj_weight, up_weight, down_weight = weights
    model_width = tokens.shape[1]
    valid_slot = segments < IMG_DEV
    allowed = (segments[:, None] == segments[None, :]) & valid_slot[None, :]
    gain_one_f = gain_one.astype(jnp.float32)
    bias_one_f = bias_one.astype(jnp.float32)
    first = halved(layer_norm(tokens, gain_one_f, bias_one_f))
    mix_bias_f = mix_bias.astype(jnp.float32)
    bias_row = jnp.concatenate(
        [mix_bias_f[:model_width], jnp.zeros((model_width,), jnp.float32), mix_bias_f[model_width:]]
    )
    projected = jnp.dot(first, mix_weight, preferred_element_type=jnp.float32) + bias_row
    queries = halved(projected[:, :model_width] * HEAD_DIM ** (-0.5))
    key_rows = halved(projected[:, model_width : 2 * model_width])
    values = halved(projected[:, 2 * model_width :])
    attended_stack, lse_stack = lax.map(
        lambda pieces: pair_forward(pieces, allowed),
        (head_pairs(queries), head_pairs(key_rows), head_pairs(values)),
    )
    attended = halved(join_pairs(attended_stack))
    residual = (
        tokens
        + jnp.dot(attended, proj_weight, preferred_element_type=jnp.float32)
        + proj_bias.astype(jnp.float32)
    )
    gain_two_f = gain_two.astype(jnp.float32)
    bias_two_f = bias_two.astype(jnp.float32)
    second = halved(layer_norm(residual, gain_two_f, bias_two_f))
    inner = jnp.dot(second, up_weight, preferred_element_type=jnp.float32) + up_bias.astype(
        jnp.float32
    )
    active = halved(jax.nn.gelu(inner, approximate=False))
    branch = jnp.dot(active, down_weight, preferred_element_type=jnp.float32) + down_bias.astype(
        jnp.float32
    )
    activations = jnp.where(valid_slot[:, None], residual + branch, 0.0)
    d_out = jnp.where(valid_slot[:, None], cotangent, 0.0)
    d_mlp = halved(d_out)
    grad_fc2_bias = jnp.sum(d_mlp, 0, dtype=jnp.float32)
    grad_fc2_weight = contract_rows(active, d_mlp)
    d_active = contract_cols(d_mlp, down_weight)
    gelu_back = jax.vjp(partial(jax.nn.gelu, approximate=False), inner)[1]
    d_inner = halved(gelu_back(d_active)[0])
    grad_fc1_bias = jnp.sum(d_inner, 0, dtype=jnp.float32)
    grad_fc1_weight = contract_rows(second, d_inner)
    d_second = contract_cols(d_inner, up_weight)
    norm_two_back = jax.vjp(layer_norm, residual, gain_two_f, bias_two_f)[1]
    d_norm2, grad_norm2_gain, grad_norm2_bias = norm_two_back(d_second)
    d_resid = d_out + d_norm2
    d_branch = halved(d_resid)
    grad_out_bias = jnp.sum(d_branch, 0, dtype=jnp.float32)
    grad_out_weight = contract_rows(attended, d_branch)
    d_attended = halved(contract_cols(d_branch, proj_weight))
    d_query_stack, d_key_stack, d_value_stack = lax.map(
        lambda pieces: pair_backward(pieces, allowed),
        (
            head_pairs(queries),
            head_pairs(key_rows),
            head_pairs(values),
            head_pairs(d_attended),
            lse_stack,
        ),
    )
    d_query = join_pairs(d_query_stack)
    d_value = join_pairs(d_value_stack)
    d_projected = jnp.concatenate([d_query, join_pairs(d_key_stack), d_value], 1)
    grad_qv_bias = jnp.concatenate(
        [jnp.sum(d_query, 0, dtype=jnp.float32), jnp.sum(d_value, 0, dtype=jnp.float32)]
    )
    grad_qkv_weight = contract_rows(first, d_projected)
    d_first = contract_cols(d_projected, mix_weight)
    norm_one_back = jax.vjp(layer_norm, tokens, gain_one_f, bias_one_f)[1]
    d_norm1, grad_norm1_gain, grad_norm1_bias = norm_one_back(d_first)
    input_grad = d_resid + d_norm1
    return (
        activations,
        input_grad,
        (grad_qkv_weight, grad_out_weight, grad_fc1_weight, grad_fc2_weight),
        (
            grad_norm1_gain,
            grad_norm1_bias,
            grad_qv_bias,
            grad_out_bias,
            grad_norm2_gain,
            grad_norm2_bias,
            grad_fc1_bias,
            grad_fc2_bias,
        ),
    )


def shards(count, tokens,
    segments,
    norm1_gain,
    norm1_bias,
    qkv_weight,
    qv_bias,
    out_weight,
    out_bias,
    norm2_gain,
    norm2_bias,
    fc1_weight,
    fc1_bias,
    fc2_weight,
    fc2_bias,
    cotangent,
):
    vector_shards = (norm1_gain, norm1_bias, qv_bias, out_bias, norm2_gain, norm2_bias, fc1_bias, fc2_bias)
    sizes = [v.shape[0] * count for v in vector_shards]
    starts = [sum(sizes[:i]) for i in range(len(sizes) + 1)]
    width = tokens.shape[1]
    position = lax.axis_index(AXIS)
    kernels = count == 32

    if kernels:
        activations, input_grad, weight_owned, vector_rows = block_all(
            count,
            tokens,
            segments,
            cotangent,
            (qkv_weight, out_weight, fc1_weight, fc2_weight),
            vector_shards,
        )
    else:
        weight_shards = [halved(w) for w in (qkv_weight, out_weight, fc1_weight, fc2_weight)]
        weights = [lax.all_gather(w, AXIS, axis=0, tiled=True) for w in weight_shards]
        vectors = [
            lax.all_gather(halved(v), AXIS, axis=0, tiled=True).astype(jnp.float32)
            for v in vector_shards
        ]
        activations, input_grad, weight_grads, vector_grads = local_math(
            tokens, segments, cotangent, vectors, weights
        )
    if kernels:
        flat = vector_rows.reshape(-1)
        vector_owned = [
            lax.dynamic_slice(flat, (starts[i] + position * (sizes[i] // count),), (sizes[i] // count,))
            for i in range(len(sizes))
        ]
    else:
        weight_owned = [
            lax.psum_scatter(g, AXIS, scatter_dimension=0, tiled=True) for g in weight_grads
        ]
        vector_owned = [
            lax.psum_scatter(g, AXIS, scatter_dimension=0, tiled=True) for g in vector_grads
        ]
    g1, b1, qvb, ob, g2, b2, f1b, f2b = vector_owned
    qkv_g, out_g, fc1_g, fc2_g = weight_owned
    return (activations, input_grad, g1, b1, qkv_g, qvb, out_g, ob, g2, b2, fc1_g, f1b, fc2_g, f2b)


def solution(mesh):
    in_specs = (
        P(AXIS, None),
        P(AXIS),
        P(AXIS),
        P(AXIS),
        P(AXIS, None),
        P(AXIS),
        P(AXIS, None),
        P(AXIS),
        P(AXIS),
        P(AXIS),
        P(AXIS, None),
        P(AXIS),
        P(AXIS, None),
        P(AXIS),
        P(AXIS, None),
    )
    out_specs = (
        P(AXIS, None),
        P(AXIS, None),
        P(AXIS),
        P(AXIS),
        P(AXIS, None),
        P(AXIS),
        P(AXIS, None),
        P(AXIS),
        P(AXIS),
        P(AXIS),
        P(AXIS, None),
        P(AXIS),
        P(AXIS, None),
        P(AXIS),
    )
    return jax.shard_map(
        partial(shards, mesh.size), mesh=mesh, in_specs=in_specs, out_specs=out_specs, check_vma=False)
```

```python
import functools
from functools import partial

import jax
import jax.numpy as jnp
from jax import lax
from jax.experimental import pallas as pl
from jax.experimental.pallas import tpu as pltpu
from jax.sharding import PartitionSpec as P

HEAD_DIM = 64
IMG_DEV = 1
AXIS = "dev"
MESH = pl.DeviceIdType.MESH


def layer_norm(rows_in, gain, bias):
    centre = rows_in - jnp.mean(rows_in, -1, keepdims=True)
    spread = jnp.mean(centre * centre, -1, keepdims=True)
    return centre * lax.rsqrt(spread + 1e-06) * gain + bias


def halved(array_in):
    return array_in.astype(jnp.bfloat16)


def contract_rows(left, right):
    return lax.dot_general(
        left, right, (((0,), (0,)), ((), ())), preferred_element_type=jnp.float32
    )


def contract_cols(left, right):
    return lax.dot_general(
        left, right, (((1,), (1,)), ((), ())), preferred_element_type=jnp.float32
    )


def head_pairs(block):
    return block.reshape(block.shape[0], -1, 2 * HEAD_DIM).transpose(1, 0, 2)


def join_pairs(stack):
    return stack.transpose(1, 0, 2).reshape(stack.shape[1], stack.shape[0] * stack.shape[2])


def masked_scores(query_heads, key_heads, allowed):
    scores = jnp.einsum("qhd,khd->hqk", query_heads, key_heads, preferred_element_type=jnp.float32)
    return jnp.where(allowed[None], scores, -1e30)


def pair_forward(pieces, allowed):
    q_pair, k_pair, v_pair = pieces
    row_count = q_pair.shape[0]
    query_heads = q_pair.reshape(row_count, 2, HEAD_DIM)
    key_heads = k_pair.reshape(row_count, 2, HEAD_DIM)
    value_heads = v_pair.reshape(row_count, 2, HEAD_DIM)
    scores = masked_scores(query_heads, key_heads, allowed)
    row_top = jnp.max(scores, -1, keepdims=True)
    powered = jnp.exp(scores - row_top)
    totals = jnp.sum(powered, -1, keepdims=True)
    probability = halved(powered / totals)
    attended = jnp.einsum(
        "hqk,khd->qhd", probability, value_heads, preferred_element_type=jnp.float32
    )
    return (attended.reshape(row_count, 2 * HEAD_DIM), row_top + jnp.log(totals))


def pair_backward(pieces, allowed):
    q_pair, k_pair, v_pair, g_pair, lse_pair = pieces
    row_count = q_pair.shape[0]
    query_heads = q_pair.reshape(row_count, 2, HEAD_DIM)
    key_heads = k_pair.reshape(row_count, 2, HEAD_DIM)
    value_heads = v_pair.reshape(row_count, 2, HEAD_DIM)
    grad_heads = g_pair.reshape(row_count, 2, HEAD_DIM)
    probability = jnp.exp(masked_scores(query_heads, key_heads, allowed) - lse_pair)
    d_prob = jnp.einsum("qhd,khd->hqk", grad_heads, value_heads, preferred_element_type=jnp.float32)
    row_inner = jnp.sum(probability * d_prob, -1, keepdims=True)
    d_scores = halved(probability * (d_prob - row_inner))
    d_query = halved(
        jnp.einsum("hqk,khd->qhd", d_scores, key_heads, preferred_element_type=jnp.float32)
    )
    d_query = d_query * jnp.bfloat16(HEAD_DIM ** (-0.5))
    d_key = halved(
        jnp.einsum("hqk,qhd->khd", d_scores, query_heads, preferred_element_type=jnp.float32)
    )
    d_value = halved(
        jnp.einsum(
            "hqk,qhd->khd", halved(probability), grad_heads, preferred_element_type=jnp.float32
        )
    )
    width_pair = 2 * HEAD_DIM
    return (
        d_query.reshape(row_count, width_pair),
        d_key.reshape(row_count, width_pair),
        d_value.reshape(row_count, width_pair),
    )


LINE, PLANE = 4, 8

def place():
    me = lax.axis_index(AXIS)
    core = me % 2
    x = (me // 2) % 2
    y = (me // 4) % 2
    z = me // PLANE
    a_bit = x * (1 - core) + y * core
    b_bit = y * (1 - core) + x * core
    a_step = (2 + 2 * core) * (1 - 2 * a_bit)
    b_step = (4 - 2 * core) * (1 - 2 * b_bit)
    return me, z, core, a_step, b_step, x, y


def remote(src, dst, send_sem, recv_sem, device):
    return pltpu.make_async_remote_copy(
        src_ref=src, dst_ref=dst, send_sem=send_sem, recv_sem=recv_sem, device_id=(device,), device_id_type=MESH
    )


def wait_for(ref, sem):
    pltpu.make_async_copy(ref, ref, sem).wait()


def entry_barrier(z, devices, up, down, far):
    bar = pltpu.get_barrier_semaphore()
    for dev in devices:
        pl.semaphore_signal(bar, inc=1, device_id=(dev,), device_id_type=MESH)

    @pl.when(z < LINE - 1)
    def _():
        pl.semaphore_signal(bar, inc=1, device_id=(up,), device_id_type=MESH)

    @pl.when(z > 0)
    def _():
        pl.semaphore_signal(bar, inc=1, device_id=(down,), device_id_type=MESH)

    pl.semaphore_signal(bar, inc=1, device_id=(far,), device_id_type=MESH)
    count = len(devices) + 1
    inner = (z > 0) & (z < LINE - 1)

    @pl.when(inner)
    def _():
        pl.semaphore_wait(bar, count + 2)

    @pl.when(jnp.logical_not(inner))
    def _():
        pl.semaphore_wait(bar, count + 1)


class Vec:
    def __init__(self, held, got, send, recv):
        me, z, core, _, _, x, y = place()
        self.to = [
            me + 1 - 2 * core,
            me + 2 - 4 * x,
            me + 4 - 8 * y,
            me + 8 - 16 * (z % 2),
            me + 16 - 32 * (z // 2),
        ]
        self.held, self.got, self.send, self.recv = held, got, send, recv

    def copy(self, i):
        return remote(self.held, self.got.at[i], self.send.at[i], self.recv.at[i], self.to[i])

    def start(self, i):
        self.copy(i).start()

    def step(self, i):
        self.copy(i).wait()
        self.held[...] += self.got[i]
        if i < 4:
            self.start(i + 1)


class Gather:
    def __init__(self, part, shard, full, z_first, start, size, send, recv, core_recv, own):
        self.p, self.z_first = part, z_first
        cols = pl.ds(start, size)
        self.shard, self.full, self.cols = shard.at[:, cols], full, cols
        self.send, self.recv, self.core_recv, self.own_sem = send, recv, core_recv, own
        self.rows = shard.shape[0]
        self.me, self.z, self.core, self.a_step, self.b_step, _, _ = place()
        self.sib = self.me + 1 - 2 * self.core

    def block(self, dev):
        return self.full.at[pl.ds(pl.multiple_of(dev * self.rows, self.rows), self.rows), self.cols]

    def ici(self, src, dev, way, to):
        remote(src, self.block(dev), self.send.at[self.p, way], self.recv.at[self.p, dev // 2], to).start()

    def to_a(self, src, dev):
        self.ici(src, dev, 0, self.me + self.a_step)

    def to_b(self, src, dev):
        self.ici(src, dev, 1, self.me + self.b_step)

    def to_core(self, src, dev):
        remote(src, self.block(dev), self.send.at[self.p, 2], self.core_recv.at[self.p], self.sib).start()

    def up(self, src, dev):
        @pl.when(self.z < LINE - 1)
        def _():
            self.ici(src, dev, 3, self.me + PLANE)

    def down(self, src, dev):
        @pl.when(self.z > 0)
        def _():
            self.ici(src, dev, 3, self.me - PLANE)

    def arrive(self, dev):
        wait_for(self.block(dev), self.recv.at[self.p, dev // 2])

    def own(self):
        pltpu.make_async_copy(self.shard, self.block(self.me), self.own_sem.at[self.p]).start()
        src = self.shard
        if self.z_first:
            self.up(src, self.me)
            self.down(src, self.me)
            self.to_a(src, self.me)
        else:
            self.to_a(src, self.me)
            self.up(src, self.me)
            self.down(src, self.me)
        self.to_b(src, self.me)
        self.to_core(src, self.me)

    def from_a(self, k=None):
        if not self.z_first:
            dev = self.me + self.a_step
            self.arrive(dev)
            src = self.block(dev)
            self.up(src, dev)
            self.down(src, dev)
            self.to_b(src, dev)
            self.to_core(src, dev)
            return

        def one(dev):
            self.arrive(dev)
            src = self.block(dev)
            self.to_b(src, dev)
            self.to_core(src, dev)

        self.sides(k, lambda off: one(self.me + self.a_step + off))

    def sides(self, k, fn):
        if k == 0:
            fn(0)
            return

        @pl.when(self.z >= k)
        def _():
            fn(-PLANE * k)

        @pl.when(self.z + k <= LINE - 1)
        def _():
            fn(PLANE * k)

    def from_z(self, k):
        for base in [self.me] if self.z_first else [self.me, self.me + self.a_step]:

            @pl.when(self.z >= k)
            def _():
                dev = base - PLANE * k
                self.arrive(dev)
                src = self.block(dev)
                self.up(src, dev)
                if self.z_first:
                    self.to_a(src, dev)
                self.to_b(src, dev)
                self.to_core(src, dev)

            @pl.when(self.z + k <= LINE - 1)
            def _():
                dev = base + PLANE * k
                self.arrive(dev)
                src = self.block(dev)
                self.down(src, dev)
                if self.z_first:
                    self.to_a(src, dev)
                self.to_b(src, dev)
                self.to_core(src, dev)

    def from_b(self, k):
        for base in [self.me + self.b_step, self.me + self.b_step + self.a_step]:

            def one(off):
                dev = base + off
                self.arrive(dev)
                self.to_core(self.block(dev), dev)

            self.sides(k, one)

    def many(self, count):
        return self.full.at[pl.ds(0, count * self.rows), self.cols]

    def steps(self):
        step = functools.partial
        z_steps = [step(self.from_z, k) for k in (1, 2, 3)]
        a_steps = [step(self.from_a, k) for k in range(LINE)] if self.z_first else [self.from_a]
        b_steps = [step(self.from_b, k) for k in range(LINE)]
        middle = z_steps + a_steps if self.z_first else a_steps + z_steps
        return [self.own] + middle + b_steps

    def ready(self):
        wait_for(self.shard, self.own_sem.at[self.p])
        wait_for(self.many(16), self.core_recv.at[self.p])

    def drain(self):
        a_count = 4 if self.z_first else 1
        z_unit = 1 if self.z_first else 2
        wait_for(self.many(a_count), self.send.at[self.p, 0])
        wait_for(self.many(8), self.send.at[self.p, 1])
        wait_for(self.many(16), self.send.at[self.p, 2])
        inner = (self.z > 0) & (self.z < LINE - 1)

        @pl.when(inner)
        def _():
            wait_for(self.many(5 * z_unit), self.send.at[self.p, 3])

        @pl.when(jnp.logical_not(inner))
        def _():
            wait_for(self.many(z_unit), self.send.at[self.p, 3])


def add_blocks(dst, terms, rows):
    def body(i, carry):
        r = pl.multiple_of(i * 16, 16)
        total = terms[0][pl.ds(r, 16), :].astype(jnp.float32)
        for term in terms[1:]:
            total = total + term[pl.ds(r, 16), :].astype(jnp.float32)
        dst[pl.ds(r, 16), :] = total.astype(dst.dtype)
        return carry

    lax.fori_loop(0, rows // 16, body, 0)


def peers():
    me, z, core, a_step, b_step, x, y = place()
    near = [me + 1 - 2 * core, me + a_step, me + b_step]
    return z, near, me + PLANE, me - PLANE, me + 16 - 32 * (z // 2)


GATHER_PARTS = (
    (0, 0, 0.5, True),
    (0, 0.5, 0.5, False),
    (1, 0, 1, False),
    (2, 0, 0.375, True),
    (2, 0.375, 0.625, False),
    (3, 0, 0.375, True),
    (3, 0.375, 0.625, False),
)
GROUPS = ((0, 1, 2), (3, 4), (5, 6))
LAG = 5
SPLIT_ROWS = 48


EPS = 1e-06
PAIR = 128
TILE = 512
ROWS = 32
GAIN_ONE, BIAS_ONE, QUERY_BIAS, VALUE_BIAS, OUT_BIAS, GAIN_TWO, BIAS_TWO, UP_BIAS, DOWN_BIAS = 0, 1, 2, 3, 4, 5, 6, 7, 11


def dot(left, right):
    return jnp.dot(left, right, preferred_element_type=jnp.float32)


def dot_nt(left, right):
    return lax.dot_general(left, right, (((1,), (1,)), ((), ())), preferred_element_type=jnp.float32)


def dot_tn(left, right):
    return lax.dot_general(left, right, (((0,), (0,)), ((), ())), preferred_element_type=jnp.float32)


def column_sums(block):
    return dot(jnp.ones((16, block.shape[0]), block.dtype), block)[0:1, :]


def columns(start, size):
    return pl.ds(pl.multiple_of(start, 128), size)


def loop(count, body):
    def step(i, carry):
        body(i)
        return carry

    lax.fori_loop(0, count, step, 0)


def centred(rows):
    centre = rows - jnp.mean(rows, -1, keepdims=True)
    spread = jnp.mean(centre * centre, -1, keepdims=True)
    return centre, lax.rsqrt(spread + EPS)


def norm_into(dst, src, vec, gain_row, bias_row):
    gain = vec[gain_row : gain_row + 1, :]
    bias = vec[bias_row : bias_row + 1, :]

    def body(i):
        r = pl.ds(pl.multiple_of(i * ROWS, ROWS), ROWS)
        centre, scale = centred(src[r, :])
        dst[r, :] = (centre * scale * gain + bias).astype(dst.dtype)

    loop(src.shape[0] // ROWS, body)


def norm_back(d_rows, src, vec, gain_row, sums, emit):
    gain = vec[gain_row : gain_row + 1, :]
    sums[...] = jnp.zeros_like(sums)

    def body(i):
        r = pl.ds(pl.multiple_of(i * ROWS, ROWS), ROWS)
        centre, scale = centred(src[r, :])
        n = centre * scale
        d = d_rows[r, :]
        e = d * gain
        dn = d * n
        for part in range(ROWS // 8):
            sums[0:8, :] += dn[8 * part : 8 * part + 8, :]
            sums[8:16, :] += d[8 * part : 8 * part + 8, :]
        back = scale * (e - jnp.mean(e, -1, keepdims=True) - n * jnp.mean(e * n, -1, keepdims=True))
        emit(r, back)

    loop(src.shape[0] // ROWS, body)


def own_half(rows, head):
    lane = lax.broadcasted_iota(jnp.int32, rows.shape, 1)
    inside = (lane < HEAD_DIM) if head == 0 else (lane >= HEAD_DIM)
    return jnp.where(inside, rows, jnp.zeros_like(rows))


def halves(first, second):
    lane = lax.broadcasted_iota(jnp.int32, first.shape, 1)
    return jnp.where(lane < HEAD_DIM, first, second)


def probabilities(query, key, bias):
    scores = dot_nt(query, key) + bias
    powered = jnp.exp(scores - jnp.max(scores, -1, keepdims=True))
    return powered * (1.0 / jnp.sum(powered, -1, keepdims=True))


def attend_pair(i, width, qkv, bias, attended):
    q = qkv[:, columns(i * PAIR, PAIR)]
    k = qkv[:, columns(width + i * PAIR, PAIR)]
    v = qkv[:, columns(2 * width + i * PAIR, PAIR)]
    parts = []
    for head in (0, 1):
        p = probabilities(own_half(q, head), k, bias[...]).astype(jnp.bfloat16)
        parts.append(dot(p, v))
    attended[:, columns(i * PAIR, PAIR)] = halves(*parts).astype(jnp.bfloat16)


UNITS = 4
VECTOR_ROWS = 16
UNIT = 32
CHIPS = 16


class Reduce:
    def __init__(self, part, z_first, first_row, mine, b_buf, z_buf, a_buf, send, b_recv, z_recv, a_recv, emit):
        self.p, self.z_first, self.first_row, self.emit = part, z_first, first_row, emit
        self.whole, self.b_buf, self.z_buf, self.a_buf = mine, b_buf, z_buf, a_buf
        self.send, self.b_recv, self.z_recv, self.a_recv = send, b_recv, z_recv, a_recv
        self.rows = b_buf.shape[1]
        self.me, self.z, self.core, self.a_step, self.b_step, self.x, self.y = place()

    def mine(self, chip):
        return self.whole.at[chip, pl.ds(self.first_row, self.rows)]

    def many(self, count):
        return self.whole.at[pl.ds(0, count), pl.ds(0, self.rows)]

    def sides(self, k, fn):
        if k == 0:
            fn(0)
            return

        @pl.when(self.z >= k)
        def _():
            fn(-k)

        @pl.when(self.z + k <= LINE - 1)
        def _():
            fn(k)

    def b_slot(self, dev):
        x = (dev // 2) % 2
        y = (dev // 4) % 2
        a_bit = x * (1 - self.core) + y * self.core
        return (dev // PLANE) * 2 + a_bit

    def send_plane(self, plane):
        for a in (self.a_step, 0):
            dev = self.me + self.b_step + a + PLANE * (plane - self.z)
            slot = self.b_slot(dev)
            remote(
                self.mine(dev // 2),
                self.b_buf.at[slot],
                self.send.at[self.p, 1],
                self.b_recv.at[self.p, slot],
                self.me + self.b_step,
            ).start()

    def send_b(self, k):
        self.sides(k, lambda sign: self.send_plane(self.z + sign))

    def after_b(self, dev):
        slot = self.b_slot(dev)
        wait_for(self.b_buf.at[slot], self.b_recv.at[self.p, slot])
        return [self.mine(dev // 2), self.b_buf.at[slot]]

    def a_slot(self, dev):
        return dev // PLANE if self.z_first else 0

    def to_a(self, dev):
        slot = self.a_slot(dev)
        remote(
            self.mine(dev // 2),
            self.a_buf.at[slot],
            self.send.at[self.p, 0],
            self.a_recv.at[self.p, slot],
            self.me + self.a_step,
        ).start()

    def send_a(self, k):
        def one(s):
            dev = self.me + self.a_step + PLANE * s
            add_blocks(self.mine(dev // 2), self.after_b(dev), self.rows)
            self.to_a(dev)

        self.sides(k, one)

    def after_a(self, dev):
        slot = self.a_slot(dev)
        wait_for(self.a_buf.at[slot], self.a_recv.at[self.p, slot])
        return [self.a_buf.at[slot]]

    def z_slot(self, i, dest):
        return i * (LINE + 1) + dest

    def along_z(self, k):
        for i, a in [(0, 0)] if self.z_first else [(1, self.a_step), (0, 0)]:
            for sign in (-1, 1):

                @pl.when((self.z >= k) if sign < 0 else (self.z + k <= LINE - 1))
                def _():
                    dev = self.me + a + sign * PLANE * k
                    chip = dev // 2
                    terms = self.after_b(dev)
                    if self.z_first:
                        terms = terms + self.after_a(dev)
                    slot = self.z_slot(i, self.z + sign * k)
                    there = self.z_slot(i, LINE) if (k == 1 and sign > 0) else slot
                    more = (self.z < LINE - 1) if sign < 0 else (self.z > 0)

                    @pl.when(more)
                    def _():
                        wait_for(self.z_buf.at[slot], self.z_recv.at[self.p, slot])
                        add_blocks(self.mine(chip), terms + [self.z_buf.at[slot]], self.rows)

                    @pl.when(jnp.logical_not(more))
                    def _():
                        add_blocks(self.mine(chip), terms, self.rows)

                    remote(
                        self.mine(chip),
                        self.z_buf.at[there],
                        self.send.at[self.p, 3],
                        self.z_recv.at[self.p, there],
                        self.me + sign * PLANE,
                    ).start()

    def home_terms(self, i, dev, fn):
        terms = self.after_b(dev)
        if self.z_first:
            terms = terms + self.after_a(dev)
        above = self.z_slot(i, self.z)
        below = self.z_slot(i, LINE)
        for has_above, has_below, cond in (
            (True, False, self.z == 0),
            (True, True, (self.z > 0) & (self.z < LINE - 1)),
            (False, True, self.z == LINE - 1),
        ):

            @pl.when(cond)
            def _():
                more = list(terms)
                for slot, has in ((above, has_above), (below, has_below)):
                    if has:
                        wait_for(self.z_buf.at[slot], self.z_recv.at[self.p, slot])
                        more.append(self.z_buf.at[slot])
                fn(more)

    def home_a(self):
        dev = self.me + self.a_step
        self.home_terms(1, dev, lambda terms: add_blocks(self.mine(dev // 2), terms, self.rows))
        self.to_a(dev)

    def home(self):
        def finish(terms):
            if not self.z_first:
                terms = terms + self.after_a(self.me)
            for chunk in range(self.rows // 16):
                r = slice(16 * chunk, 16 * chunk + 16)
                total = terms[0][r, :].astype(jnp.float32)
                for term in terms[1:]:
                    total = total + term[r, :].astype(jnp.float32)
                self.emit(self.first_row // 16 + chunk, total)

        self.home_terms(0, self.me, finish)

    def stages(self):
        step = functools.partial
        z_steps = [step(self.along_z, k) for k in (3, 2, 1)]
        if self.z_first:
            return [step(self.send_a, k) for k in (3, 2, 1, 0)] + z_steps + [self.home]
        return z_steps + [None, None, None, self.home_a, self.home]

    def drain(self):
        wait_for(self.many(8), self.send.at[self.p, 1])
        wait_for(self.many(4 if self.z_first else 1), self.send.at[self.p, 0])
        wait_for(self.many(3 if self.z_first else 6), self.send.at[self.p, 3])


def attend_back_pair(i, width, qkv, d_attended, bias, d_proj, gvec):
    rows = d_attended.shape[0]
    q = qkv[:, columns(i * PAIR, PAIR)]
    k = qkv[:, columns(width + i * PAIR, PAIR)]
    v = qkv[:, columns(2 * width + i * PAIR, PAIR)]
    g = d_attended[:, columns(i * PAIR, PAIR)]
    d_query, d_key, d_value = [], 0.0, 0.0
    for head in (0, 1):
        qh, gh = own_half(q, head), own_half(g, head)
        p = probabilities(qh, k, bias[...])
        d_p = dot_nt(gh, v)
        inner = jnp.sum(p * d_p, -1, keepdims=True)
        d_s = (p * (d_p - inner)).astype(jnp.bfloat16)
        d_query.append(dot(d_s, k))
        d_key = d_key + dot_tn(d_s, qh)
        d_value = d_value + dot_tn(p.astype(jnp.bfloat16), gh)
    d_q = (halves(*d_query).astype(jnp.bfloat16).astype(jnp.float32) * HEAD_DIM ** (-0.5)).astype(jnp.bfloat16)
    d_v = d_value.astype(jnp.bfloat16)
    top = pl.ds(0, rows)
    d_proj[top, columns(i * PAIR, PAIR)] = d_q
    d_proj[top, columns(width + i * PAIR, PAIR)] = d_key.astype(jnp.bfloat16)
    d_proj[top, columns(2 * width + i * PAIR, PAIR)] = d_v
    gvec[QUERY_BIAS : QUERY_BIAS + 1, columns(i * PAIR, PAIR)] = column_sums(d_q)
    gvec[VALUE_BIAS : VALUE_BIAS + 1, columns(i * PAIR, PAIR)] = column_sums(d_v)


def transpose_blocks(stack, turned):
    def body(i):
        part = stack[:, columns(i * 128, 128)].astype(jnp.float32).T.astype(jnp.bfloat16)
        turned[pl.ds(2 * i, 2)] = part.reshape(2, 2, UNIT, stack.shape[0])

    loop(stack.shape[1] // 128, body)


def turned_product(turned, core, right, mine, unit, right_column):
    width = mine.shape[2]
    tokens = turned.shape[3]

    def body(j):
        left = turned[:, pl.ds(core, 1)].reshape(CHIPS * UNIT, tokens)
        out = dot(left, right[:, columns(right_column + j * TILE, TILE)]).astype(jnp.bfloat16)
        mine[:, UNIT * unit : UNIT * unit + UNIT, columns(j * TILE, TILE)] = out.reshape(CHIPS, UNIT, TILE)

    loop(width // TILE, body)


class Both:
    def __init__(self, copies):
        self.copies = copies

    def start(self):
        for copy in self.copies:
            copy.start()

    def wait(self):
        for copy in self.copies:
            copy.wait()


def stream(total, begin, count, copy_of, body):
    if begin == 0:
        copy_of(0, 0).start()

    def step(n):
        j = begin + n

        @pl.when(j + 1 < total)
        def _():
            copy_of(j + 1, (j + 1) % 2).start()

        copy_of(j, j % 2).wait()
        body(j, j % 2)

    loop(count, step)


OPERANDS = ("tokens", "cotangent", "qkv", "out", "fc1", "fc2")


def small_rows(segments, parts):
    slots = jnp.pad(segments.astype(jnp.float32), (0, -segments.shape[0] % 128), constant_values=IMG_DEV)
    flat = jnp.concatenate([p for part in parts for p in [part] * (128 // part.shape[0])] + [slots])
    return jnp.pad(flat, (0, 2048 - flat.shape[0])).reshape(16, 128)


def spread(dst, small, sizes, count, width):
    me = lax.axis_index(AXIS)
    dst[...] = jnp.zeros_like(dst)
    at = 0
    for i, size in enumerate(sizes):
        row = small[i : i + 1, :].astype(jnp.bfloat16).astype(jnp.float32)
        lane = lax.broadcasted_iota(jnp.int32, (1, width), 1)
        for r in range(size * count // width):
            wide = jnp.concatenate([row] * (width // 128), 1)
            inside = (lane + r * width) // size == me
            dst[at : at + 1, :] = jnp.where(inside, wide, 0.0)
            at += 1


def settle(arrays):
    n = len(arrays)

    def kernel(*refs):
        sems = refs[3 * n]
        loads = [pltpu.make_async_copy(refs[i], refs[2 * n + i], sems.at[i]) for i in range(n)]
        stores = [pltpu.make_async_copy(refs[2 * n + i], refs[n + i], sems.at[n + i]) for i in range(n)]
        for copy in loads:
            copy.start()
        for load, store in zip(loads, stores):
            load.wait()
            store.start()
        for copy in stores:
            copy.wait()

    anyspec = pl.BlockSpec(memory_space=pl.ANY)
    return pl.pallas_call(
        kernel,
        out_shape=[jax.ShapeDtypeStruct(a.shape, a.dtype) for a in arrays],
        in_specs=[pl.BlockSpec(memory_space=pltpu.HBM)] * n,
        out_specs=[anyspec] * n,
        scratch_shapes=[pltpu.VMEM(a.shape, a.dtype) for a in arrays] + [pltpu.SemaphoreType.DMA((2 * n,))],
        compiler_params=pltpu.CompilerParams(vmem_limit_bytes=63 << 20),
    )(*arrays)


def block_all(count, tokens, segments, cotangent, shards, vectors):
    rows, width = tokens.shape
    hidden = shards[2].shape[1]
    f32, b16 = jnp.float32, jnp.bfloat16
    vec = jax.ShapeDtypeStruct((VECTOR_ROWS, width), f32)
    sizes = [v.shape[0] for v in vectors]
    both, half = 2 * rows, hidden // 2
    block = (hidden // count, width)
    tiles, tiles_in, per = hidden // TILE, width // TILE, width // TILE
    kinds = {
        "slope": ((rows, hidden), f32),
        "sh_q": (shards[0].shape, b16),
        "sh_o": (shards[1].shape, b16),
        "sh_u": (shards[2].shape, b16),
        "sh_d": (shards[3].shape, b16),
        "resid": ((rows, width), f32),
        "d_resid": ((rows, width), f32),
        "acc": ((rows, width), f32),
        "x_active": ((both, half), b16),
        "other": ((rows, half), b16),
        "y_mlp": ((both, width), b16),
        "y_inner": ((both, hidden), b16),
        "x_second": ((both, width), b16),
        "x_attended": ((both, width), b16),
        "y_branch": ((both, width), b16),
        "x_first": ((both, width), b16),
        "turned": ((CHIPS, 2, UNIT, both), b16),
        "qkv": ((rows, 3 * width), b16),
        "wo": ((width, width), b16),
        "cols": ((2, width, TILE), b16),
        "bias": ((rows, rows), f32),
        "gvec": (vec.shape, f32),
        "vecs": (vec.shape, f32),
    }
    names = list(kinds)
    crossing = ("y_mlp", "x_first", "x_second", "x_attended", "y_branch", "y_proj", "a0", "a1", "i0", "i1")

    def kernel(small, *refs):
        src = dict(zip(OPERANDS, refs[:6]))
        act_out, grad_out, wq_h, wu_h, wd_h, q_out, o_out, u_out, d_out, gvec_out = refs[6:16]
        refs = refs[16:]
        s = dict(zip(names, refs[: len(names)]))
        refs = refs[len(names) :]
        bufs, refs = refs[:21], refs[21:]
        (held, got, g_send, g_recv, g_core, g_own, vsend, vrecv) = refs[:8]
        (send, b_recv, z_recv, a_recv, x_send, x_recv, load, tile_sem, leave_sem, free) = refs[8:]
        me, z, core, _, _, _, _ = place()
        sib = me + 1 - 2 * core
        _, near, up, down, far = peers()
        top, low = pl.ds(0, rows), pl.ds(rows, rows)
        resid, d_resid, acc, vecs, gvec = (s[k] for k in ("resid", "d_resid", "acc", "vecs", "gvec"))
        tok = s["slope"].at[:, pl.ds(hidden - width, width)]

        homes = [tok, d_resid]
        at = 0
        for sh in shards:
            homes.append(s["slope"].at[pl.ds(at, sh.shape[0]), pl.ds(0, sh.shape[1])])
            at += sh.shape[0]
        loads = [pltpu.make_async_copy(src[n], h, load.at[i]) for i, (n, h) in enumerate(zip(OPERANDS, homes))]
        for i in (2, 3, 4, 5, 1):
            loads[i].start()
        entry_barrier(z, near, up, down, far)
        spread(held, small, sizes, count, width)
        v = Vec(held, got, vsend, vrecv)
        v.start(0)

        def cast_shard(i):
            loads[2 + i].wait()
            s[("sh_q", "sh_o", "sh_u", "sh_d")[i]][...] = homes[2 + i][...].astype(b16)

        homes_w = (wq_h, s["wo"], wu_h, wd_h)
        parts = []
        for p, (w, begin_at, share, zf) in enumerate(GATHER_PARTS):
            sh = s[("sh_q", "sh_o", "sh_u", "sh_d")[w]]
            wide = sh.shape[1]
            parts.append(
                Gather(p, sh, homes_w[w], zf, int(begin_at * wide), int(share * wide), g_send, g_recv, g_core, g_own)
            )
        timed = []
        for gi, group in enumerate(GROUPS):
            for p in group:
                timed += [(LAG * gi + j, gi, step) for j, step in enumerate(parts[p].steps())]

        def gather_at(t):
            for gi in range(len(GROUPS)):
                for tt, g, step in timed:
                    if (tt, g) == (t, gi):
                        step()

        def gathered(*which):
            for p in which:
                parts[p].ready()

        def cross_copy(name):
            i = crossing.index(name)
            if name == "y_proj":
                c = pl.ds(0, 3 * width)
                own, to = s["y_inner"].at[top, c], s["y_inner"].at[low, c]
            elif name in ("a0", "a1"):
                c = pl.ds(int(name[1]) * (half // 2), half // 2)
                own, to = s["other"].at[:, c], s["x_active"].at[low, c]
            elif name in ("i0", "i1"):
                c = pl.ds(int(name[1]) * half, half)
                own, to = s["y_inner"].at[top, c], s["y_inner"].at[low, c]
            else:
                own, to = s[name].at[top], s[name].at[low]
            return remote(own, to, x_send.at[i], x_recv.at[i], sib)

        def cross(name):
            cross_copy(name).start()

        def crossed(*which):
            for name in which:
                cross_copy(name).wait()

        def col_copy(full):
            return lambda j, slot: pltpu.make_async_copy(
                full.at[:, columns(j * TILE, TILE)], s["cols"].at[slot], tile_sem.at[slot]
            )

        def row_copy(full):
            def copy_of(j, slot):
                r = pl.ds(pl.multiple_of(j * TILE, TILE), TILE)
                return Both(
                    [
                        pltpu.make_async_copy(
                            full.at[r, pl.ds(i * TILE, TILE)],
                            s["cols"].at[slot, pl.ds(i * TILE, TILE)],
                            tile_sem.at[2 * (i + 1) + slot],
                        )
                        for i in range(width // TILE)
                    ]
                )

            return copy_of

        def leave(i, source, dst):
            return pltpu.make_async_copy(source, dst, leave_sem.at[i])

        first = len(sizes)
        seg_row = jnp.concatenate([small[first + i : first + i + 1, :] for i in range(-(-rows // 128))], 1)
        seg_col = jnp.broadcast_to(seg_row, (128, seg_row.shape[1])).T[:rows, 0:1]
        seg_row = seg_row[:, :rows]
        valid_col = seg_col < IMG_DEV

        def begin():
            allowed = (seg_col == seg_row) & (seg_row < IMG_DEV)
            s["bias"][...] = jnp.where(allowed, 0.0, -1e30)
            loads[1].wait()
            d_resid[...] = jnp.where(valid_col, d_resid[...], 0.0)
            s["y_mlp"][top, :] = d_resid[...].astype(b16)
            gvec[DOWN_BIAS : DOWN_BIAS + 1, :] = column_sums(s["y_mlp"][top, :])

        def project(part):
            def body(t, slot):
                j = t - tiles_in * part
                out = dot(s["x_first"][top, :], s["cols"][slot])
                if part == 0:
                    out = (out + vecs[QUERY_BIAS : QUERY_BIAS + 1, columns(j * TILE, TILE)]) * HEAD_DIM ** (-0.5)
                elif part == 2:
                    out = out + vecs[VALUE_BIAS : VALUE_BIAS + 1, columns(j * TILE, TILE)]
                s["qkv"][:, columns(t * TILE, TILE)] = out.astype(b16)

            stream(3 * tiles_in, tiles_in * part, tiles_in, col_copy(wq_h), body)

        def attend(first, n):
            loop(n, lambda i: attend_pair(first + i, width, s["qkv"], s["bias"], s["x_attended"].at[top]))

        def project_out():
            def body(j):
                c = columns(j * TILE, TILE)
                resid[:, c] = tok[:, c] + dot(s["x_attended"][top, :], s["wo"][:, c]) + vecs[OUT_BIAS : OUT_BIAS + 1, c]

            loop(tiles_in, body)

        def up_tiles(first, n):
            def body(j, slot):
                t = dot(s["x_second"][top, :], s["cols"][slot])
                t = t + vecs[pl.ds(UP_BIAS + j // per, 1), columns((j % per) * TILE, TILE)]
                cdf = 0.5 + 0.5 * lax.erf(t * (0.5**0.5))
                s["slope"][:, columns(j * TILE, TILE)] = cdf + t * (0.3989422804014327 * jnp.exp(-0.5 * t * t))
                act = (t * cdf).astype(b16)
                for i in range(TILE // 256):
                    even, odd = act[:, 256 * i : 256 * i + 128], act[:, 256 * i + 128 : 256 * i + 256]
                    c = columns((2 * j + i) * 128, 128)
                    s["x_active"][top, c] = jnp.where(core == 0, even, odd)
                    s["other"][:, c] = jnp.where(core == 0, odd, even)

            stream(tiles, first, n, col_copy(wu_h), body)

        def d_inner_tiles(first, n):
            def body(j, slot):
                size = TILE // 2
                for i in (0, 1):
                    c = columns(j * TILE + i * size, size)
                    d_act = 0.0
                    for part in range(width // TILE):
                        wrows = slice(part * TILE + i * size, part * TILE + i * size + size)
                        d_act = d_act + dot_nt(s["y_mlp"][top, part * TILE : part * TILE + TILE], s["cols"][slot, wrows, :])
                    dd = (d_act * s["slope"][:, c]).astype(b16)
                    s["y_inner"][top, c] = dd
                    gvec[pl.ds(UP_BIAS + j // per, 1), columns((j % per) * TILE + i * size, size)] = column_sums(dd)

            stream(tiles, first, n, row_copy(wd_h), body)

        def d_second_tiles(first, n):
            def body(j, slot):
                acc[...] += dot_nt(s["y_inner"][top, columns(j * TILE, TILE)], s["cols"][slot])

            stream(tiles, first, n, col_copy(wu_h), body)

        def d_first_tiles(first, n):
            def body(j, slot):
                acc[...] += dot_nt(s["y_inner"][top, columns(j * TILE, TILE)], s["cols"][slot])

            stream(3 * tiles_in, first, n, col_copy(wq_h), body)

        def down_tiles(first, n):
            def body(j, slot):
                c = columns(2 * j * 128, 256)
                for which, left in ((core, s["x_active"][top, c]), (1 - core, s["other"][:, c])):
                    for part in range(width // TILE):
                        right = [
                            s["cols"][slot, pl.ds(pl.multiple_of(part * TILE + (2 * i + which) * 128, 128), 128), :]
                            for i in (0, 1)
                        ]
                        acc[:, part * TILE : part * TILE + TILE] += dot(left, jnp.concatenate(right, 0))

            stream(tiles, first, n, row_copy(wd_h), body)

        def second_norm_back():
            def emit(r, back):
                total = d_resid[r, :] + back
                d_resid[r, :] = total
                s["y_branch"][r, :] = total.astype(b16)

            norm_back(acc, resid, vecs, GAIN_TWO, held, emit)
            gvec[GAIN_TWO : GAIN_TWO + 1, :] = jnp.sum(held[0:8, :], 0, keepdims=True)
            gvec[BIAS_TWO : BIAS_TWO + 1, :] = jnp.sum(held[8:16, :], 0, keepdims=True)

        def first_norm_back():
            def emit(r, back):
                d_resid[r, :] += back

            loads[0].wait()
            norm_back(acc, tok, vecs, GAIN_ONE, held, emit)
            gvec[GAIN_ONE : GAIN_ONE + 1, :] = jnp.sum(held[0:8, :], 0, keepdims=True)
            gvec[BIAS_ONE : BIAS_ONE + 1, :] = jnp.sum(held[8:16, :], 0, keepdims=True)

        stacked = pl.ds(96, block[0])
        results = [homes[2], homes[3]] + [s["slope"].at[stacked, pl.ds(i * width, width)] for i in (1, 0)]

        def leave_result(i):
            if i != 2:
                return leave(2 + i, results[i], (q_out, o_out, u_out, d_out)[i])
            return Both(
                [
                    leave(6 + unit, results[2].at[pl.ds(unit * UNIT, UNIT)], u_out.at[:, pl.ds(unit * width, width)])
                    for unit in range(UNITS)
                ]
            )

        def emit_down(chunk, total):
            results[3][pl.ds(16 * chunk, 16), :] = total

        def emit_up(chunk, total):
            results[2][pl.ds(16 * chunk, 16), :] = total

        def emit_attn(chunk, total):
            unit, r = chunk // 2, 16 * (chunk % 2)
            if unit == 3:
                results[1][pl.ds(r, 16), :] = total
            else:
                results[0][pl.ds(r, 16), width * unit : width * unit + width] = total

        mines = bufs[:3]
        reduces = []
        for piece, emit in enumerate((emit_down, emit_up, emit_attn)):
            pair = []
            for zf in (True, False):
                p = 2 * piece + (0 if zf else 1)
                mid = bufs[3 + 3 * p : 6 + 3 * p]
                row = 0 if zf else SPLIT_ROWS
                pair.append(Reduce(p, zf, row, mines[piece], *mid, send, b_recv, z_recv, a_recv, emit))
            reduces.append(pair)

        def stage(piece, j):
            for r in reduces[piece]:
                step = r.stages()[j]
                if step is not None:
                    step()

        def send_blocks(piece):
            for k in (3, 2, 1, 0):
                for r in reduces[piece]:
                    r.send_b(k)

        def drain(piece):
            for r in reduces[piece]:
                r.drain()

        def down_grad(n):
            i = n + (1 - z // 2) * (LINE - 1 - 2 * n)
            out = dot_tn(s["x_active"][:, columns(i * TILE, TILE)], s["y_mlp"][...]).astype(b16)
            mines[0][pl.ds(4 * i, 4)] = out.reshape(4, block[0], width)
            for r in reduces[0]:
                r.send_plane(i)

        def up_grad(first):
            for unit in (first, first + 1):
                turned_product(s["turned"], core, s["y_inner"], mines[1], unit, unit * width)

        def out_grad():
            transpose_blocks(s["x_attended"], s["turned"])
            turned_product(s["turned"], core, s["y_branch"], mines[2], 3, 0)
            transpose_blocks(s["x_first"], s["turned"])

        def qkv_grad():
            for unit in range(3):
                turned_product(s["turned"], core, s["y_inner"], mines[2], unit, unit * width)

        def finish_activations():
            resid[...] = jnp.where(valid_col, resid[...] + acc[...] + vecs[DOWN_BIAS : DOWN_BIAS + 1, :], 0.0)
            leave(0, resid, act_out).start()

        def clear():
            acc[...] = jnp.zeros_like(acc)

        def share_vectors():
            leave(1, d_resid, grad_out).start()
            held[...] = gvec[...]
            v.start(0)

        def d_attended_tile(j):
            size = TILE // 2
            wrows = pl.ds(pl.multiple_of(j * size, size), size)
            c = columns(j * size, size)
            s["y_mlp"][top, c] = dot_nt(s["y_branch"][top, :], s["wo"][wrows, :]).astype(b16)
            gvec[OUT_BIAS : OUT_BIAS + 1, c] = column_sums(s["y_branch"][top, c])

        def attend_back(first, n):
            loop(
                n,
                lambda i: attend_back_pair(
                    first + i, width, s["qkv"], s["y_mlp"].at[top], s["bias"], s["y_inner"], gvec
                ),
            )

        def known():
            vecs[...] = held[...]

        def norm_one():
            loads[0].wait()
            norm_into(s["x_first"].at[top], tok, vecs, GAIN_ONE, BIAS_ONE)

        def norm_two():
            norm_into(s["x_second"].at[top], resid, vecs, GAIN_TWO, BIAS_TWO)

        gvec[...] = jnp.zeros_like(gvec)
        for i in range(4):
            cast_shard(i)
        loads[0].start()
        gather_at(0)
        v.step(0)
        gather_at(1)
        gather_at(2)
        v.step(1)
        gather_at(3)
        v.step(2)
        gather_at(4)
        gather_at(5)
        v.step(3)
        begin()
        cross("y_mlp")
        gather_at(6)
        gather_at(7)
        v.step(4)
        known()
        gather_at(8)
        norm_one()
        cross("x_first")
        gather_at(9)
        gather_at(10)
        gather_at(11)
        gathered(0, 1)
        project(0)
        gather_at(12)
        project(1)
        project(2)
        attend(0, 2)
        gather_at(13)
        attend(2, 2)
        attend(4, 2)
        gather_at(14)
        attend(6, 2)
        cross("x_attended")
        gathered(2)
        project_out()
        norm_two()
        cross("x_second")
        gather_at(15)
        gather_at(16)
        gathered(3, 4)
        up_tiles(0, 2)
        up_tiles(2, 2)
        cross("a0")
        gather_at(17)
        up_tiles(4, 2)
        gather_at(18)
        up_tiles(6, 2)
        cross("a1")
        gather_at(19)
        crossed("y_mlp", "a0", "a1")
        down_grad(0)
        down_grad(1)
        down_grad(2)
        down_grad(3)
        gather_at(20)
        gather_at(21)
        crossed("x_second")
        transpose_blocks(s["x_second"], s["turned"])
        gathered(5, 6)
        d_inner_tiles(0, 2)
        d_inner_tiles(2, 2)
        cross("i0")
        stage(0, 0)
        d_inner_tiles(4, 2)
        d_inner_tiles(6, 2)
        cross("i1")
        loads[0].start()
        stage(0, 1)
        crossed("i0")
        up_grad(0)
        crossed("i1")
        up_grad(2)
        send_blocks(1)
        pl.semaphore_signal(free, inc=1, device_id=(sib,), device_id_type=MESH)
        stage(0, 2)
        clear()
        d_second_tiles(0, 4)
        d_second_tiles(4, 4)
        stage(0, 3)
        second_norm_back()
        cross("y_branch")
        loop(width // (TILE // 2), d_attended_tile)
        stage(0, 4)
        attend_back(0, 2)
        stage(0, 5)
        stage(1, 0)
        attend_back(2, 2)
        stage(1, 1)
        attend_back(4, 2)
        stage(0, 6)
        stage(1, 2)
        attend_back(6, 2)
        pl.semaphore_wait(free, 1)
        cross("y_proj")
        crossed("x_attended", "x_first", "y_branch")
        out_grad()
        stage(1, 3)
        crossed("y_proj")
        qkv_grad()
        send_blocks(2)
        stage(0, 7)
        leave_result(3).start()
        stage(1, 4)
        stage(1, 5)
        clear()
        d_first_tiles(0, 3)
        d_first_tiles(3, 3)
        stage(2, 0)
        first_norm_back()
        share_vectors()
        stage(1, 6)
        stage(2, 1)
        v.step(0)
        clear()
        down_tiles(0, 4)
        down_tiles(4, 4)
        finish_activations()
        stage(2, 2)
        stage(1, 7)
        leave_result(2).start()
        v.step(1)
        stage(2, 3)
        v.step(2)
        stage(2, 4)
        v.step(3)
        stage(2, 5)
        v.step(4)
        stage(2, 6)
        stage(2, 7)
        leave_result(0).start()
        leave_result(1).start()
        gvec_out[...] = held[...]
        for g in parts:
            g.drain()
        for piece in range(3):
            drain(piece)
        leave(0, resid, act_out).wait()
        leave(1, d_resid, grad_out).wait()
        for i in range(4):
            leave_result(i).wait()

    anyspec = pl.BlockSpec(memory_space=pl.ANY)
    vm = pl.BlockSpec(memory_space=pltpu.VMEM)
    dma = pltpu.SemaphoreType.DMA
    shape = jax.ShapeDtypeStruct
    n = len(GATHER_PARTS)
    bufs = [pltpu.VMEM((CHIPS,) + block, b16)] * 3
    for _ in range(3):
        for zf, height in ((True, SPLIT_ROWS), (False, block[0] - SPLIT_ROWS)):
            bufs += [pltpu.VMEM((m, height, width), b16) for m in (8, 5 if zf else 10, 4 if zf else 1)]
    outs = [
        ((rows, width), f32),
        ((rows, width), f32),
        ((width, 3 * width), b16),
        ((width, hidden), b16),
        ((hidden, width), b16),
        (shards[0].shape, f32),
        (shards[1].shape, f32),
        (shards[2].shape, f32),
        (shards[3].shape, f32),
        (vec.shape, f32),
    ]
    results = pl.pallas_call(
        kernel,
        out_shape=[shape(*o) for o in outs],
        in_specs=[vm] + [anyspec] * len(OPERANDS),
        out_specs=[anyspec] * 9 + [vm],
        scratch_shapes=[pltpu.VMEM(*kinds[k]) for k in names]
        + bufs
        + [
            pltpu.VMEM(vec.shape, f32),
            pltpu.VMEM((5,) + vec.shape, f32),
            dma((n, 4)),
            dma((n, 16)),
            dma((n,)),
            dma((n,)),
            dma((5,)),
            dma((5,)),
            dma((6, 4)),
            dma((6, 8)),
            dma((6, 10)),
            dma((6, 4)),
            dma((len(crossing),)),
            dma((len(crossing),)),
            dma((len(OPERANDS),)),
            dma((2 * (1 + width // TILE),)),
            dma((6 + UNITS,)),
            pltpu.SemaphoreType.REGULAR,
        ],
        compiler_params=pltpu.CompilerParams(collective_id=0, has_side_effects=True, vmem_limit_bytes=63 << 20),
    )(small_rows(segments, vectors), tokens, cotangent, *shards)
    settled = settle([results[0], results[1], *results[5:9]])
    return settled[0], settled[1], settled[2:], results[9]


def local_math(tokens, segments, cotangent, vectors, weights):
    gain_one, bias_one, mix_bias, proj_bias, gain_two, bias_two, up_bias, down_bias = vectors
    mix_weight, proj_weight, up_weight, down_weight = weights
    model_width = tokens.shape[1]
    valid_slot = segments < IMG_DEV
    allowed = (segments[:, None] == segments[None, :]) & valid_slot[None, :]
    gain_one_f = gain_one.astype(jnp.float32)
    bias_one_f = bias_one.astype(jnp.float32)
    first = halved(layer_norm(tokens, gain_one_f, bias_one_f))
    mix_bias_f = mix_bias.astype(jnp.float32)
    bias_row = jnp.concatenate(
        [mix_bias_f[:model_width], jnp.zeros((model_width,), jnp.float32), mix_bias_f[model_width:]]
    )
    projected = jnp.dot(first, mix_weight, preferred_element_type=jnp.float32) + bias_row
    queries = halved(projected[:, :model_width] * HEAD_DIM ** (-0.5))
    key_rows = halved(projected[:, model_width : 2 * model_width])
    values = halved(projected[:, 2 * model_width :])
    attended_stack, lse_stack = lax.map(
        lambda pieces: pair_forward(pieces, allowed),
        (head_pairs(queries), head_pairs(key_rows), head_pairs(values)),
    )
    attended = halved(join_pairs(attended_stack))
    residual = (
        tokens
        + jnp.dot(attended, proj_weight, preferred_element_type=jnp.float32)
        + proj_bias.astype(jnp.float32)
    )
    gain_two_f = gain_two.astype(jnp.float32)
    bias_two_f = bias_two.astype(jnp.float32)
    second = halved(layer_norm(residual, gain_two_f, bias_two_f))
    inner = jnp.dot(second, up_weight, preferred_element_type=jnp.float32) + up_bias.astype(
        jnp.float32
    )
    active = halved(jax.nn.gelu(inner, approximate=False))
    branch = jnp.dot(active, down_weight, preferred_element_type=jnp.float32) + down_bias.astype(
        jnp.float32
    )
    activations = jnp.where(valid_slot[:, None], residual + branch, 0.0)
    d_out = jnp.where(valid_slot[:, None], cotangent, 0.0)
    d_mlp = halved(d_out)
    grad_fc2_bias = jnp.sum(d_mlp, 0, dtype=jnp.float32)
    grad_fc2_weight = contract_rows(active, d_mlp)
    d_active = contract_cols(d_mlp, down_weight)
    gelu_back = jax.vjp(partial(jax.nn.gelu, approximate=False), inner)[1]
    d_inner = halved(gelu_back(d_active)[0])
    grad_fc1_bias = jnp.sum(d_inner, 0, dtype=jnp.float32)
    grad_fc1_weight = contract_rows(second, d_inner)
    d_second = contract_cols(d_inner, up_weight)
    norm_two_back = jax.vjp(layer_norm, residual, gain_two_f, bias_two_f)[1]
    d_norm2, grad_norm2_gain, grad_norm2_bias = norm_two_back(d_second)
    d_resid = d_out + d_norm2
    d_branch = halved(d_resid)
    grad_out_bias = jnp.sum(d_branch, 0, dtype=jnp.float32)
    grad_out_weight = contract_rows(attended, d_branch)
    d_attended = halved(contract_cols(d_branch, proj_weight))
    d_query_stack, d_key_stack, d_value_stack = lax.map(
        lambda pieces: pair_backward(pieces, allowed),
        (
            head_pairs(queries),
            head_pairs(key_rows),
            head_pairs(values),
            head_pairs(d_attended),
            lse_stack,
        ),
    )
    d_query = join_pairs(d_query_stack)
    d_value = join_pairs(d_value_stack)
    d_projected = jnp.concatenate([d_query, join_pairs(d_key_stack), d_value], 1)
    grad_qv_bias = jnp.concatenate(
        [jnp.sum(d_query, 0, dtype=jnp.float32), jnp.sum(d_value, 0, dtype=jnp.float32)]
    )
    grad_qkv_weight = contract_rows(first, d_projected)
    d_first = contract_cols(d_projected, mix_weight)
    norm_one_back = jax.vjp(layer_norm, tokens, gain_one_f, bias_one_f)[1]
    d_norm1, grad_norm1_gain, grad_norm1_bias = norm_one_back(d_first)
    input_grad = d_resid + d_norm1
    return (
        activations,
        input_grad,
        (grad_qkv_weight, grad_out_weight, grad_fc1_weight, grad_fc2_weight),
        (
            grad_norm1_gain,
            grad_norm1_bias,
            grad_qv_bias,
            grad_out_bias,
            grad_norm2_gain,
            grad_norm2_bias,
            grad_fc1_bias,
            grad_fc2_bias,
        ),
    )


def shards(count, tokens,
    segments,
    norm1_gain,
    norm1_bias,
    qkv_weight,
    qv_bias,
    out_weight,
    out_bias,
    norm2_gain,
    norm2_bias,
    fc1_weight,
    fc1_bias,
    fc2_weight,
    fc2_bias,
    cotangent,
):
    vector_shards = (norm1_gain, norm1_bias, qv_bias, out_bias, norm2_gain, norm2_bias, fc1_bias, fc2_bias)
    sizes = [v.shape[0] * count for v in vector_shards]
    starts = [sum(sizes[:i]) for i in range(len(sizes) + 1)]
    width = tokens.shape[1]
    position = lax.axis_index(AXIS)
    kernels = count == 32

    if kernels:
        activations, input_grad, weight_owned, vector_rows = block_all(
            count,
            tokens,
            segments,
            cotangent,
            (qkv_weight, out_weight, fc1_weight, fc2_weight),
            vector_shards,
        )
    else:
        weight_shards = [halved(w) for w in (qkv_weight, out_weight, fc1_weight, fc2_weight)]
        weights = [lax.all_gather(w, AXIS, axis=0, tiled=True) for w in weight_shards]
        vectors = [
            lax.all_gather(halved(v), AXIS, axis=0, tiled=True).astype(jnp.float32)
            for v in vector_shards
        ]
        activations, input_grad, weight_grads, vector_grads = local_math(
            tokens, segments, cotangent, vectors, weights
        )
    if kernels:
        flat = vector_rows.reshape(-1)
        vector_owned = [
            lax.dynamic_slice(flat, (starts[i] + position * (sizes[i] // count),), (sizes[i] // count,))
            for i in range(len(sizes))
        ]
    else:
        weight_owned = [
            lax.psum_scatter(g, AXIS, scatter_dimension=0, tiled=True) for g in weight_grads
        ]
        vector_owned = [
            lax.psum_scatter(g, AXIS, scatter_dimension=0, tiled=True) for g in vector_grads
        ]
    g1, b1, qvb, ob, g2, b2, f1b, f2b = vector_owned
    qkv_g, out_g, fc1_g, fc2_g = weight_owned
    return (activations, input_grad, g1, b1, qkv_g, qvb, out_g, ob, g2, b2, fc1_g, f1b, fc2_g, f2b)


def solution(mesh):
    in_specs = (
        P(AXIS, None),
        P(AXIS),
        P(AXIS),
        P(AXIS),
        P(AXIS, None),
        P(AXIS),
        P(AXIS, None),
        P(AXIS),
        P(AXIS),
        P(AXIS),
        P(AXIS, None),
        P(AXIS),
        P(AXIS, None),
        P(AXIS),
        P(AXIS, None),
    )
    out_specs = (
        P(AXIS, None),
        P(AXIS, None),
        P(AXIS),
        P(AXIS),
        P(AXIS, None),
        P(AXIS),
        P(AXIS, None),
        P(AXIS),
        P(AXIS),
        P(AXIS),
        P(AXIS, None),
        P(AXIS),
        P(AXIS, None),
        P(AXIS),
    )
    return jax.shard_map(
        partial(shards, mesh.size), mesh=mesh, in_specs=in_specs, out_specs=out_specs, check_vma=False)
```

```python
import functools
from functools import partial

import jax
import jax.numpy as jnp
from jax import lax
from jax.experimental import pallas as pl
from jax.experimental.pallas import tpu as pltpu
from jax.sharding import PartitionSpec as P

HEAD_DIM = 64
IMG_DEV = 1
AXIS = "dev"
MESH = pl.DeviceIdType.MESH


def layer_norm(rows_in, gain, bias):
    centre = rows_in - jnp.mean(rows_in, -1, keepdims=True)
    spread = jnp.mean(centre * centre, -1, keepdims=True)
    return centre * lax.rsqrt(spread + 1e-06) * gain + bias


def halved(array_in):
    return array_in.astype(jnp.bfloat16)


def contract_rows(left, right):
    return lax.dot_general(
        left, right, (((0,), (0,)), ((), ())), preferred_element_type=jnp.float32
    )


def contract_cols(left, right):
    return lax.dot_general(
        left, right, (((1,), (1,)), ((), ())), preferred_element_type=jnp.float32
    )


def head_pairs(block):
    return block.reshape(block.shape[0], -1, 2 * HEAD_DIM).transpose(1, 0, 2)


def join_pairs(stack):
    return stack.transpose(1, 0, 2).reshape(stack.shape[1], stack.shape[0] * stack.shape[2])


def masked_scores(query_heads, key_heads, allowed):
    scores = jnp.einsum("qhd,khd->hqk", query_heads, key_heads, preferred_element_type=jnp.float32)
    return jnp.where(allowed[None], scores, -1e30)


def pair_forward(pieces, allowed):
    q_pair, k_pair, v_pair = pieces
    row_count = q_pair.shape[0]
    query_heads = q_pair.reshape(row_count, 2, HEAD_DIM)
    key_heads = k_pair.reshape(row_count, 2, HEAD_DIM)
    value_heads = v_pair.reshape(row_count, 2, HEAD_DIM)
    scores = masked_scores(query_heads, key_heads, allowed)
    row_top = jnp.max(scores, -1, keepdims=True)
    powered = jnp.exp(scores - row_top)
    totals = jnp.sum(powered, -1, keepdims=True)
    probability = halved(powered / totals)
    attended = jnp.einsum(
        "hqk,khd->qhd", probability, value_heads, preferred_element_type=jnp.float32
    )
    return (attended.reshape(row_count, 2 * HEAD_DIM), row_top + jnp.log(totals))


def pair_backward(pieces, allowed):
    q_pair, k_pair, v_pair, g_pair, lse_pair = pieces
    row_count = q_pair.shape[0]
    query_heads = q_pair.reshape(row_count, 2, HEAD_DIM)
    key_heads = k_pair.reshape(row_count, 2, HEAD_DIM)
    value_heads = v_pair.reshape(row_count, 2, HEAD_DIM)
    grad_heads = g_pair.reshape(row_count, 2, HEAD_DIM)
    probability = jnp.exp(masked_scores(query_heads, key_heads, allowed) - lse_pair)
    d_prob = jnp.einsum("qhd,khd->hqk", grad_heads, value_heads, preferred_element_type=jnp.float32)
    row_inner = jnp.sum(probability * d_prob, -1, keepdims=True)
    d_scores = halved(probability * (d_prob - row_inner))
    d_query = halved(
        jnp.einsum("hqk,khd->qhd", d_scores, key_heads, preferred_element_type=jnp.float32)
    )
    d_query = d_query * jnp.bfloat16(HEAD_DIM ** (-0.5))
    d_key = halved(
        jnp.einsum("hqk,qhd->khd", d_scores, query_heads, preferred_element_type=jnp.float32)
    )
    d_value = halved(
        jnp.einsum(
            "hqk,qhd->khd", halved(probability), grad_heads, preferred_element_type=jnp.float32
        )
    )
    width_pair = 2 * HEAD_DIM
    return (
        d_query.reshape(row_count, width_pair),
        d_key.reshape(row_count, width_pair),
        d_value.reshape(row_count, width_pair),
    )


LINE, PLANE = 4, 8

def place():
    me = lax.axis_index(AXIS)
    core = me % 2
    x = (me // 2) % 2
    y = (me // 4) % 2
    z = me // PLANE
    a_bit = x * (1 - core) + y * core
    b_bit = y * (1 - core) + x * core
    a_step = (2 + 2 * core) * (1 - 2 * a_bit)
    b_step = (4 - 2 * core) * (1 - 2 * b_bit)
    return me, z, core, a_step, b_step, x, y


def remote(src, dst, send_sem, recv_sem, device):
    return pltpu.make_async_remote_copy(
        src_ref=src, dst_ref=dst, send_sem=send_sem, recv_sem=recv_sem, device_id=(device,), device_id_type=MESH
    )


def wait_for(ref, sem):
    pltpu.make_async_copy(ref, ref, sem).wait()


def entry_barrier(z, devices, up, down, far):
    bar = pltpu.get_barrier_semaphore()
    for dev in devices:
        pl.semaphore_signal(bar, inc=1, device_id=(dev,), device_id_type=MESH)

    @pl.when(z < LINE - 1)
    def _():
        pl.semaphore_signal(bar, inc=1, device_id=(up,), device_id_type=MESH)

    @pl.when(z > 0)
    def _():
        pl.semaphore_signal(bar, inc=1, device_id=(down,), device_id_type=MESH)

    pl.semaphore_signal(bar, inc=1, device_id=(far,), device_id_type=MESH)
    count = len(devices) + 1
    inner = (z > 0) & (z < LINE - 1)

    @pl.when(inner)
    def _():
        pl.semaphore_wait(bar, count + 2)

    @pl.when(jnp.logical_not(inner))
    def _():
        pl.semaphore_wait(bar, count + 1)


class Vec:
    def __init__(self, held, got, send, recv):
        me, z, core, _, _, x, y = place()
        self.to = [
            me + 1 - 2 * core,
            me + 2 - 4 * x,
            me + 4 - 8 * y,
            me + 8 - 16 * (z % 2),
            me + 16 - 32 * (z // 2),
        ]
        self.held, self.got, self.send, self.recv = held, got, send, recv

    def copy(self, i):
        return remote(self.held, self.got.at[i], self.send.at[i], self.recv.at[i], self.to[i])

    def start(self, i):
        self.copy(i).start()

    def step(self, i):
        self.copy(i).wait()
        self.held[...] += self.got[i]
        if i < 4:
            self.start(i + 1)


class Gather:
    def __init__(self, part, shard, full, z_first, start, size, send, recv, core_recv, own):
        self.p, self.z_first = part, z_first
        cols = pl.ds(start, size)
        self.shard, self.full, self.cols = shard.at[:, cols], full, cols
        self.send, self.recv, self.core_recv, self.own_sem = send, recv, core_recv, own
        self.rows = shard.shape[0]
        self.me, self.z, self.core, self.a_step, self.b_step, _, _ = place()
        self.sib = self.me + 1 - 2 * self.core

    def block(self, dev):
        return self.full.at[pl.ds(pl.multiple_of(dev * self.rows, self.rows), self.rows), self.cols]

    def ici(self, src, dev, way, to):
        remote(src, self.block(dev), self.send.at[self.p, way], self.recv.at[self.p, dev // 2], to).start()

    def to_a(self, src, dev):
        self.ici(src, dev, 0, self.me + self.a_step)

    def to_b(self, src, dev):
        self.ici(src, dev, 1, self.me + self.b_step)

    def to_core(self, src, dev):
        remote(src, self.block(dev), self.send.at[self.p, 2], self.core_recv.at[self.p], self.sib).start()

    def up(self, src, dev):
        @pl.when(self.z < LINE - 1)
        def _():
            self.ici(src, dev, 3, self.me + PLANE)

    def down(self, src, dev):
        @pl.when(self.z > 0)
        def _():
            self.ici(src, dev, 3, self.me - PLANE)

    def arrive(self, dev):
        wait_for(self.block(dev), self.recv.at[self.p, dev // 2])

    def own(self):
        pltpu.make_async_copy(self.shard, self.block(self.me), self.own_sem.at[self.p]).start()
        src = self.shard
        if self.z_first:
            self.up(src, self.me)
            self.down(src, self.me)
            self.to_a(src, self.me)
        else:
            self.to_a(src, self.me)
            self.up(src, self.me)
            self.down(src, self.me)
        self.to_b(src, self.me)
        self.to_core(src, self.me)

    def from_a(self, k=None):
        if not self.z_first:
            dev = self.me + self.a_step
            self.arrive(dev)
            src = self.block(dev)
            self.up(src, dev)
            self.down(src, dev)
            self.to_b(src, dev)
            self.to_core(src, dev)
            return

        def one(dev):
            self.arrive(dev)
            src = self.block(dev)
            self.to_b(src, dev)
            self.to_core(src, dev)

        self.sides(k, lambda off: one(self.me + self.a_step + off))

    def sides(self, k, fn):
        if k == 0:
            fn(0)
            return

        @pl.when(self.z >= k)
        def _():
            fn(-PLANE * k)

        @pl.when(self.z + k <= LINE - 1)
        def _():
            fn(PLANE * k)

    def from_z(self, k):
        for base in [self.me] if self.z_first else [self.me, self.me + self.a_step]:

            @pl.when(self.z >= k)
            def _():
                dev = base - PLANE * k
                self.arrive(dev)
                src = self.block(dev)
                self.up(src, dev)
                if self.z_first:
                    self.to_a(src, dev)
                self.to_b(src, dev)
                self.to_core(src, dev)

            @pl.when(self.z + k <= LINE - 1)
            def _():
                dev = base + PLANE * k
                self.arrive(dev)
                src = self.block(dev)
                self.down(src, dev)
                if self.z_first:
                    self.to_a(src, dev)
                self.to_b(src, dev)
                self.to_core(src, dev)

    def from_b(self, k):
        for base in [self.me + self.b_step, self.me + self.b_step + self.a_step]:

            def one(off):
                dev = base + off
                self.arrive(dev)
                self.to_core(self.block(dev), dev)

            self.sides(k, one)

    def many(self, count):
        return self.full.at[pl.ds(0, count * self.rows), self.cols]

    def steps(self):
        step = functools.partial
        z_steps = [step(self.from_z, k) for k in (1, 2, 3)]
        a_steps = [step(self.from_a, k) for k in range(LINE)] if self.z_first else [self.from_a]
        b_steps = [step(self.from_b, k) for k in range(LINE)]
        middle = z_steps + a_steps if self.z_first else a_steps + z_steps
        return [self.own] + middle + b_steps

    def ready(self):
        wait_for(self.shard, self.own_sem.at[self.p])
        wait_for(self.many(16), self.core_recv.at[self.p])

    def drain(self):
        a_count = 4 if self.z_first else 1
        z_unit = 1 if self.z_first else 2
        wait_for(self.many(a_count), self.send.at[self.p, 0])
        wait_for(self.many(8), self.send.at[self.p, 1])
        wait_for(self.many(16), self.send.at[self.p, 2])
        inner = (self.z > 0) & (self.z < LINE - 1)

        @pl.when(inner)
        def _():
            wait_for(self.many(5 * z_unit), self.send.at[self.p, 3])

        @pl.when(jnp.logical_not(inner))
        def _():
            wait_for(self.many(z_unit), self.send.at[self.p, 3])


def add_blocks(dst, terms, rows):
    def body(i, carry):
        r = pl.multiple_of(i * 16, 16)
        total = terms[0][pl.ds(r, 16), :].astype(jnp.float32)
        for term in terms[1:]:
            total = total + term[pl.ds(r, 16), :].astype(jnp.float32)
        dst[pl.ds(r, 16), :] = total.astype(dst.dtype)
        return carry

    lax.fori_loop(0, rows // 16, body, 0)


def peers():
    me, z, core, a_step, b_step, x, y = place()
    near = [me + 1 - 2 * core, me + a_step, me + b_step]
    return z, near, me + PLANE, me - PLANE, me + 16 - 32 * (z // 2)


GATHER_PARTS = (
    (0, 0, 0.5, True),
    (0, 0.5, 0.5, False),
    (1, 0, 1, False),
    (2, 0, 0.375, True),
    (2, 0.375, 0.625, False),
    (3, 0, 0.375, True),
    (3, 0.375, 0.625, False),
)
GROUPS = ((0, 1, 2), (3, 4), (5, 6))
LAG = 5
SPLIT_ROWS = 48


EPS = 1e-06
PAIR = 128
TILE = 512
ROWS = 32
GAIN_ONE, BIAS_ONE, QUERY_BIAS, VALUE_BIAS, OUT_BIAS, GAIN_TWO, BIAS_TWO, UP_BIAS, DOWN_BIAS = 0, 1, 2, 3, 4, 5, 6, 7, 11


def dot(left, right):
    return jnp.dot(left, right, preferred_element_type=jnp.float32)


def dot_nt(left, right):
    return lax.dot_general(left, right, (((1,), (1,)), ((), ())), preferred_element_type=jnp.float32)


def dot_tn(left, right):
    return lax.dot_general(left, right, (((0,), (0,)), ((), ())), preferred_element_type=jnp.float32)


def column_sums(block):
    return dot(jnp.ones((16, block.shape[0]), block.dtype), block)[0:1, :]


def columns(start, size):
    return pl.ds(pl.multiple_of(start, 128), size)


def loop(count, body):
    def step(i, carry):
        body(i)
        return carry

    lax.fori_loop(0, count, step, 0)


def centred(rows):
    centre = rows - jnp.mean(rows, -1, keepdims=True)
    spread = jnp.mean(centre * centre, -1, keepdims=True)
    return centre, lax.rsqrt(spread + EPS)


def norm_into(dst, src, vec, gain_row, bias_row):
    gain = vec[gain_row : gain_row + 1, :]
    bias = vec[bias_row : bias_row + 1, :]

    def body(i):
        r = pl.ds(pl.multiple_of(i * ROWS, ROWS), ROWS)
        centre, scale = centred(src[r, :])
        dst[r, :] = (centre * scale * gain + bias).astype(dst.dtype)

    loop(src.shape[0] // ROWS, body)


def norm_back(d_rows, src, vec, gain_row, sums, emit):
    gain = vec[gain_row : gain_row + 1, :]
    sums[...] = jnp.zeros_like(sums)

    def body(i):
        r = pl.ds(pl.multiple_of(i * ROWS, ROWS), ROWS)
        centre, scale = centred(src[r, :])
        n = centre * scale
        d = d_rows[r, :]
        e = d * gain
        dn = d * n
        for part in range(ROWS // 8):
            sums[0:8, :] += dn[8 * part : 8 * part + 8, :]
            sums[8:16, :] += d[8 * part : 8 * part + 8, :]
        back = scale * (e - jnp.mean(e, -1, keepdims=True) - n * jnp.mean(e * n, -1, keepdims=True))
        emit(r, back)

    loop(src.shape[0] // ROWS, body)


def own_half(rows, head):
    lane = lax.broadcasted_iota(jnp.int32, rows.shape, 1)
    inside = (lane < HEAD_DIM) if head == 0 else (lane >= HEAD_DIM)
    return jnp.where(inside, rows, jnp.zeros_like(rows))


def halves(first, second):
    lane = lax.broadcasted_iota(jnp.int32, first.shape, 1)
    return jnp.where(lane < HEAD_DIM, first, second)


def probabilities(query, key, bias):
    scores = dot_nt(query, key) + bias
    powered = jnp.exp(scores - jnp.max(scores, -1, keepdims=True))
    return powered * (1.0 / jnp.sum(powered, -1, keepdims=True))


def attend_pair(i, width, qkv, bias, attended):
    q = qkv[:, columns(i * PAIR, PAIR)]
    k = qkv[:, columns(width + i * PAIR, PAIR)]
    v = qkv[:, columns(2 * width + i * PAIR, PAIR)]
    parts = []
    for head in (0, 1):
        p = probabilities(own_half(q, head), k, bias[...]).astype(jnp.bfloat16)
        parts.append(dot(p, v))
    attended[:, columns(i * PAIR, PAIR)] = halves(*parts).astype(jnp.bfloat16)


UNITS = 4
VECTOR_ROWS = 16
UNIT = 32
CHIPS = 16


class Reduce:
    def __init__(self, part, z_first, first_row, mine, b_buf, z_buf, a_buf, send, b_recv, z_recv, a_recv, emit):
        self.p, self.z_first, self.first_row, self.emit = part, z_first, first_row, emit
        self.whole, self.b_buf, self.z_buf, self.a_buf = mine, b_buf, z_buf, a_buf
        self.send, self.b_recv, self.z_recv, self.a_recv = send, b_recv, z_recv, a_recv
        self.rows = b_buf.shape[1]
        self.me, self.z, self.core, self.a_step, self.b_step, self.x, self.y = place()

    def mine(self, chip):
        return self.whole.at[chip, pl.ds(self.first_row, self.rows)]

    def many(self, count):
        return self.whole.at[pl.ds(0, count), pl.ds(0, self.rows)]

    def sides(self, k, fn):
        if k == 0:
            fn(0)
            return

        @pl.when(self.z >= k)
        def _():
            fn(-k)

        @pl.when(self.z + k <= LINE - 1)
        def _():
            fn(k)

    def b_slot(self, dev):
        x = (dev // 2) % 2
        y = (dev // 4) % 2
        a_bit = x * (1 - self.core) + y * self.core
        return (dev // PLANE) * 2 + a_bit

    def send_plane(self, plane):
        for a in (self.a_step, 0):
            dev = self.me + self.b_step + a + PLANE * (plane - self.z)
            slot = self.b_slot(dev)
            remote(
                self.mine(dev // 2),
                self.b_buf.at[slot],
                self.send.at[self.p, 1],
                self.b_recv.at[self.p, slot],
                self.me + self.b_step,
            ).start()

    def send_b(self, k):
        self.sides(k, lambda sign: self.send_plane(self.z + sign))

    def after_b(self, dev):
        slot = self.b_slot(dev)
        wait_for(self.b_buf.at[slot], self.b_recv.at[self.p, slot])
        return [self.mine(dev // 2), self.b_buf.at[slot]]

    def a_slot(self, dev):
        return dev // PLANE if self.z_first else 0

    def to_a(self, dev):
        slot = self.a_slot(dev)
        remote(
            self.mine(dev // 2),
            self.a_buf.at[slot],
            self.send.at[self.p, 0],
            self.a_recv.at[self.p, slot],
            self.me + self.a_step,
        ).start()

    def send_a(self, k):
        def one(s):
            dev = self.me + self.a_step + PLANE * s
            add_blocks(self.mine(dev // 2), self.after_b(dev), self.rows)
            self.to_a(dev)

        self.sides(k, one)

    def after_a(self, dev):
        slot = self.a_slot(dev)
        wait_for(self.a_buf.at[slot], self.a_recv.at[self.p, slot])
        return [self.a_buf.at[slot]]

    def z_slot(self, i, dest):
        return i * (LINE + 1) + dest

    def along_z(self, k):
        for i, a in [(0, 0)] if self.z_first else [(1, self.a_step), (0, 0)]:
            for sign in (-1, 1):

                @pl.when((self.z >= k) if sign < 0 else (self.z + k <= LINE - 1))
                def _():
                    dev = self.me + a + sign * PLANE * k
                    chip = dev // 2
                    terms = self.after_b(dev)
                    if self.z_first:
                        terms = terms + self.after_a(dev)
                    slot = self.z_slot(i, self.z + sign * k)
                    there = self.z_slot(i, LINE) if (k == 1 and sign > 0) else slot
                    more = (self.z < LINE - 1) if sign < 0 else (self.z > 0)

                    @pl.when(more)
                    def _():
                        wait_for(self.z_buf.at[slot], self.z_recv.at[self.p, slot])
                        add_blocks(self.mine(chip), terms + [self.z_buf.at[slot]], self.rows)

                    @pl.when(jnp.logical_not(more))
                    def _():
                        add_blocks(self.mine(chip), terms, self.rows)

                    remote(
                        self.mine(chip),
                        self.z_buf.at[there],
                        self.send.at[self.p, 3],
                        self.z_recv.at[self.p, there],
                        self.me + sign * PLANE,
                    ).start()

    def home_terms(self, i, dev, fn):
        terms = self.after_b(dev)
        if self.z_first:
            terms = terms + self.after_a(dev)
        above = self.z_slot(i, self.z)
        below = self.z_slot(i, LINE)
        for has_above, has_below, cond in (
            (True, False, self.z == 0),
            (True, True, (self.z > 0) & (self.z < LINE - 1)),
            (False, True, self.z == LINE - 1),
        ):

            @pl.when(cond)
            def _():
                more = list(terms)
                for slot, has in ((above, has_above), (below, has_below)):
                    if has:
                        wait_for(self.z_buf.at[slot], self.z_recv.at[self.p, slot])
                        more.append(self.z_buf.at[slot])
                fn(more)

    def home_a(self):
        dev = self.me + self.a_step
        self.home_terms(1, dev, lambda terms: add_blocks(self.mine(dev // 2), terms, self.rows))
        self.to_a(dev)

    def home(self):
        def finish(terms):
            if not self.z_first:
                terms = terms + self.after_a(self.me)
            for chunk in range(self.rows // 16):
                r = slice(16 * chunk, 16 * chunk + 16)
                total = terms[0][r, :].astype(jnp.float32)
                for term in terms[1:]:
                    total = total + term[r, :].astype(jnp.float32)
                self.emit(self.first_row // 16 + chunk, total)

        self.home_terms(0, self.me, finish)

    def stages(self):
        step = functools.partial
        z_steps = [step(self.along_z, k) for k in (3, 2, 1)]
        if self.z_first:
            return [step(self.send_a, k) for k in (3, 2, 1, 0)] + z_steps + [self.home]
        return z_steps + [None, None, None, self.home_a, self.home]

    def drain(self):
        wait_for(self.many(8), self.send.at[self.p, 1])
        wait_for(self.many(4 if self.z_first else 1), self.send.at[self.p, 0])
        wait_for(self.many(3 if self.z_first else 6), self.send.at[self.p, 3])


def attend_back_pair(i, width, qkv, d_attended, bias, d_proj, gvec):
    rows = d_attended.shape[0]
    q = qkv[:, columns(i * PAIR, PAIR)]
    k = qkv[:, columns(width + i * PAIR, PAIR)]
    v = qkv[:, columns(2 * width + i * PAIR, PAIR)]
    g = d_attended[:, columns(i * PAIR, PAIR)]
    d_query, d_key, d_value = [], 0.0, 0.0
    for head in (0, 1):
        qh, gh = own_half(q, head), own_half(g, head)
        p = probabilities(qh, k, bias[...])
        d_p = dot_nt(gh, v)
        inner = jnp.sum(p * d_p, -1, keepdims=True)
        d_s = (p * (d_p - inner)).astype(jnp.bfloat16)
        d_query.append(dot(d_s, k))
        d_key = d_key + dot_tn(d_s, qh)
        d_value = d_value + dot_tn(p.astype(jnp.bfloat16), gh)
    d_q = (halves(*d_query).astype(jnp.bfloat16).astype(jnp.float32) * HEAD_DIM ** (-0.5)).astype(jnp.bfloat16)
    d_v = d_value.astype(jnp.bfloat16)
    top = pl.ds(0, rows)
    d_proj[top, columns(i * PAIR, PAIR)] = d_q
    d_proj[top, columns(width + i * PAIR, PAIR)] = d_key.astype(jnp.bfloat16)
    d_proj[top, columns(2 * width + i * PAIR, PAIR)] = d_v
    gvec[QUERY_BIAS : QUERY_BIAS + 1, columns(i * PAIR, PAIR)] = column_sums(d_q)
    gvec[VALUE_BIAS : VALUE_BIAS + 1, columns(i * PAIR, PAIR)] = column_sums(d_v)


def transpose_blocks(stack, turned):
    def body(i):
        part = stack[:, columns(i * 128, 128)].astype(jnp.float32).T.astype(jnp.bfloat16)
        turned[pl.ds(2 * i, 2)] = part.reshape(2, 2, UNIT, stack.shape[0])

    loop(stack.shape[1] // 128, body)


def turned_product(turned, core, right, mine, unit, right_column):
    width = mine.shape[2]
    tokens = turned.shape[3]

    def body(j):
        left = turned[:, pl.ds(core, 1)].reshape(CHIPS * UNIT, tokens)
        out = dot(left, right[:, columns(right_column + j * TILE, TILE)]).astype(jnp.bfloat16)
        mine[:, UNIT * unit : UNIT * unit + UNIT, columns(j * TILE, TILE)] = out.reshape(CHIPS, UNIT, TILE)

    loop(width // TILE, body)


class Both:
    def __init__(self, copies):
        self.copies = copies

    def start(self):
        for copy in self.copies:
            copy.start()

    def wait(self):
        for copy in self.copies:
            copy.wait()


def stream(total, begin, count, copy_of, body):
    if begin == 0:
        copy_of(0, 0).start()

    def step(n):
        j = begin + n

        @pl.when(j + 1 < total)
        def _():
            copy_of(j + 1, (j + 1) % 2).start()

        copy_of(j, j % 2).wait()
        body(j, j % 2)

    loop(count, step)


OPERANDS = ("tokens", "cotangent", "qkv", "out", "fc1", "fc2")


def small_rows(segments, parts):
    slots = jnp.pad(segments.astype(jnp.float32), (0, -segments.shape[0] % 128), constant_values=IMG_DEV)
    flat = jnp.concatenate([p for part in parts for p in [part] * (128 // part.shape[0])] + [slots])
    return jnp.pad(flat, (0, 2048 - flat.shape[0])).reshape(16, 128)


def spread(dst, small, sizes, count, width):
    me = lax.axis_index(AXIS)
    dst[...] = jnp.zeros_like(dst)
    at = 0
    for i, size in enumerate(sizes):
        row = small[i : i + 1, :].astype(jnp.bfloat16).astype(jnp.float32)
        lane = lax.broadcasted_iota(jnp.int32, (1, width), 1)
        for r in range(size * count // width):
            wide = jnp.concatenate([row] * (width // 128), 1)
            inside = (lane + r * width) // size == me
            dst[at : at + 1, :] = jnp.where(inside, wide, 0.0)
            at += 1


def settle(arrays):
    n = len(arrays)

    def kernel(*refs):
        sems = refs[3 * n]
        loads = [pltpu.make_async_copy(refs[i], refs[2 * n + i], sems.at[i]) for i in range(n)]
        stores = [pltpu.make_async_copy(refs[2 * n + i], refs[n + i], sems.at[n + i]) for i in range(n)]
        for copy in loads:
            copy.start()
        for load, store in zip(loads, stores):
            load.wait()
            store.start()
        for copy in stores:
            copy.wait()

    anyspec = pl.BlockSpec(memory_space=pl.ANY)
    return pl.pallas_call(
        kernel,
        out_shape=[jax.ShapeDtypeStruct(a.shape, a.dtype) for a in arrays],
        in_specs=[pl.BlockSpec(memory_space=pltpu.HBM)] * n,
        out_specs=[anyspec] * n,
        scratch_shapes=[pltpu.VMEM(a.shape, a.dtype) for a in arrays] + [pltpu.SemaphoreType.DMA((2 * n,))],
        compiler_params=pltpu.CompilerParams(vmem_limit_bytes=63 << 20),
    )(*arrays)


def block_all(count, tokens, segments, cotangent, shards, vectors):
    rows, width = tokens.shape
    hidden = shards[2].shape[1]
    f32, b16 = jnp.float32, jnp.bfloat16
    vec = jax.ShapeDtypeStruct((VECTOR_ROWS, width), f32)
    sizes = [v.shape[0] for v in vectors]
    both, half = 2 * rows, hidden // 2
    block = (hidden // count, width)
    tiles, tiles_in, per = hidden // TILE, width // TILE, width // TILE
    kinds = {
        "slope": ((rows, hidden), f32),
        "sh_q": (shards[0].shape, b16),
        "sh_o": (shards[1].shape, b16),
        "sh_u": (shards[2].shape, b16),
        "sh_d": (shards[3].shape, b16),
        "resid": ((rows, width), f32),
        "d_resid": ((rows, width), f32),
        "acc": ((rows, width), f32),
        "x_active": ((both, half), b16),
        "other": ((rows, half), b16),
        "y_mlp": ((both, width), b16),
        "y_inner": ((both, hidden), b16),
        "x_second": ((both, width), b16),
        "x_attended": ((both, width), b16),
        "y_branch": ((both, width), b16),
        "x_first": ((both, width), b16),
        "turned": ((CHIPS, 2, UNIT, both), b16),
        "qkv": ((rows, 3 * width), b16),
        "wo": ((width, width), b16),
        "cols": ((2, width, TILE), b16),
        "bias": ((rows, rows), f32),
        "gvec": (vec.shape, f32),
        "vecs": (vec.shape, f32),
    }
    names = list(kinds)
    crossing = ("y_mlp", "x_first", "x_second", "x_attended", "y_branch", "y_proj", "a0", "a1", "i0", "i1")

    def kernel(small, *refs):
        src = dict(zip(OPERANDS, refs[:6]))
        act_out, grad_out, wq_h, wu_h, wd_h, q_out, o_out, u_out, d_out, gvec_out = refs[6:16]
        refs = refs[16:]
        s = dict(zip(names, refs[: len(names)]))
        refs = refs[len(names) :]
        bufs, refs = refs[:21], refs[21:]
        (held, got, g_send, g_recv, g_core, g_own, vsend, vrecv) = refs[:8]
        (send, b_recv, z_recv, a_recv, x_send, x_recv, load, tile_sem, leave_sem, free) = refs[8:]
        me, z, core, _, _, _, _ = place()
        sib = me + 1 - 2 * core
        _, near, up, down, far = peers()
        top, low = pl.ds(0, rows), pl.ds(rows, rows)
        resid, d_resid, acc, vecs, gvec = (s[k] for k in ("resid", "d_resid", "acc", "vecs", "gvec"))
        tok = s["slope"].at[:, pl.ds(hidden - width, width)]

        homes = [tok, d_resid]
        at = 0
        for sh in shards:
            homes.append(s["slope"].at[pl.ds(at, sh.shape[0]), pl.ds(0, sh.shape[1])])
            at += sh.shape[0]
        loads = [pltpu.make_async_copy(src[n], h, load.at[i]) for i, (n, h) in enumerate(zip(OPERANDS, homes))]
        for i in (2, 3, 4, 5, 1):
            loads[i].start()
        entry_barrier(z, near, up, down, far)
        spread(held, small, sizes, count, width)
        v = Vec(held, got, vsend, vrecv)
        v.start(0)

        def cast_shard(i):
            loads[2 + i].wait()
            s[("sh_q", "sh_o", "sh_u", "sh_d")[i]][...] = homes[2 + i][...].astype(b16)

        homes_w = (wq_h, s["wo"], wu_h, wd_h)
        parts = []
        for p, (w, begin_at, share, zf) in enumerate(GATHER_PARTS):
            sh = s[("sh_q", "sh_o", "sh_u", "sh_d")[w]]
            wide = sh.shape[1]
            parts.append(
                Gather(p, sh, homes_w[w], zf, int(begin_at * wide), int(share * wide), g_send, g_recv, g_core, g_own)
            )
        timed = []
        for gi, group in enumerate(GROUPS):
            for p in group:
                timed += [(LAG * gi + j, gi, step) for j, step in enumerate(parts[p].steps())]

        def gather_at(t):
            for gi in range(len(GROUPS)):
                for tt, g, step in timed:
                    if (tt, g) == (t, gi):
                        step()

        def gathered(*which):
            for p in which:
                parts[p].ready()

        def cross_copy(name):
            i = crossing.index(name)
            if name == "y_proj":
                c = pl.ds(0, 3 * width)
                own, to = s["y_inner"].at[top, c], s["y_inner"].at[low, c]
            elif name in ("a0", "a1"):
                c = pl.ds(int(name[1]) * (half // 2), half // 2)
                own, to = s["other"].at[:, c], s["x_active"].at[low, c]
            elif name in ("i0", "i1"):
                c = pl.ds(int(name[1]) * half, half)
                own, to = s["y_inner"].at[top, c], s["y_inner"].at[low, c]
            else:
                own, to = s[name].at[top], s[name].at[low]
            return remote(own, to, x_send.at[i], x_recv.at[i], sib)

        def cross(name):
            cross_copy(name).start()

        def crossed(*which):
            for name in which:
                cross_copy(name).wait()

        def col_copy(full):
            return lambda j, slot: pltpu.make_async_copy(
                full.at[:, columns(j * TILE, TILE)], s["cols"].at[slot], tile_sem.at[slot]
            )

        def row_copy(full):
            def copy_of(j, slot):
                r = pl.ds(pl.multiple_of(j * TILE, TILE), TILE)
                return Both(
                    [
                        pltpu.make_async_copy(
                            full.at[r, pl.ds(i * TILE, TILE)],
                            s["cols"].at[slot, pl.ds(i * TILE, TILE)],
                            tile_sem.at[2 * (i + 1) + slot],
                        )
                        for i in range(width // TILE)
                    ]
                )

            return copy_of

        def leave(i, source, dst):
            return pltpu.make_async_copy(source, dst, leave_sem.at[i])

        first = len(sizes)
        seg_row = jnp.concatenate([small[first + i : first + i + 1, :] for i in range(-(-rows // 128))], 1)
        seg_col = jnp.broadcast_to(seg_row, (128, seg_row.shape[1])).T[:rows, 0:1]
        seg_row = seg_row[:, :rows]
        valid_col = seg_col < IMG_DEV

        def begin():
            allowed = (seg_col == seg_row) & (seg_row < IMG_DEV)
            s["bias"][...] = jnp.where(allowed, 0.0, -1e30)
            loads[1].wait()
            d_resid[...] = jnp.where(valid_col, d_resid[...], 0.0)
            s["y_mlp"][top, :] = d_resid[...].astype(b16)
            gvec[DOWN_BIAS : DOWN_BIAS + 1, :] = column_sums(s["y_mlp"][top, :])

        def project(part):
            def body(t, slot):
                j = t - tiles_in * part
                out = dot(s["x_first"][top, :], s["cols"][slot])
                if part == 0:
                    out = (out + vecs[QUERY_BIAS : QUERY_BIAS + 1, columns(j * TILE, TILE)]) * HEAD_DIM ** (-0.5)
                elif part == 2:
                    out = out + vecs[VALUE_BIAS : VALUE_BIAS + 1, columns(j * TILE, TILE)]
                s["qkv"][:, columns(t * TILE, TILE)] = out.astype(b16)

            stream(3 * tiles_in, tiles_in * part, tiles_in, col_copy(wq_h), body)

        def attend(first, n):
            loop(n, lambda i: attend_pair(first + i, width, s["qkv"], s["bias"], s["x_attended"].at[top]))

        def project_out():
            def body(j):
                c = columns(j * TILE, TILE)
                resid[:, c] = tok[:, c] + dot(s["x_attended"][top, :], s["wo"][:, c]) + vecs[OUT_BIAS : OUT_BIAS + 1, c]

            loop(tiles_in, body)

        def up_tiles(first, n):
            def body(j, slot):
                t = dot(s["x_second"][top, :], s["cols"][slot])
                t = t + vecs[pl.ds(UP_BIAS + j // per, 1), columns((j % per) * TILE, TILE)]
                cdf = 0.5 + 0.5 * lax.erf(t * (0.5**0.5))
                s["slope"][:, columns(j * TILE, TILE)] = cdf + t * (0.3989422804014327 * jnp.exp(-0.5 * t * t))
                act = (t * cdf).astype(b16)
                for i in range(TILE // 256):
                    even, odd = act[:, 256 * i : 256 * i + 128], act[:, 256 * i + 128 : 256 * i + 256]
                    c = columns((2 * j + i) * 128, 128)
                    s["x_active"][top, c] = jnp.where(core == 0, even, odd)
                    s["other"][:, c] = jnp.where(core == 0, odd, even)

            stream(tiles, first, n, col_copy(wu_h), body)

        def d_inner_tiles(first, n):
            def body(j, slot):
                size = TILE // 2
                for i in (0, 1):
                    c = columns(j * TILE + i * size, size)
                    d_act = 0.0
                    for part in range(width // TILE):
                        wrows = slice(part * TILE + i * size, part * TILE + i * size + size)
                        d_act = d_act + dot_nt(s["y_mlp"][top, part * TILE : part * TILE + TILE], s["cols"][slot, wrows, :])
                    dd = (d_act * s["slope"][:, c]).astype(b16)
                    s["y_inner"][top, c] = dd
                    gvec[pl.ds(UP_BIAS + j // per, 1), columns((j % per) * TILE + i * size, size)] = column_sums(dd)

            stream(tiles, first, n, row_copy(wd_h), body)

        def d_second_tiles(first, n):
            def body(j, slot):
                acc[...] += dot_nt(s["y_inner"][top, columns(j * TILE, TILE)], s["cols"][slot])

            stream(tiles, first, n, col_copy(wu_h), body)

        def d_first_tiles(first, n):
            def body(j, slot):
                acc[...] += dot_nt(s["y_inner"][top, columns(j * TILE, TILE)], s["cols"][slot])

            stream(3 * tiles_in, first, n, col_copy(wq_h), body)

        def down_tiles(first, n):
            def body(j, slot):
                c = columns(2 * j * 128, 256)
                for which, left in ((core, s["x_active"][top, c]), (1 - core, s["other"][:, c])):
                    for part in range(width // TILE):
                        right = [
                            s["cols"][slot, pl.ds(pl.multiple_of(part * TILE + (2 * i + which) * 128, 128), 128), :]
                            for i in (0, 1)
                        ]
                        acc[:, part * TILE : part * TILE + TILE] += dot(left, jnp.concatenate(right, 0))

            stream(tiles, first, n, row_copy(wd_h), body)

        def second_norm_back():
            def emit(r, back):
                total = d_resid[r, :] + back
                d_resid[r, :] = total
                s["y_branch"][r, :] = total.astype(b16)

            norm_back(acc, resid, vecs, GAIN_TWO, held, emit)
            gvec[GAIN_TWO : GAIN_TWO + 1, :] = jnp.sum(held[0:8, :], 0, keepdims=True)
            gvec[BIAS_TWO : BIAS_TWO + 1, :] = jnp.sum(held[8:16, :], 0, keepdims=True)

        def first_norm_back():
            def emit(r, back):
                d_resid[r, :] += back

            loads[0].wait()
            norm_back(acc, tok, vecs, GAIN_ONE, held, emit)
            gvec[GAIN_ONE : GAIN_ONE + 1, :] = jnp.sum(held[0:8, :], 0, keepdims=True)
            gvec[BIAS_ONE : BIAS_ONE + 1, :] = jnp.sum(held[8:16, :], 0, keepdims=True)

        stacked = pl.ds(96, block[0])
        results = [homes[2], homes[3]] + [s["slope"].at[stacked, pl.ds(i * width, width)] for i in (1, 0)]

        def leave_result(i):
            if i != 2:
                return leave(2 + i, results[i], (q_out, o_out, u_out, d_out)[i])
            return Both(
                [
                    leave(6 + unit, results[2].at[pl.ds(unit * UNIT, UNIT)], u_out.at[:, pl.ds(unit * width, width)])
                    for unit in range(UNITS)
                ]
            )

        def emit_down(chunk, total):
            results[3][pl.ds(16 * chunk, 16), :] = total

        def emit_up(chunk, total):
            results[2][pl.ds(16 * chunk, 16), :] = total

        def emit_attn(chunk, total):
            unit, r = chunk // 2, 16 * (chunk % 2)
            if unit == 3:
                results[1][pl.ds(r, 16), :] = total
            else:
                results[0][pl.ds(r, 16), width * unit : width * unit + width] = total

        mines = bufs[:3]
        reduces = []
        for piece, emit in enumerate((emit_down, emit_up, emit_attn)):
            pair = []
            for zf in (True, False):
                p = 2 * piece + (0 if zf else 1)
                mid = bufs[3 + 3 * p : 6 + 3 * p]
                row = 0 if zf else SPLIT_ROWS
                pair.append(Reduce(p, zf, row, mines[piece], *mid, send, b_recv, z_recv, a_recv, emit))
            reduces.append(pair)

        def stage(piece, j):
            for r in reduces[piece]:
                step = r.stages()[j]
                if step is not None:
                    step()

        def send_blocks(piece):
            for k in (3, 2, 1, 0):
                for r in reduces[piece]:
                    r.send_b(k)

        def drain(piece):
            for r in reduces[piece]:
                r.drain()

        def down_grad(n):
            i = n + (1 - z // 2) * (LINE - 1 - 2 * n)
            out = dot_tn(s["x_active"][:, columns(i * TILE, TILE)], s["y_mlp"][...]).astype(b16)
            mines[0][pl.ds(4 * i, 4)] = out.reshape(4, block[0], width)
            for r in reduces[0]:
                r.send_plane(i)

        def up_grad(first):
            for unit in (first, first + 1):
                turned_product(s["turned"], core, s["y_inner"], mines[1], unit, unit * width)

        def out_grad():
            transpose_blocks(s["x_attended"], s["turned"])
            turned_product(s["turned"], core, s["y_branch"], mines[2], 3, 0)
            transpose_blocks(s["x_first"], s["turned"])

        def qkv_grad():
            for unit in range(3):
                turned_product(s["turned"], core, s["y_inner"], mines[2], unit, unit * width)

        def finish_activations():
            resid[...] = jnp.where(valid_col, resid[...] + acc[...] + vecs[DOWN_BIAS : DOWN_BIAS + 1, :], 0.0)
            leave(0, resid, act_out).start()

        def clear():
            acc[...] = jnp.zeros_like(acc)

        def share_vectors():
            leave(1, d_resid, grad_out).start()
            held[...] = gvec[...]
            v.start(0)

        def d_attended_tile(j):
            size = TILE // 2
            wrows = pl.ds(pl.multiple_of(j * size, size), size)
            c = columns(j * size, size)
            s["y_mlp"][top, c] = dot_nt(s["y_branch"][top, :], s["wo"][wrows, :]).astype(b16)
            gvec[OUT_BIAS : OUT_BIAS + 1, c] = column_sums(s["y_branch"][top, c])

        def attend_back(first, n):
            loop(
                n,
                lambda i: attend_back_pair(
                    first + i, width, s["qkv"], s["y_mlp"].at[top], s["bias"], s["y_inner"], gvec
                ),
            )

        def known():
            vecs[...] = held[...]

        def norm_one():
            loads[0].wait()
            norm_into(s["x_first"].at[top], tok, vecs, GAIN_ONE, BIAS_ONE)

        def norm_two():
            norm_into(s["x_second"].at[top], resid, vecs, GAIN_TWO, BIAS_TWO)

        gvec[...] = jnp.zeros_like(gvec)
        cast_shard(0)
        cast_shard(1)
        gather_at(0)
        cast_shard(2)
        cast_shard(3)
        loads[0].start()
        v.step(0)
        gather_at(1)
        gather_at(2)
        v.step(1)
        gather_at(3)
        v.step(2)
        gather_at(4)
        gather_at(5)
        v.step(3)
        begin()
        cross("y_mlp")
        gather_at(6)
        gather_at(7)
        v.step(4)
        known()
        gather_at(8)
        norm_one()
        cross("x_first")
        gather_at(9)
        gather_at(10)
        gather_at(11)
        gathered(0, 1)
        project(0)
        gather_at(12)
        project(1)
        project(2)
        attend(0, 2)
        gather_at(13)
        attend(2, 2)
        attend(4, 2)
        gather_at(14)
        attend(6, 2)
        cross("x_attended")
        gathered(2)
        project_out()
        norm_two()
        cross("x_second")
        gather_at(15)
        gather_at(16)
        gathered(3, 4)
        up_tiles(0, 2)
        up_tiles(2, 2)
        cross("a0")
        gather_at(17)
        up_tiles(4, 2)
        gather_at(18)
        up_tiles(6, 2)
        cross("a1")
        gather_at(19)
        crossed("y_mlp", "a0", "a1")
        down_grad(0)
        down_grad(1)
        down_grad(2)
        down_grad(3)
        gather_at(20)
        gather_at(21)
        crossed("x_second")
        transpose_blocks(s["x_second"], s["turned"])
        gathered(5, 6)
        d_inner_tiles(0, 2)
        d_inner_tiles(2, 2)
        cross("i0")
        stage(0, 0)
        d_inner_tiles(4, 2)
        d_inner_tiles(6, 2)
        cross("i1")
        loads[0].start()
        stage(0, 1)
        crossed("i0")
        up_grad(0)
        crossed("i1")
        up_grad(2)
        send_blocks(1)
        pl.semaphore_signal(free, inc=1, device_id=(sib,), device_id_type=MESH)
        stage(0, 2)
        clear()
        d_second_tiles(0, 4)
        d_second_tiles(4, 4)
        stage(0, 3)
        second_norm_back()
        cross("y_branch")
        loop(width // (TILE // 2), d_attended_tile)
        stage(0, 4)
        attend_back(0, 2)
        stage(0, 5)
        stage(1, 0)
        attend_back(2, 2)
        stage(1, 1)
        attend_back(4, 2)
        stage(0, 6)
        stage(1, 2)
        attend_back(6, 2)
        pl.semaphore_wait(free, 1)
        cross("y_proj")
        crossed("x_attended", "x_first", "y_branch")
        out_grad()
        stage(1, 3)
        crossed("y_proj")
        qkv_grad()
        send_blocks(2)
        stage(0, 7)
        leave_result(3).start()
        stage(1, 4)
        stage(1, 5)
        clear()
        d_first_tiles(0, 3)
        d_first_tiles(3, 3)
        stage(2, 0)
        first_norm_back()
        share_vectors()
        stage(1, 6)
        stage(2, 1)
        v.step(0)
        clear()
        down_tiles(0, 4)
        down_tiles(4, 4)
        finish_activations()
        stage(2, 2)
        stage(1, 7)
        leave_result(2).start()
        v.step(1)
        stage(2, 3)
        v.step(2)
        stage(2, 4)
        v.step(3)
        stage(2, 5)
        v.step(4)
        stage(2, 6)
        stage(2, 7)
        leave_result(0).start()
        leave_result(1).start()
        gvec_out[...] = held[...]
        for g in parts:
            g.drain()
        for piece in range(3):
            drain(piece)
        leave(0, resid, act_out).wait()
        leave(1, d_resid, grad_out).wait()
        for i in range(4):
            leave_result(i).wait()

    anyspec = pl.BlockSpec(memory_space=pl.ANY)
    vm = pl.BlockSpec(memory_space=pltpu.VMEM)
    dma = pltpu.SemaphoreType.DMA
    shape = jax.ShapeDtypeStruct
    n = len(GATHER_PARTS)
    bufs = [pltpu.VMEM((CHIPS,) + block, b16)] * 3
    for _ in range(3):
        for zf, height in ((True, SPLIT_ROWS), (False, block[0] - SPLIT_ROWS)):
            bufs += [pltpu.VMEM((m, height, width), b16) for m in (8, 5 if zf else 10, 4 if zf else 1)]
    outs = [
        ((rows, width), f32),
        ((rows, width), f32),
        ((width, 3 * width), b16),
        ((width, hidden), b16),
        ((hidden, width), b16),
        (shards[0].shape, f32),
        (shards[1].shape, f32),
        (shards[2].shape, f32),
        (shards[3].shape, f32),
        (vec.shape, f32),
    ]
    results = pl.pallas_call(
        kernel,
        out_shape=[shape(*o) for o in outs],
        in_specs=[vm] + [anyspec] * len(OPERANDS),
        out_specs=[anyspec] * 9 + [vm],
        scratch_shapes=[pltpu.VMEM(*kinds[k]) for k in names]
        + bufs
        + [
            pltpu.VMEM(vec.shape, f32),
            pltpu.VMEM((5,) + vec.shape, f32),
            dma((n, 4)),
            dma((n, 16)),
            dma((n,)),
            dma((n,)),
            dma((5,)),
            dma((5,)),
            dma((6, 4)),
            dma((6, 8)),
            dma((6, 10)),
            dma((6, 4)),
            dma((len(crossing),)),
            dma((len(crossing),)),
            dma((len(OPERANDS),)),
            dma((2 * (1 + width // TILE),)),
            dma((6 + UNITS,)),
            pltpu.SemaphoreType.REGULAR,
        ],
        compiler_params=pltpu.CompilerParams(collective_id=0, has_side_effects=True, vmem_limit_bytes=63 << 20),
    )(small_rows(segments, vectors), tokens, cotangent, *shards)
    settled = settle([results[0], results[1], *results[5:9]])
    return settled[0], settled[1], settled[2:], results[9]


def local_math(tokens, segments, cotangent, vectors, weights):
    gain_one, bias_one, mix_bias, proj_bias, gain_two, bias_two, up_bias, down_bias = vectors
    mix_weight, proj_weight, up_weight, down_weight = weights
    model_width = tokens.shape[1]
    valid_slot = segments < IMG_DEV
    allowed = (segments[:, None] == segments[None, :]) & valid_slot[None, :]
    gain_one_f = gain_one.astype(jnp.float32)
    bias_one_f = bias_one.astype(jnp.float32)
    first = halved(layer_norm(tokens, gain_one_f, bias_one_f))
    mix_bias_f = mix_bias.astype(jnp.float32)
    bias_row = jnp.concatenate(
        [mix_bias_f[:model_width], jnp.zeros((model_width,), jnp.float32), mix_bias_f[model_width:]]
    )
    projected = jnp.dot(first, mix_weight, preferred_element_type=jnp.float32) + bias_row
    queries = halved(projected[:, :model_width] * HEAD_DIM ** (-0.5))
    key_rows = halved(projected[:, model_width : 2 * model_width])
    values = halved(projected[:, 2 * model_width :])
    attended_stack, lse_stack = lax.map(
        lambda pieces: pair_forward(pieces, allowed),
        (head_pairs(queries), head_pairs(key_rows), head_pairs(values)),
    )
    attended = halved(join_pairs(attended_stack))
    residual = (
        tokens
        + jnp.dot(attended, proj_weight, preferred_element_type=jnp.float32)
        + proj_bias.astype(jnp.float32)
    )
    gain_two_f = gain_two.astype(jnp.float32)
    bias_two_f = bias_two.astype(jnp.float32)
    second = halved(layer_norm(residual, gain_two_f, bias_two_f))
    inner = jnp.dot(second, up_weight, preferred_element_type=jnp.float32) + up_bias.astype(
        jnp.float32
    )
    active = halved(jax.nn.gelu(inner, approximate=False))
    branch = jnp.dot(active, down_weight, preferred_element_type=jnp.float32) + down_bias.astype(
        jnp.float32
    )
    activations = jnp.where(valid_slot[:, None], residual + branch, 0.0)
    d_out = jnp.where(valid_slot[:, None], cotangent, 0.0)
    d_mlp = halved(d_out)
    grad_fc2_bias = jnp.sum(d_mlp, 0, dtype=jnp.float32)
    grad_fc2_weight = contract_rows(active, d_mlp)
    d_active = contract_cols(d_mlp, down_weight)
    gelu_back = jax.vjp(partial(jax.nn.gelu, approximate=False), inner)[1]
    d_inner = halved(gelu_back(d_active)[0])
    grad_fc1_bias = jnp.sum(d_inner, 0, dtype=jnp.float32)
    grad_fc1_weight = contract_rows(second, d_inner)
    d_second = contract_cols(d_inner, up_weight)
    norm_two_back = jax.vjp(layer_norm, residual, gain_two_f, bias_two_f)[1]
    d_norm2, grad_norm2_gain, grad_norm2_bias = norm_two_back(d_second)
    d_resid = d_out + d_norm2
    d_branch = halved(d_resid)
    grad_out_bias = jnp.sum(d_branch, 0, dtype=jnp.float32)
    grad_out_weight = contract_rows(attended, d_branch)
    d_attended = halved(contract_cols(d_branch, proj_weight))
    d_query_stack, d_key_stack, d_value_stack = lax.map(
        lambda pieces: pair_backward(pieces, allowed),
        (
            head_pairs(queries),
            head_pairs(key_rows),
            head_pairs(values),
            head_pairs(d_attended),
            lse_stack,
        ),
    )
    d_query = join_pairs(d_query_stack)
    d_value = join_pairs(d_value_stack)
    d_projected = jnp.concatenate([d_query, join_pairs(d_key_stack), d_value], 1)
    grad_qv_bias = jnp.concatenate(
        [jnp.sum(d_query, 0, dtype=jnp.float32), jnp.sum(d_value, 0, dtype=jnp.float32)]
    )
    grad_qkv_weight = contract_rows(first, d_projected)
    d_first = contract_cols(d_projected, mix_weight)
    norm_one_back = jax.vjp(layer_norm, tokens, gain_one_f, bias_one_f)[1]
    d_norm1, grad_norm1_gain, grad_norm1_bias = norm_one_back(d_first)
    input_grad = d_resid + d_norm1
    return (
        activations,
        input_grad,
        (grad_qkv_weight, grad_out_weight, grad_fc1_weight, grad_fc2_weight),
        (
            grad_norm1_gain,
            grad_norm1_bias,
            grad_qv_bias,
            grad_out_bias,
            grad_norm2_gain,
            grad_norm2_bias,
            grad_fc1_bias,
            grad_fc2_bias,
        ),
    )


def shards(count, tokens,
    segments,
    norm1_gain,
    norm1_bias,
    qkv_weight,
    qv_bias,
    out_weight,
    out_bias,
    norm2_gain,
    norm2_bias,
    fc1_weight,
    fc1_bias,
    fc2_weight,
    fc2_bias,
    cotangent,
):
    vector_shards = (norm1_gain, norm1_bias, qv_bias, out_bias, norm2_gain, norm2_bias, fc1_bias, fc2_bias)
    sizes = [v.shape[0] * count for v in vector_shards]
    starts = [sum(sizes[:i]) for i in range(len(sizes) + 1)]
    width = tokens.shape[1]
    position = lax.axis_index(AXIS)
    kernels = count == 32

    if kernels:
        activations, input_grad, weight_owned, vector_rows = block_all(
            count,
            tokens,
            segments,
            cotangent,
            (qkv_weight, out_weight, fc1_weight, fc2_weight),
            vector_shards,
        )
    else:
        weight_shards = [halved(w) for w in (qkv_weight, out_weight, fc1_weight, fc2_weight)]
        weights = [lax.all_gather(w, AXIS, axis=0, tiled=True) for w in weight_shards]
        vectors = [
            lax.all_gather(halved(v), AXIS, axis=0, tiled=True).astype(jnp.float32)
            for v in vector_shards
        ]
        activations, input_grad, weight_grads, vector_grads = local_math(
            tokens, segments, cotangent, vectors, weights
        )
    if kernels:
        flat = vector_rows.reshape(-1)
        vector_owned = [
            lax.dynamic_slice(flat, (starts[i] + position * (sizes[i] // count),), (sizes[i] // count,))
            for i in range(len(sizes))
        ]
    else:
        weight_owned = [
            lax.psum_scatter(g, AXIS, scatter_dimension=0, tiled=True) for g in weight_grads
        ]
        vector_owned = [
            lax.psum_scatter(g, AXIS, scatter_dimension=0, tiled=True) for g in vector_grads
        ]
    g1, b1, qvb, ob, g2, b2, f1b, f2b = vector_owned
    qkv_g, out_g, fc1_g, fc2_g = weight_owned
    return (activations, input_grad, g1, b1, qkv_g, qvb, out_g, ob, g2, b2, fc1_g, f1b, fc2_g, f2b)


def solution(mesh):
    in_specs = (
        P(AXIS, None),
        P(AXIS),
        P(AXIS),
        P(AXIS),
        P(AXIS, None),
        P(AXIS),
        P(AXIS, None),
        P(AXIS),
        P(AXIS),
        P(AXIS),
        P(AXIS, None),
        P(AXIS),
        P(AXIS, None),
        P(AXIS),
        P(AXIS, None),
    )
    out_specs = (
        P(AXIS, None),
        P(AXIS, None),
        P(AXIS),
        P(AXIS),
        P(AXIS, None),
        P(AXIS),
        P(AXIS, None),
        P(AXIS),
        P(AXIS),
        P(AXIS),
        P(AXIS, None),
        P(AXIS),
        P(AXIS, None),
        P(AXIS),
    )
    return jax.shard_map(
        partial(shards, mesh.size), mesh=mesh, in_specs=in_specs, out_specs=out_specs, check_vma=False)
```
